512 devices in a mesh: line: 2 (over core), tile: 256 (over z, y, x).
Axes of the slice: x: 4, y: 8, z: 8, core: 2. Of those that a mesh axis runs over, the one named last changes fastest.
Arguments:
- field: float32 [2, 256, 32768], P(None, 'line', 'tile'), as said below
- saturation: float32 [256, 32768], P('line', 'tile'), may hold values from 0.025 to 1
- solid_mask: int32 [2, 32768], P('line', 'tile'), may hold values 0 or 1
Outputs:
- new_field: float32 [2, 256, 32768], P(None, 'line', 'tile')
The draws below stay inside these ranges and needn't reach their ends.
Inputs may be any that keep to these rules, and one draw needn't show every extreme that they name: 2048 * field lies within -8 to 8.
All inputs are finite; a program needn't handle non-finite values. No bound on the sum of `solid_mask` on one device may be relied on, other than what follows from the above.
Results may differ from the reference program's by a relative error of at most 0.0005.
Values sent between devices are 32-bit elements; how exact they have to be, the bound alone decides.
No kernel may reach another device: no remote copies, remote signals or barrier semaphores. Data moves between devices by JAX's collectives and lax.ppermute only.
A program may use at most 64 MiB of HBM per device.

```python
import math
import jax
import jax.numpy as jnp
from jax import lax

XS = 64
ZBLK = 128
NZ = 256
NLINES = 32768
ZSTIFF = 2048


def draw_field(key, part):
    key = jax.random.fold_in(key, 11)
    first, second = jax.random.split(key)
    rough = jax.random.normal(first, (2, NZ, NLINES), jnp.float32)
    level = jax.random.normal(second, (2, 1, NLINES), jnp.float32)
    return jnp.clip(rough + level, -8.0, 8.0) * (1.0 / ZSTIFF)


def draw_saturation(key, part):
    key = jax.random.fold_in(key, 23)
    first, second = jax.random.split(key)
    level = jnp.exp(jax.random.uniform(first, (1, NLINES), jnp.float32, math.log(0.05), 0.0))
    factor = jnp.exp(jax.random.uniform(second, (NZ, NLINES), jnp.float32, math.log(0.5), 0.0))
    return jnp.clip(level * factor, 0.025, 1.0)


def set_ends(entries, stream_key, smallest, high):
    longest = entries.shape.index(max(entries.shape))
    spots = []
    for shift in (0, 1):
        where = [jax.random.randint(jax.random.fold_in(stream_key, axis), (), 0, length) for axis, length in enumerate(entries.shape)]
        where[longest] = (where[longest] + shift) % entries.shape[longest]
        spots.append(tuple(where))
    return entries.at[spots[0]].set(smallest).at[spots[1]].set(high)


def setup_inputs(seed: int = 0) -> dict:
    keys = jax.random.split(jax.random.key(seed), 4)
    return {
        "field": draw_field(jax.random.fold_in(keys[3], 71), 0),
        "saturation": draw_saturation(jax.random.fold_in(keys[3], 71), 0),
        "solid_mask": set_ends((jax.random.randint(keys[2], (NZ // ZBLK, NLINES), 0, 8) < 1).astype(jnp.int32), jax.random.fold_in(keys[2], 1), 0, 1),
    }


def coefficients(signed):
    dry = jnp.maximum(signed, 0.0)
    moist_pore = 0.004 + dry * dry * dry
    is_pore = signed > 0.0
    is_solid = signed < 0.0
    k_heat = jnp.where(is_pore, 1.0 + 2.0 * dry, jnp.where(is_solid, 3.0, 0.0))
    k_cross_heat = jnp.where(is_pore, 0.5 * moist_pore, 0.0)
    k_cross_moist = jnp.where(is_pore, 0.2 * moist_pore, 0.0)
    k_moist = jnp.where(is_pore, moist_pore, jnp.where(is_solid, 0.004, 0.0))
    return jnp.stack([k_heat, k_cross_heat, k_cross_moist, k_moist])


def mat_mul(left, right):
    return jnp.stack([left[0] * right[0] + left[1] * right[2],
                      left[0] * right[1] + left[1] * right[3],
                      left[2] * right[0] + left[3] * right[2],
                      left[2] * right[1] + left[3] * right[3]])


def mat_vec(matrix, vector):
    return jnp.stack([matrix[0] * vector[0] + matrix[1] * vector[1],
                      matrix[2] * vector[0] + matrix[3] * vector[1]])


def inverse(matrix):
    determinant = matrix[0] * matrix[3] - matrix[1] * matrix[2]
    return jnp.stack([matrix[3], -matrix[1], -matrix[2], matrix[0]]) / determinant


def flux(center_field, center_coeff, other_field, other_coeff):
    return mat_vec(0.5 * (center_coeff + other_coeff), other_field - center_field)


def explicit_slice(field_slice, signed_slice):
    columns = NLINES // XS
    coeff = coefficients(signed_slice)
    grid_field = field_slice.reshape(2, columns, XS)
    grid_coeff = coeff.reshape(4, columns, XS)
    pad_field = jnp.pad(grid_field, ((0, 0), (1, 1), (1, 1)))
    pad_coeff = jnp.pad(grid_coeff, ((0, 0), (1, 1), (1, 1)))
    total = jnp.zeros_like(grid_field)
    for row_off, col_off in ((0, 1), (2, 1), (1, 0), (1, 2)):
        other_field = pad_field[:, row_off:row_off + columns, col_off:col_off + XS]
        other_coeff = pad_coeff[:, row_off:row_off + columns, col_off:col_off + XS]
        total = total + flux(grid_field, grid_coeff, other_field, other_coeff)
    explicit = grid_field + ZSTIFF * total
    return explicit.reshape(2, NLINES), coeff


def reference(field, saturation, solid_mask):
    solid = jnp.repeat(solid_mask, ZBLK, axis=0) > 0
    signed = jnp.where(solid, -saturation, saturation)
    signed_next = jnp.concatenate([signed[1:], jnp.zeros((1, NLINES), jnp.float32)], axis=0)
    field_rows = jnp.moveaxis(field, 1, 0)

    def forward(carry, inputs):
        coeff_prev, c_prev, d_prev = carry
        field_slice, signed_slice, signed_after = inputs
        explicit, coeff = explicit_slice(field_slice, signed_slice)
        coeff_next = coefficients(signed_after)
        lower = ZSTIFF * (0.5 * (coeff_prev + coeff))
        upper = ZSTIFF * (0.5 * (coeff + coeff_next))
        diagonal = lower + upper
        diagonal = jnp.stack([diagonal[0] + 1.0, diagonal[1], diagonal[2], diagonal[3] + 1.0])
        pivot = inverse(diagonal - mat_mul(lower, c_prev))
        c_new = mat_mul(pivot, upper)
        d_new = mat_vec(pivot, explicit + mat_vec(lower, d_prev))
        return (coeff, c_new, d_new), (c_new, d_new)

    start = (jnp.zeros((4, NLINES), jnp.float32), jnp.zeros((4, NLINES), jnp.float32), jnp.zeros((2, NLINES), jnp.float32))
    carry, (c_all, d_all) = lax.scan(forward, start, (field_rows, signed, signed_next))

    def backward(after, inputs):
        c_here, d_here = inputs
        value = d_here + mat_vec(c_here, after)
        return value, value

    final, values = lax.scan(backward, jnp.zeros((2, NLINES), jnp.float32), (c_all, d_all), reverse=True)
    return jnp.moveaxis(values, 0, 1)
```

```python
import jax
import jax.numpy as jnp
from jax import lax
from jax.experimental import pallas as pl
from jax.experimental.pallas import tpu as pltpu
from jax.sharding import PartitionSpec as P

XS = 64
ZSTIFF = 2048
HALF = 0.5 * ZSTIFF
STEPS = 16
CHUNKS = 8
LANES = 128
TILE = (CHUNKS, LANES)
LIMIT = 12 * 1024 * 1024


def mat_mul(a, b):
    return (
        a[0] * b[0] + a[1] * b[2],
        a[0] * b[1] + a[1] * b[3],
        a[2] * b[0] + a[3] * b[2],
        a[2] * b[1] + a[3] * b[3],
    )


def mat_vec(a, v):
    return (a[0] * v[0] + a[1] * v[1], a[2] * v[0] + a[3] * v[1])


def add(*items):
    total = items[0]
    for item in items[1:]:
        total = tuple(x + y for x, y in zip(total, item))
    return total


def inverse(a):
    scale = 1.0 / (a[0] * a[3] - a[1] * a[2])
    return (a[3] * scale, -a[1] * scale, -a[2] * scale, a[0] * scale)


def full(k):
    return (k[0], 0.5 * k[2], 0.2 * k[2], k[1])


def conduct(signed):
    dry = jnp.maximum(signed, 0.0)
    moist = 0.004 + dry * dry * dry
    pore = signed > 0.0
    solid = signed < 0.0
    heat = jnp.where(pore, 1.0 + 2.0 * dry, jnp.where(solid, 3.0, 0.0))
    cross = jnp.where(pore, moist, 0.0)
    return (heat, jnp.where(solid, 0.004, cross), cross)


def flux(k, drop):
    return mat_vec(full(k), drop)


def roll(x, shift, axis):
    return pltpu.roll(x, shift % x.shape[axis], axis)


def down(items, shift):
    return tuple(roll(x, shift, 0) for x in items)


def lanes():
    return lax.broadcasted_iota(jnp.int32, TILE, 1)


def chunks():
    return lax.broadcasted_iota(jnp.int32, TILE, 0)


def toward_odd():
    parity = lax.rem(lax.axis_index("tile"), 2)
    return (lanes() >= XS) == (parity == 1)


def load(ref, *index):
    return tuple(ref[(*index, j)] for j in range(ref.shape[len(index)]))


def store(ref, index, items):
    for j, item in enumerate(items):
        ref[(*index, j)] = item


def levels():
    stride = 1
    while stride < STEPS:
        yield stride, range(0, STEPS, 2 * stride), range(stride, STEPS, 2 * stride)
        stride *= 2


def rows_of():
    place, at = {}, 0
    for stride, kept, _ in levels():
        for step in kept:
            place[stride, step] = at
            at += 1
    return place


PLACE = rows_of()


def prepare(field_hbm, sat_hbm, mask_hbm, field, signed, odd, even, fbuf, sbuf, mbuf, sems):
    copies = [
        pltpu.make_async_copy(mask_hbm, mbuf, sems.at[0]),
        pltpu.make_async_copy(sat_hbm, sbuf, sems.at[1]),
        pltpu.make_async_copy(field_hbm.at[0], fbuf.at[0], sems.at[2]),
        pltpu.make_async_copy(field_hbm.at[1], fbuf.at[1], sems.at[3]),
    ]
    for copy in copies:
        copy.start()
    for copy in copies:
        copy.wait()
    near = toward_odd()
    solid = jnp.broadcast_to(mbuf[...], TILE) > 0
    held = []
    for i in range(STEPS):
        here = pl.ds(i, CHUNKS, stride=STEPS)
        f0, f1, s = fbuf[0, here, :], fbuf[1, here, :], sbuf[here, :]
        s = jnp.where(solid, -s, s)
        field[0, i], field[1, i], signed[i] = f0, f1, s
        held.append(s)
        f1 = roll(f1, XS, 1)
        odd[i] = jnp.where(near, f0, f1)
        even[i] = jnp.where(near, f1, f0)
    for i in range(STEPS // 2):
        low, high = held[i], roll(held[i + STEPS // 2], XS, 1)
        odd[STEPS + i] = jnp.where(near, low, high)
        even[STEPS + i] = jnp.where(near, high, low)


def local(field, signed, k_all, rhs, ab, dpq, ring, final, answer, share):
    line = lax.axis_index("line")
    first, last = chunks() == 0, chunks() == CHUNKS - 1
    low_line, high_line = line == 0, line == 1
    column = lax.rem(lanes(), XS)
    west_end, east_end = column == 0, column == XS - 1
    zero = jnp.zeros(TILE, jnp.float32)
    one = jnp.ones(TILE, jnp.float32)
    unit = (one, zero, zero, one)

    k = []
    for i in range(STEPS):
        ki = conduct(signed[i])
        k.append(ki)
        store(k_all, (i,), ki)
        f = (field[0, i], field[1, i])
        both = (*ki, *f)
        other = tuple(roll(x, XS, 1) for x in both)
        total = flux(add(ki, other[:3]), (other[3] - f[0], other[4] - f[1]))
        before = tuple(jnp.where(west_end, 0.0, roll(x, 1, 1)) for x in both)
        west = flux(add(ki, before[:3]), (before[3] - f[0], before[4] - f[1]))
        edge = flux(ki, (-f[0], -f[1]))
        east = tuple(jnp.where(east_end, e, -roll(w, -1, 1)) for e, w in zip(edge, west))
        total = add(total, west, east)
        rhs[0, i] = f[0] + HALF * total[0]
        rhs[1, i] = f[1] + HALF * total[1]

    faces = [full(tuple(HALF * (x + y) for x, y in zip(k[i], k[i + 1]))) for i in range(STEPS - 1)]
    after = down(k[0], -1)
    outer = full(tuple(HALF * (x + y) for x, y in zip(k[-1], after)))
    faces.append(tuple(jnp.where(last, 0.0, x) for x in outer))
    entry = down(faces[-1], 1)
    bottom = jnp.logical_and(first, low_line)
    top = jnp.logical_and(last, high_line)
    excess = {i: unit for i in range(STEPS)}
    excess[0] = add(unit, tuple(jnp.where(bottom, HALF * x, 0.0) for x in full(k[0])))
    excess[STEPS - 1] = add(unit, tuple(jnp.where(top, HALF * x, 0.0) for x in full(k[-1])))
    lower = {i: faces[i - 1] if i else entry for i in range(STEPS)}
    upper = {i: faces[i] for i in range(STEPS)}

    for stride, kept, dropped in levels():
        inv = {}
        for i in dropped:
            inv[i] = inverse(add(excess[i], lower[i], upper[i]))
            store(dpq, (i,), (*inv[i], *mat_mul(inv[i], lower[i]), *mat_mul(inv[i], upper[i])))
        for i in kept:
            right = i + stride
            left = i - stride
            if left < 0:
                left += STEPS
                prev = tuple(down(x[left], 1) for x in (inv, lower, excess))
            else:
                prev = tuple(x[left] for x in (inv, lower, excess))
            a = mat_mul(lower[i], prev[0])
            b = mat_mul(upper[i], inv[right])
            store(ab, (PLACE[stride, i],), (*a, *b))
            up_a = a if prev[2] is unit else mat_mul(a, prev[2])
            up_b = b if excess[right] is unit else mat_mul(b, excess[right])
            excess[i] = add(excess[i], up_a, up_b)
            lower[i] = mat_mul(a, prev[1])
            upper[i] = mat_mul(b, upper[right])

    start = jnp.logical_and(high_line, first)
    end = jnp.logical_and(low_line, last)
    sides = {STEPS - 1: tuple(jnp.where(end, x, 0.0) for x in unit)}
    source = None
    for stride, kept, _ in levels():
        i = kept[-1]
        b = load(ab, PLACE[stride, i])[4:8]
        source = tuple(jnp.where(end, x, 0.0) for x in b) if source is None else mat_mul(b, source)
        sides[i] = source
    vec = add(tuple(jnp.where(start, x, 0.0) for x in unit), sides[0])

    low, up, ex = lower[0], upper[0], excess[0]
    shift, place = 1, 0
    while shift < CHUNKS:
        inv = inverse(add(ex, low, up))
        a = mat_mul(low, down(inv, shift))
        b = mat_mul(up, down(inv, -shift))
        store(ring, (place,), (*a, *b))
        vec = add(vec, mat_mul(a, down(vec, shift)), mat_mul(b, down(vec, -shift)))
        ex = add(ex, mat_mul(a, down(ex, shift)), mat_mul(b, down(ex, -shift)))
        low, up = mat_mul(a, down(low, shift)), mat_mul(b, down(up, -shift))
        shift *= 2
        place += 1
    inv = inverse(ex)
    store(final, (), inv)
    w = {0: mat_mul(inv, vec)}
    for stride, kept, dropped in reversed(list(levels())):
        for i in dropped:
            d = load(dpq, i)
            right = w[i + stride] if i + stride < STEPS else down(w[0], -1)
            w[i] = add(mat_mul(d[4:8], w[i - stride]), mat_mul(d[8:12], right))
            if i in sides:
                w[i] = add(w[i], mat_mul(d[0:4], sides[i]))
    for i in range(STEPS):
        store(answer, (i,), w[i])

    tail = (*down(w[STEPS - 1], 1), *down(k[STEPS - 1], 1))
    head = (*w[0], *k[0])
    for j, (x, y) in enumerate(zip(head, tail)):
        share[pl.ds(2 + j, 1), :] = jnp.where(low_line, y, x)[0:1]


def finish(field, k_all, rhs, ab, dpq, ring, final, share, odd, even, local_x, message):
    line = lax.axis_index("line")
    parity = lax.rem(lax.axis_index("tile"), 2)
    near = toward_odd()
    theirs = 1 - parity
    half = STEPS // 2
    far_signed = [None] * STEPS
    for i in range(half):
        o, e = odd[STEPS + i], even[theirs, STEPS + i]
        far_signed[i] = roll(jnp.where(near, e, o), XS, 1)
        far_signed[i + half] = jnp.where(near, o, e)
    b = {}
    for i in range(STEPS):
        o, e = odd[i], even[theirs, i]
        far = (roll(jnp.where(near, e, o), XS, 1), jnp.where(near, o, e))
        drop = (far[0] - field[0, i], far[1] - field[1, i])
        total = flux(add(load(k_all, i), conduct(far_signed[i])), drop)
        b[i] = (rhs[0, i] + HALF * total[0], rhs[1, i] + HALF * total[1])
    for stride, kept, _ in levels():
        for i in kept:
            left = i - stride
            prev = b[left] if left >= 0 else down(b[left + STEPS], 1)
            c = load(ab, PLACE[stride, i])
            b[i] = add(b[i], mat_vec(c[0:4], prev), mat_vec(c[4:8], b[i + stride]))
    vec = b[0]
    shift, place = 1, 0
    while shift < CHUNKS:
        c = load(ring, place)
        vec = add(vec, mat_vec(c[0:4], down(vec, shift)), mat_vec(c[4:8], down(vec, -shift)))
        shift *= 2
        place += 1
    x = {0: mat_vec(load(final), vec)}
    for stride, _, dropped in reversed(list(levels())):
        for i in dropped:
            d = load(dpq, i)
            right = x[i + stride] if i + stride < STEPS else down(x[0], -1)
            x[i] = add(mat_vec(d[0:4], b[i]), mat_vec(d[4:8], x[i - stride]), mat_vec(d[8:12], right))
    for i in range(STEPS):
        store(local_x, (i,), x[i])
    message[...] = share[...]
    tail = down(x[STEPS - 1], 1)
    for j in range(2):
        message[pl.ds(j, 1), :] = jnp.where(line == 0, tail[j], x[0][j])[0:1]


def join(local_x, answer, both, out):
    line = lax.axis_index("line")

    def row(who, j):
        return jnp.broadcast_to(both[who, pl.ds(j, 1), :], TILE)

    sign = jnp.where(line == 0, 1.0, -1.0)
    drop = tuple(sign * (row(1, j) - row(0, j)) for j in range(2))
    reach = tuple(row(0, 2 + j) + row(1, 2 + j) for j in range(4))
    face = full(tuple(HALF * (row(0, 6 + j) + row(1, 6 + j)) for j in range(3)))
    one, zero = jnp.ones(TILE, jnp.float32), jnp.zeros(TILE, jnp.float32)
    inv = inverse(add((one, zero, zero, one), mat_mul(face, reach)))
    through = mat_vec(inv, mat_vec(face, drop))
    for i in range(STEPS):
        x = add(load(local_x, i), mat_vec(load(answer, i), through))
        here = pl.ds(i, CHUNKS, stride=STEPS)
        out[0, here, :] = x[0]
        out[1, here, :] = x[1]


def tiles(*lead):
    return jax.ShapeDtypeStruct((*lead, *TILE), jnp.float32)


def call(kernel, outs, args, name, flops, **more):
    vmem = pl.BlockSpec(memory_space=pltpu.VMEM)
    more.setdefault("in_specs", [vmem] * len(args))
    one = not isinstance(outs, (list, tuple))
    return pl.pallas_call(
        kernel,
        out_shape=outs,
        out_specs=vmem if one else [vmem] * len(outs),
        compiler_params=pltpu.CompilerParams(vmem_limit_bytes=LIMIT),
        cost_estimate=pl.CostEstimate(flops=flops, bytes_accessed=1 << 20, transcendentals=0),
        name=name,
        **more,
    )(*args)


def body(field, saturation, solid_mask):
    count = lax.axis_size("tile")
    evens = [[t, t + 1] for t in range(0, count, 2)]
    odds = [pair for t in range(1, count - 1, 2) for pair in ((t, t + 1), (t + 1, t))]
    cells = STEPS * CHUNKS
    pack = STEPS + STEPS // 2
    kept, signed, odd, even = call(
        prepare,
        [tiles(2, STEPS), tiles(STEPS), tiles(pack), tiles(pack)],
        (field, saturation, solid_mask),
        "prepare",
        1 << 16,
        in_specs=[pl.BlockSpec(memory_space=pl.ANY)] * 3,
        scratch_shapes=[
            pltpu.VMEM((2, cells, LANES), jnp.float32),
            pltpu.VMEM((cells, LANES), jnp.float32),
            pltpu.VMEM((1, LANES), jnp.int32),
            pltpu.SemaphoreType.DMA((4,)),
        ],
    )
    odd = lax.ppermute(odd, "tile", odds)
    even = lax.all_gather(even, "tile", axis_index_groups=evens, axis=0)
    k_all, rhs, ab, dpq, ring, final, answer, share = call(
        local,
        [
            tiles(STEPS, 3),
            tiles(2, STEPS),
            tiles(STEPS - 1, 8),
            tiles(STEPS, 12),
            tiles(3, 8),
            tiles(4),
            tiles(STEPS, 4),
            jax.ShapeDtypeStruct((16, LANES), jnp.float32),
        ],
        (kept, signed),
        "local",
        1 << 23,
    )
    local_x, message = call(
        finish,
        [tiles(STEPS, 2), jax.ShapeDtypeStruct((16, LANES), jnp.float32)],
        (kept, k_all, rhs, ab, dpq, ring, final, share, odd, even),
        "finish",
        1 << 21,
    )
    both = lax.all_gather(message, "line", axis=0)
    out = jax.ShapeDtypeStruct((2, cells, LANES), jnp.float32)
    return call(join, out, (local_x, answer, both), "join", 1 << 18)


def solution(mesh):
    in_specs = (P(None, "line", "tile"), P("line", "tile"), P("line", "tile"))
    out_specs = P(None, "line", "tile")
    return jax.shard_map(body, mesh=mesh, in_specs=in_specs, out_specs=out_specs, check_vma=False)
```

```python
import jax
import jax.numpy as jnp
from jax import lax
from jax.experimental import pallas as pl
from jax.experimental.pallas import tpu as pltpu
from jax.sharding import PartitionSpec as P

XS = 64
ZSTIFF = 2048
HALF = 0.5 * ZSTIFF
STEPS = 16
CHUNKS = 8
LANES = 128
TILE = (CHUNKS, LANES)
LIMIT = 12 * 1024 * 1024


def mat_mul(a, b):
    return (
        a[0] * b[0] + a[1] * b[2],
        a[0] * b[1] + a[1] * b[3],
        a[2] * b[0] + a[3] * b[2],
        a[2] * b[1] + a[3] * b[3],
    )


def mat_vec(a, v):
    return (a[0] * v[0] + a[1] * v[1], a[2] * v[0] + a[3] * v[1])


def add(*items):
    total = items[0]
    for item in items[1:]:
        total = tuple(x + y for x, y in zip(total, item))
    return total


def inverse(a):
    scale = 1.0 / (a[0] * a[3] - a[1] * a[2])
    return (a[3] * scale, -a[1] * scale, -a[2] * scale, a[0] * scale)


def full(k):
    return (k[0], 0.5 * k[2], 0.2 * k[2], k[1])


def conduct(signed):
    dry = jnp.maximum(signed, 0.0)
    moist = 0.004 + dry * dry * dry
    pore = signed > 0.0
    solid = signed < 0.0
    heat = jnp.where(pore, 1.0 + 2.0 * dry, jnp.where(solid, 3.0, 0.0))
    cross = jnp.where(pore, moist, 0.0)
    return (heat, jnp.where(solid, 0.004, cross), cross)


def flux(k, drop):
    return mat_vec(full(k), drop)


def roll(x, shift, axis):
    return pltpu.roll(x, shift % x.shape[axis], axis)


def down(items, shift):
    return tuple(roll(x, shift, 0) for x in items)


def lanes():
    return lax.broadcasted_iota(jnp.int32, TILE, 1)


def chunks():
    return lax.broadcasted_iota(jnp.int32, TILE, 0)


def toward_odd():
    parity = lax.rem(lax.axis_index("tile"), 2)
    return (lanes() >= XS) == (parity == 1)


def load(ref, *index):
    return tuple(ref[(*index, j)] for j in range(ref.shape[len(index)]))


def store(ref, index, items):
    for j, item in enumerate(items):
        ref[(*index, j)] = item


def levels():
    stride = 1
    while stride < STEPS:
        yield stride, range(0, STEPS, 2 * stride), range(stride, STEPS, 2 * stride)
        stride *= 2


def rows_of():
    place, at = {}, 0
    for stride, kept, _ in levels():
        for step in kept:
            place[stride, step] = at
            at += 1
    return place


PLACE = rows_of()


def prepare(field_hbm, sat_hbm, mask_hbm, field, signed, odd, even, fbuf, sbuf, mbuf, sems):
    copies = [
        pltpu.make_async_copy(mask_hbm, mbuf, sems.at[0]),
        pltpu.make_async_copy(sat_hbm, sbuf, sems.at[1]),
        pltpu.make_async_copy(field_hbm.at[0], fbuf.at[0], sems.at[2]),
        pltpu.make_async_copy(field_hbm.at[1], fbuf.at[1], sems.at[3]),
    ]
    for copy in copies:
        copy.start()
    for copy in copies:
        copy.wait()
    near = toward_odd()
    solid = jnp.broadcast_to(mbuf[...], TILE) > 0
    held = []
    for i in range(STEPS):
        here = pl.ds(i, CHUNKS, stride=STEPS)
        f0, f1, s = fbuf[0, here, :], fbuf[1, here, :], sbuf[here, :]
        s = jnp.where(solid, -s, s)
        field[0, i], field[1, i], signed[i] = f0, f1, s
        held.append(s)
        f1 = roll(f1, XS, 1)
        odd[i] = jnp.where(near, f0, f1)
        even[i] = jnp.where(near, f1, f0)
    for i in range(STEPS // 2):
        low, high = held[i], roll(held[i + STEPS // 2], XS, 1)
        odd[STEPS + i] = jnp.where(near, low, high)
        even[STEPS + i] = jnp.where(near, high, low)


def local(field, signed, k_all, rhs, ab, dpq, ring, final, answer, share):
    line = lax.axis_index("line")
    first, last = chunks() == 0, chunks() == CHUNKS - 1
    low_line, high_line = line == 0, line == 1
    column = lax.rem(lanes(), XS)
    west_end, east_end = column == 0, column == XS - 1
    zero = jnp.zeros(TILE, jnp.float32)
    one = jnp.ones(TILE, jnp.float32)
    unit = (one, zero, zero, one)

    k = []
    for i in range(STEPS):
        ki = conduct(signed[i])
        k.append(ki)
        store(k_all, (i,), ki)
        f = (field[0, i], field[1, i])
        both = (*ki, *f)
        other = tuple(roll(x, XS, 1) for x in both)
        total = flux(add(ki, other[:3]), (other[3] - f[0], other[4] - f[1]))
        before = tuple(jnp.where(west_end, 0.0, roll(x, 1, 1)) for x in both)
        west = flux(add(ki, before[:3]), (before[3] - f[0], before[4] - f[1]))
        edge = flux(ki, (-f[0], -f[1]))
        east = tuple(jnp.where(east_end, e, -roll(w, -1, 1)) for e, w in zip(edge, west))
        total = add(total, west, east)
        rhs[0, i] = f[0] + HALF * total[0]
        rhs[1, i] = f[1] + HALF * total[1]

    faces = [full(tuple(HALF * (x + y) for x, y in zip(k[i], k[i + 1]))) for i in range(STEPS - 1)]
    after = down(k[0], -1)
    outer = full(tuple(HALF * (x + y) for x, y in zip(k[-1], after)))
    faces.append(tuple(jnp.where(last, 0.0, x) for x in outer))
    entry = down(faces[-1], 1)
    bottom = jnp.logical_and(first, low_line)
    top = jnp.logical_and(last, high_line)
    excess = {i: unit for i in range(STEPS)}
    excess[0] = add(unit, tuple(jnp.where(bottom, HALF * x, 0.0) for x in full(k[0])))
    excess[STEPS - 1] = add(unit, tuple(jnp.where(top, HALF * x, 0.0) for x in full(k[-1])))
    lower = {i: faces[i - 1] if i else entry for i in range(STEPS)}
    upper = {i: faces[i] for i in range(STEPS)}

    for stride, kept, dropped in levels():
        inv = {}
        for i in dropped:
            inv[i] = inverse(add(excess[i], lower[i], upper[i]))
            store(dpq, (i,), (*inv[i], *mat_mul(inv[i], lower[i]), *mat_mul(inv[i], upper[i])))
        for i in kept:
            right = i + stride
            left = i - stride
            if left < 0:
                left += STEPS
                prev = tuple(down(x[left], 1) for x in (inv, lower, excess))
            else:
                prev = tuple(x[left] for x in (inv, lower, excess))
            a = mat_mul(lower[i], prev[0])
            b = mat_mul(upper[i], inv[right])
            store(ab, (PLACE[stride, i],), (*a, *b))
            up_a = a if prev[2] is unit else mat_mul(a, prev[2])
            up_b = b if excess[right] is unit else mat_mul(b, excess[right])
            excess[i] = add(excess[i], up_a, up_b)
            lower[i] = mat_mul(a, prev[1])
            upper[i] = mat_mul(b, upper[right])

    start = jnp.logical_and(high_line, first)
    end = jnp.logical_and(low_line, last)
    sides = {STEPS - 1: tuple(jnp.where(end, x, 0.0) for x in unit)}
    source = None
    for stride, kept, _ in levels():
        i = kept[-1]
        b = load(ab, PLACE[stride, i])[4:8]
        source = tuple(jnp.where(end, x, 0.0) for x in b) if source is None else mat_mul(b, source)
        sides[i] = source
    vec = add(tuple(jnp.where(start, x, 0.0) for x in unit), sides[0])

    low, up, ex = lower[0], upper[0], excess[0]
    shift, place = 1, 0
    while shift < CHUNKS:
        inv = inverse(add(ex, low, up))
        a = mat_mul(low, down(inv, shift))
        b = mat_mul(up, down(inv, -shift))
        store(ring, (place,), (*a, *b))
        vec = add(vec, mat_mul(a, down(vec, shift)), mat_mul(b, down(vec, -shift)))
        ex = add(ex, mat_mul(a, down(ex, shift)), mat_mul(b, down(ex, -shift)))
        low, up = mat_mul(a, down(low, shift)), mat_mul(b, down(up, -shift))
        shift *= 2
        place += 1
    inv = inverse(ex)
    store(final, (), inv)
    w = {0: mat_mul(inv, vec)}
    for stride, kept, dropped in reversed(list(levels())):
        for i in dropped:
            d = load(dpq, i)
            right = w[i + stride] if i + stride < STEPS else down(w[0], -1)
            w[i] = add(mat_mul(d[4:8], w[i - stride]), mat_mul(d[8:12], right))
            if i in sides:
                w[i] = add(w[i], mat_mul(d[0:4], sides[i]))
    for i in range(STEPS):
        store(answer, (i,), w[i])

    tail = (*down(w[STEPS - 1], 1), *down(k[STEPS - 1], 1))
    head = (*w[0], *k[0])
    for j, (x, y) in enumerate(zip(head, tail)):
        share[pl.ds(2 + j, 1), :] = jnp.where(low_line, y, x)[0:1]


def finish(field, k_all, rhs, ab, dpq, ring, final, share, odd, even, local_x, message):
    line = lax.axis_index("line")
    parity = lax.rem(lax.axis_index("tile"), 2)
    near = toward_odd()
    theirs = 1 - parity
    half = STEPS // 2
    far_signed = [None] * STEPS
    for i in range(half):
        o, e = odd[STEPS + i], even[theirs, STEPS + i]
        far_signed[i] = roll(jnp.where(near, e, o), XS, 1)
        far_signed[i + half] = jnp.where(near, o, e)
    b = {}
    for i in range(STEPS):
        o, e = odd[i], even[theirs, i]
        far = (roll(jnp.where(near, e, o), XS, 1), jnp.where(near, o, e))
        drop = (far[0] - field[0, i], far[1] - field[1, i])
        total = flux(add(load(k_all, i), conduct(far_signed[i])), drop)
        b[i] = (rhs[0, i] + HALF * total[0], rhs[1, i] + HALF * total[1])
    for stride, kept, _ in levels():
        for i in kept:
            left = i - stride
            prev = b[left] if left >= 0 else down(b[left + STEPS], 1)
            c = load(ab, PLACE[stride, i])
            b[i] = add(b[i], mat_vec(c[0:4], prev), mat_vec(c[4:8], b[i + stride]))
    vec = b[0]
    shift, place = 1, 0
    while shift < CHUNKS:
        c = load(ring, place)
        vec = add(vec, mat_vec(c[0:4], down(vec, shift)), mat_vec(c[4:8], down(vec, -shift)))
        shift *= 2
        place += 1
    x = {0: mat_vec(load(final), vec)}
    for stride, _, dropped in reversed(list(levels())):
        for i in dropped:
            d = load(dpq, i)
            right = x[i + stride] if i + stride < STEPS else down(x[0], -1)
            x[i] = add(mat_vec(d[0:4], b[i]), mat_vec(d[4:8], x[i - stride]), mat_vec(d[8:12], right))
    for i in range(STEPS):
        store(local_x, (i,), x[i])
    message[...] = share[...]
    tail = down(x[STEPS - 1], 1)
    for j in range(2):
        message[pl.ds(j, 1), :] = jnp.where(line == 0, tail[j], x[0][j])[0:1]


def join(local_x, answer, both, out):
    line = lax.axis_index("line")

    def row(who, j):
        return jnp.broadcast_to(both[who, pl.ds(j, 1), :], TILE)

    sign = jnp.where(line == 0, 1.0, -1.0)
    drop = tuple(sign * (row(1, j) - row(0, j)) for j in range(2))
    reach = tuple(row(0, 2 + j) + row(1, 2 + j) for j in range(4))
    face = full(tuple(HALF * (row(0, 6 + j) + row(1, 6 + j)) for j in range(3)))
    one, zero = jnp.ones(TILE, jnp.float32), jnp.zeros(TILE, jnp.float32)
    inv = inverse(add((one, zero, zero, one), mat_mul(face, reach)))
    through = mat_vec(inv, mat_vec(face, drop))
    for i in range(STEPS):
        x = add(load(local_x, i), mat_vec(load(answer, i), through))
        here = pl.ds(i, CHUNKS, stride=STEPS)
        out[0, here, :] = x[0]
        out[1, here, :] = x[1]


def tiles(*lead):
    return jax.ShapeDtypeStruct((*lead, *TILE), jnp.float32)


def call(kernel, outs, args, name, flops, **more):
    vmem = pl.BlockSpec(memory_space=pltpu.VMEM)
    more.setdefault("in_specs", [vmem] * len(args))
    one = not isinstance(outs, (list, tuple))
    return pl.pallas_call(
        kernel,
        out_shape=outs,
        out_specs=vmem if one else [vmem] * len(outs),
        compiler_params=pltpu.CompilerParams(vmem_limit_bytes=LIMIT),
        cost_estimate=pl.CostEstimate(flops=flops, bytes_accessed=1 << 20, transcendentals=0),
        name=name,
        **more,
    )(*args)


def body(field, saturation, solid_mask):
    count = lax.axis_size("tile")
    evens = [[t, t + 1] for t in range(0, count, 2)]
    odds = [pair for t in range(1, count - 1, 2) for pair in ((t, t + 1), (t + 1, t))]
    cells = STEPS * CHUNKS
    pack = STEPS + STEPS // 2
    args = [pltpu.with_memory_space_constraint(x, pltpu.HBM) for x in (field, saturation, solid_mask)]
    kept, signed, odd, even = call(
        prepare,
        [tiles(2, STEPS), tiles(STEPS), tiles(pack), tiles(pack)],
        args,
        "prepare",
        1 << 16,
        in_specs=[pl.BlockSpec(memory_space=pltpu.HBM)] * 3,
        scratch_shapes=[
            pltpu.VMEM((2, cells, LANES), jnp.float32),
            pltpu.VMEM((cells, LANES), jnp.float32),
            pltpu.VMEM((1, LANES), jnp.int32),
            pltpu.SemaphoreType.DMA((4,)),
        ],
    )
    odd = lax.ppermute(odd, "tile", odds)
    even = lax.all_gather(even, "tile", axis_index_groups=evens, axis=0)
    k_all, rhs, ab, dpq, ring, final, answer, share = call(
        local,
        [
            tiles(STEPS, 3),
            tiles(2, STEPS),
            tiles(STEPS - 1, 8),
            tiles(STEPS, 12),
            tiles(3, 8),
            tiles(4),
            tiles(STEPS, 4),
            jax.ShapeDtypeStruct((16, LANES), jnp.float32),
        ],
        (kept, signed),
        "local",
        1 << 23,
    )
    local_x, message = call(
        finish,
        [tiles(STEPS, 2), jax.ShapeDtypeStruct((16, LANES), jnp.float32)],
        (kept, k_all, rhs, ab, dpq, ring, final, share, odd, even),
        "finish",
        1 << 21,
    )
    both = lax.all_gather(message, "line", axis=0)
    out = jax.ShapeDtypeStruct((2, cells, LANES), jnp.float32)
    return call(join, out, (local_x, answer, both), "join", 1 << 18)


def solution(mesh):
    in_specs = (P(None, "line", "tile"), P("line", "tile"), P("line", "tile"))
    out_specs = P(None, "line", "tile")
    return jax.shard_map(body, mesh=mesh, in_specs=in_specs, out_specs=out_specs, check_vma=False)
```

```python
import jax
import jax.numpy as jnp
from jax import lax
from jax.experimental import pallas as pl
from jax.experimental.pallas import tpu as pltpu
from jax.sharding import PartitionSpec as P

XS = 64
ZSTIFF = 2048
HALF = 0.5 * ZSTIFF
STEPS = 16
CHUNKS = 8
LANES = 128
TILE = (CHUNKS, LANES)
ROW = 4
SCALE = 0.4**0.5
CROSS = 0.1**0.5
LIMIT = 12 * 1024 * 1024


def mul(a, b):
    return (
        a[0] * b[0] + a[1] * b[2],
        a[0] * b[1] + a[1] * b[3],
        a[2] * b[0] + a[3] * b[2],
        a[2] * b[1] + a[3] * b[3],
    )


def wide(s):
    return (s[0], s[1], s[1], s[2])


def turn(a):
    return (a[0], a[2], a[1], a[3])


def apply(a, v):
    return (a[0] * v[0] + a[1] * v[1], a[2] * v[0] + a[3] * v[1])


def add(*items):
    total = items[0]
    for item in items[1:]:
        total = tuple(x + y for x, y in zip(total, item))
    return total


def symmetric(a, *more):
    return add(*((m[0], m[1], m[3]) for m in (a, *more)))


def inverse(s):
    scale = 1.0 / (s[0] * s[2] - s[1] * s[1])
    return (s[2] * scale, -s[1] * scale, s[0] * scale)


def conduct(signed):
    dry = jnp.maximum(signed, 0.0)
    moist = 0.004 + dry * dry * dry
    pore = signed > 0.0
    return (jnp.where(pore, 1.0 + 2.0 * signed, 3.0), jnp.where(pore, CROSS * moist, 0.0), moist)


def conduct_or_none(signed):
    inside = signed != 0.0
    heat, cross, moist = conduct(signed)
    return (jnp.where(inside, heat, 0.0), cross, jnp.where(inside, moist, 0.0))


def flux(k, drop):
    return (k[0] * drop[0] + k[1] * drop[1], k[1] * drop[0] + k[2] * drop[1])


def roll(x, shift, axis):
    return pltpu.roll(x, shift % x.shape[axis], axis)


def down(items, shift):
    return tuple(roll(x, shift, 0) for x in items)


def lanes():
    return lax.broadcasted_iota(jnp.int32, TILE, 1)


def chunks():
    return lax.broadcasted_iota(jnp.int32, TILE, 0)


def toward_odd():
    parity = lax.rem(lax.axis_index("tile"), 2)
    return (lanes() >= XS) == (parity == 1)


def load(ref, *index):
    return tuple(ref[(*index, j)] for j in range(ref.shape[len(index)]))


def store(ref, index, items):
    for j, item in enumerate(items):
        ref[(*index, j)] = item


def levels():
    stride = 1
    while stride < STEPS:
        yield stride, range(0, STEPS, 2 * stride), range(stride, STEPS, 2 * stride)
        stride *= 2


def rows_of():
    place, at = {}, 0
    for stride, kept, _ in levels():
        for step in kept:
            place[stride, step] = at
            at += 1
    return place


PLACE = rows_of()


def prepare(field_hbm, sat_hbm, mask_hbm, kept, turned, odd, fbuf, sbuf, mbuf, sems):
    fetch_f1 = pltpu.make_async_copy(field_hbm.at[1], fbuf.at[1], sems.at[0])
    fetch_s = pltpu.make_async_copy(sat_hbm, sbuf, sems.at[1])
    fetch_mask = pltpu.make_async_copy(mask_hbm, mbuf, sems.at[2])
    fetch_f0 = pltpu.make_async_copy(field_hbm.at[0], fbuf.at[0], sems.at[3])
    for copy in (fetch_f1, fetch_s, fetch_mask, fetch_f0):
        copy.start()
    near = toward_odd()
    half = STEPS // 2
    rows = [pl.ds(i, CHUNKS, stride=STEPS) for i in range(STEPS)]
    fetch_f1.wait()
    for i in range(STEPS):
        f1 = fbuf[1, rows[i], :] * (1.0 / SCALE)
        kept[1, i] = f1
        turned[i] = roll(f1, XS, 1)
    fetch_s.wait()
    fetch_mask.wait()
    solid = jnp.broadcast_to(mbuf[...], TILE) > 0
    for i in range(STEPS):
        s = sbuf[rows[i], :]
        s = jnp.where(solid, -s, s)
        kept[2, i] = s
        if i >= half:
            high = roll(s, XS, 1)
            turned[STEPS + i - half] = high
            odd[STEPS + i - half] = jnp.where(near, kept[2, i - half], high)
    fetch_f0.wait()
    for i in range(STEPS):
        f0 = fbuf[0, rows[i], :]
        kept[0, i] = f0
        odd[i] = jnp.where(near, f0, turned[i])


def waits_long():
    return lax.rem(lax.axis_index("tile"), ROW) == 0


def early(field_hbm, sat_hbm, mask_hbm, kept, turned, odd, *rest):
    prepare(field_hbm, sat_hbm, mask_hbm, kept, turned, odd, *rest[-4:])

    @pl.when(waits_long())
    def _():
        local(kept, turned, *rest[:-4])


def late(kept, turned, *rest):
    @pl.when(jnp.logical_not(waits_long()))
    def _():
        local(kept, turned, *rest[len(rest) // 2 :])


def local(kept, turned, even, k_all, rhs, ab, dinv, ring, final, answer, share):
    line = lax.axis_index("line")
    first, last = chunks() == 0, chunks() == CHUNKS - 1
    low_line, high_line = line == 0, line == 1
    near = toward_odd()
    column = lax.rem(lanes(), XS)
    west_end, east_end = column == 0, column == XS - 1
    zero = jnp.zeros(TILE, jnp.float32)
    one = jnp.ones(TILE, jnp.float32)
    unit = (one, zero, zero, one)
    half = STEPS // 2

    for i in range(STEPS):
        even[i] = jnp.where(near, turned[i], kept[0, i])
    for i in range(half):
        even[STEPS + i] = jnp.where(near, turned[STEPS + i], kept[2, i])

    k = []
    for i in range(STEPS):
        s = kept[2, i]
        ki = conduct(s)
        k.append(ki)
        store(k_all, (i,), ki)
        f = (kept[0, i], kept[1, i])
        far = (roll(f[0], XS, 1), turned[i])
        far_s = turned[STEPS + i - half] if i >= half else roll(s, XS, 1)
        total = flux(add(ki, conduct(far_s)), (far[0] - f[0], far[1] - f[1]))
        west_k = conduct(roll(s, 1, 1))
        west = flux(add(ki, west_k), (roll(f[0], 1, 1) - f[0], roll(f[1], 1, 1) - f[1]))
        edge = flux(ki, f)
        west = tuple(jnp.where(west_end, -e, w) for e, w in zip(edge, west))
        east = tuple(jnp.where(east_end, e, roll(w, -1, 1)) for e, w in zip(edge, west))
        for j in range(2):
            rhs[j, i] = f[j] + HALF * (total[j] + (west[j] - east[j]))

    upper = {i: wide(tuple(HALF * (x + y) for x, y in zip(k[i], k[i + 1]))) for i in range(STEPS - 1)}
    outer = tuple(HALF * (x + y) for x, y in zip(k[-1], down(k[0], -1)))
    upper[STEPS - 1] = wide(tuple(jnp.where(last, 0.0, x) for x in outer))
    bottom = jnp.logical_and(first, low_line)
    top = jnp.logical_and(last, high_line)
    bottom = wide(tuple(jnp.where(bottom, HALF * x, 0.0) for x in k[0]))
    top = wide(tuple(jnp.where(top, HALF * x, 0.0) for x in k[-1]))
    excess = {i: unit for i in range(STEPS)}
    excess[0] = add(unit, bottom)
    excess[STEPS - 1] = add(unit, top)

    for stride, keep, drop in levels():
        lower = {}
        for i in (*keep, *drop):
            left = i - stride
            lower[i] = turn(upper[left] if left >= 0 else down(upper[left + STEPS], 1))
        inv = {}
        for i in drop:
            inv[i] = inverse(symmetric(excess[i], lower[i], upper[i]))
            store(dinv, (i,), inv[i])
        for i in keep:
            right, left = i + stride, i - stride
            if left < 0:
                before = wide(down(inv[left + STEPS], 1))
            else:
                before = wide(inv[left])
            a = mul(lower[i], before)
            b = mul(upper[i], wide(inv[right]))
            store(ab, (PLACE[stride, i],), (*a, *b))
            if stride == 1:
                more = add(excess[i], a, b)
                if right == STEPS - 1:
                    more = add(more, mul(b, top))
            else:
                prev = excess[left] if left >= 0 else down(excess[left + STEPS], 1)
                more = add(excess[i], mul(a, prev), mul(b, excess[right]))
            excess[i] = more
            upper[i] = mul(b, upper[right])

    start = jnp.logical_and(high_line, first)
    end = jnp.logical_and(low_line, last)
    sides = {STEPS - 1: tuple(jnp.where(end, x, 0.0) for x in unit)}
    source = None
    for stride, keep, _ in levels():
        i = keep[-1]
        b = load(ab, PLACE[stride, i])[4:8]
        source = tuple(jnp.where(end, x, 0.0) for x in b) if source is None else mul(b, source)
        sides[i] = source
    vec = add(tuple(jnp.where(start, x, 0.0) for x in unit), sides[0])

    up, ex = upper[0], excess[0]
    low = turn(down(up, 1))
    shift, place = 1, 0
    while shift < CHUNKS:
        inv = inverse(symmetric(ex, low, up))
        a = mul(low, wide(down(inv, shift)))
        b = mul(up, wide(down(inv, -shift)))
        store(ring, (place,), (*a, *b))
        vec = add(vec, mul(a, down(vec, shift)), mul(b, down(vec, -shift)))
        ex = add(ex, mul(a, down(ex, shift)), mul(b, down(ex, -shift)))
        up = mul(b, down(up, -shift))
        shift *= 2
        place += 1
        low = turn(down(up, shift))
    inv = inverse(symmetric(ex))
    store(final, (), inv)
    w = {0: mul(wide(inv), vec)}
    for stride, keep, drop in reversed(list(levels())):
        for i in drop:
            left, right = i - stride, i + stride
            prev = turn(load(ab, PLACE[stride, left])[4:8])
            if right < STEPS:
                after, later = turn(load(ab, PLACE[stride, right])[0:4]), w[right]
            else:
                after, later = turn(down(load(ab, PLACE[stride, 0])[0:4], -1)), down(w[0], -1)
            w[i] = add(mul(prev, w[left]), mul(after, later))
            if i in sides:
                w[i] = add(w[i], mul(wide(load(dinv, i)), sides[i]))
    for i in range(STEPS):
        store(answer, (i,), (w[i][0], w[i][1], SCALE * w[i][2], SCALE * w[i][3]))

    tail = w[STEPS - 1]
    tail = down((tail[0], tail[1], tail[3], kept[2, STEPS - 1]), 1)
    head = (w[0][0], w[0][1], w[0][3], kept[2, 0])
    for j, (x, y) in enumerate(zip(head, tail)):
        share[pl.ds(2 + j, 1), :] = jnp.where(low_line, y, x)[0:1]
    share[pl.ds(0, 2), :] = zero[0:2]
    share[pl.ds(6, 2), :] = zero[0:2]


def finish(k_all, rhs, kept, ab, dinv, ring, final, share, odd, even, local_x, message):
    line = lax.axis_index("line")
    theirs = 1 - lax.rem(lax.axis_index("tile"), 2)
    near = toward_odd()
    half = STEPS // 2
    far_signed = [None] * STEPS
    for i in range(half):
        o, e = odd[STEPS + i], even[theirs, STEPS + i]
        far_signed[i] = roll(jnp.where(near, e, o), XS, 1)
        far_signed[i + half] = jnp.where(near, o, e)
    b = {}
    for i in range(STEPS):
        o, e = odd[i], even[theirs, i]
        far = (roll(jnp.where(near, e, o), XS, 1), jnp.where(near, o, e))
        drop = (far[0] - kept[0, i], far[1] - kept[1, i])
        total = flux(add(load(k_all, i), conduct_or_none(far_signed[i])), drop)
        b[i] = (rhs[0, i] + HALF * total[0], rhs[1, i] + HALF * total[1])
    for stride, keep, _ in levels():
        for i in keep:
            left = i - stride
            prev = b[left] if left >= 0 else down(b[left + STEPS], 1)
            c = load(ab, PLACE[stride, i])
            b[i] = add(b[i], apply(c[0:4], prev), apply(c[4:8], b[i + stride]))
    vec = b[0]
    shift, place = 1, 0
    while shift < CHUNKS:
        c = load(ring, place)
        vec = add(vec, apply(c[0:4], down(vec, shift)), apply(c[4:8], down(vec, -shift)))
        shift *= 2
        place += 1
    x = {0: apply(wide(load(final)), vec)}
    for stride, keep, drop in reversed(list(levels())):
        for i in drop:
            left, right = i - stride, i + stride
            prev = turn(load(ab, PLACE[stride, left])[4:8])
            if right < STEPS:
                after, later = turn(load(ab, PLACE[stride, right])[0:4]), x[right]
            else:
                after, later = turn(down(load(ab, PLACE[stride, 0])[0:4], -1)), down(x[0], -1)
            x[i] = add(apply(wide(load(dinv, i)), b[i]), apply(prev, x[left]), apply(after, later))
    for i in range(STEPS):
        store(local_x, (i,), (x[i][0], SCALE * x[i][1]))
    message[...] = share[...]
    tail = down(x[STEPS - 1], 1)
    for j in range(2):
        message[pl.ds(j, 1), :] = jnp.where(line == 0, tail[j], x[0][j])[0:1]


def join(local_x, answer, both, out_hbm, out, sems):
    line = lax.axis_index("line")

    def row(who, j):
        return jnp.broadcast_to(both[who, pl.ds(j, 1), :], TILE)

    sign = jnp.where(line == 0, 1.0, -1.0)
    drop = tuple(sign * (row(1, j) - row(0, j)) for j in range(2))
    reach = wide(tuple(row(0, 2 + j) + row(1, 2 + j) for j in range(3)))
    face = tuple(HALF * (x + y) for x, y in zip(conduct(row(0, 5)), conduct(row(1, 5))))
    m = mul(wide(face), reach)
    m = (m[0] + 1.0, m[1], m[2], m[3] + 1.0)
    push = flux(face, drop)
    scale = 1.0 / (m[0] * m[3] - m[1] * m[2])
    through = ((m[3] * push[0] - m[1] * push[1]) * scale, (m[0] * push[1] - m[2] * push[0]) * scale)
    copies = [pltpu.make_async_copy(out.at[j], out_hbm.at[j], sems.at[j]) for j in range(2)]
    for j in range(2):
        for i in range(STEPS):
            x = local_x[i, j] + (answer[i, 2 * j] * through[0] + answer[i, 2 * j + 1] * through[1])
            out[j, pl.ds(i, CHUNKS, stride=STEPS), :] = x
        copies[j].start()
    for copy in copies:
        copy.wait()


def tiles(*lead):
    return jax.ShapeDtypeStruct((*lead, *TILE), jnp.float32)


def call(kernel, outs, args, name, flops, **more):
    vmem = pl.BlockSpec(memory_space=pltpu.VMEM)
    more.setdefault("in_specs", [vmem] * len(args))
    if "out_specs" not in more:
        more["out_specs"] = [vmem] * len(outs)
    return pl.pallas_call(
        kernel,
        out_shape=outs,
        compiler_params=pltpu.CompilerParams(vmem_limit_bytes=LIMIT),
        cost_estimate=pl.CostEstimate(flops=flops, bytes_accessed=1 << 20, transcendentals=0),
        name=name,
        **more,
    )(*args)


def body(field, saturation, solid_mask):
    count = lax.axis_size("tile")
    evens = [[t, t + 1] for t in range(0, count, 2)]
    odds = [pair for t in range(1, count - 1, 2) for pair in ((t, t + 1), (t + 1, t))]
    cells = STEPS * CHUNKS
    pack = STEPS + STEPS // 2
    args = [pltpu.with_memory_space_constraint(x, pltpu.HBM) for x in (field, saturation, solid_mask)]
    parts = [
        tiles(pack),
        tiles(STEPS, 3),
        tiles(2, STEPS),
        tiles(STEPS - 1, 8),
        tiles(STEPS, 3),
        tiles(3, 8),
        tiles(3),
        tiles(STEPS, 4),
        jax.ShapeDtypeStruct((8, LANES), jnp.float32),
    ]
    kept, turned, odd, *parts_early = call(
        early,
        [tiles(3, STEPS), tiles(pack), tiles(pack), *parts],
        args,
        "early",
        1 << 16,
        in_specs=[pl.BlockSpec(memory_space=pltpu.HBM)] * 3,
        scratch_shapes=[
            pltpu.VMEM((2, cells, LANES), jnp.float32),
            pltpu.VMEM((cells, LANES), jnp.float32),
            pltpu.VMEM((1, LANES), jnp.int32),
            pltpu.SemaphoreType.DMA((4,)),
        ],
    )
    odd = lax.ppermute(odd, "tile", odds)
    even, k_all, rhs, ab, dinv, ring, final, answer, share = call(
        late,
        parts,
        (kept, turned, *parts_early),
        "late",
        1 << 23,
        input_output_aliases={2 + j: j for j in range(len(parts))},
    )
    even = lax.all_gather(even, "tile", axis_index_groups=evens, axis=0)
    local_x, message = call(
        finish,
        [tiles(STEPS, 2), jax.ShapeDtypeStruct((8, LANES), jnp.float32)],
        (k_all, rhs, kept, ab, dinv, ring, final, share, odd, even),
        "finish",
        1 << 21,
    )
    both = lax.all_gather(message, "line", axis=0)
    return call(
        join,
        jax.ShapeDtypeStruct((2, cells, LANES), jnp.float32),
        (local_x, answer, both),
        "join",
        1 << 18,
        out_specs=pl.BlockSpec(memory_space=pltpu.HBM),
        scratch_shapes=[pltpu.VMEM((2, cells, LANES), jnp.float32), pltpu.SemaphoreType.DMA((2,))],
    )


def solution(mesh):
    in_specs = (P(None, "line", "tile"), P("line", "tile"), P("line", "tile"))
    out_specs = P(None, "line", "tile")
    return jax.shard_map(body, mesh=mesh, in_specs=in_specs, out_specs=out_specs, check_vma=False)
```

```python
import jax
import jax.numpy as jnp
from jax import lax
from jax.experimental import pallas as pl
from jax.experimental.pallas import tpu as pltpu
from jax.sharding import PartitionSpec as P

XS = 64
ZSTIFF = 2048
HALF = 0.5 * ZSTIFF
STEPS = 16
CHUNKS = 8
LANES = 128
TILE = (CHUNKS, LANES)
ROW = 4
SCALE = 0.4**0.5
CROSS = 0.1**0.5
GROW = HALF ** (1.0 / 3.0)
PACK = STEPS + STEPS // 2
LIMIT = 12 * 1024 * 1024


def mul(a, b):
    return (
        a[0] * b[0] + a[1] * b[2],
        a[0] * b[1] + a[1] * b[3],
        a[2] * b[0] + a[3] * b[2],
        a[2] * b[1] + a[3] * b[3],
    )


def wide(s):
    return (s[0], s[1], s[1], s[2])


def turn(a):
    return (a[0], a[2], a[1], a[3])


def apply(a, v):
    return (a[0] * v[0] + a[1] * v[1], a[2] * v[0] + a[3] * v[1])


def add(*items):
    total = items[0]
    for item in items[1:]:
        total = tuple(x + y for x, y in zip(total, item))
    return total


def symmetric(a, *more):
    return add(*((m[0], m[1], m[3]) for m in (a, *more)))


def inverse(s):
    scale = 1.0 / (s[0] * s[2] - s[1] * s[1])
    return (s[2] * scale, -s[1] * scale, s[0] * scale)


def conduct(signed, inside=None):
    dry = jnp.maximum(signed, 0.0)
    moist = HALF * 0.004 + dry * dry * dry
    pore = signed > 0.0
    heat = jnp.where(pore, HALF + (2.0 * HALF / GROW) * signed, 3.0 * HALF)
    cross = jnp.where(pore, CROSS * moist, 0.0)
    if inside is None:
        return (heat, cross, moist)
    return (jnp.where(inside, heat, 0.0), cross, jnp.where(inside, moist, 0.0))


def flux(k, drop):
    return (k[0] * drop[0] + k[1] * drop[1], k[1] * drop[0] + k[2] * drop[1])


def roll(x, shift, axis):
    return pltpu.roll(x, shift % x.shape[axis], axis)


def down(items, shift):
    return tuple(roll(x, shift, 0) for x in items)


def lanes():
    return lax.broadcasted_iota(jnp.int32, TILE, 1)


def chunks():
    return lax.broadcasted_iota(jnp.int32, TILE, 0)


def toward_odd():
    parity = lax.rem(lax.axis_index("tile"), 2)
    return (lanes() >= XS) == (parity == 1)


def load(ref, *index):
    return tuple(ref[(*index, j)] for j in range(ref.shape[len(index)]))


def store(ref, index, items):
    for j, item in enumerate(items):
        ref[(*index, j)] = item


def levels():
    stride = 1
    while stride < STEPS:
        yield stride, range(0, STEPS, 2 * stride), range(stride, STEPS, 2 * stride)
        stride *= 2


def rows_of():
    place, at = {}, 0
    for stride, kept, _ in levels():
        for step in kept:
            place[stride, step] = at
            at += 1
    return place


PLACE = rows_of()


def pack_even(kept, turned, even):
    near = toward_odd()
    half = STEPS // 2
    for i in range(STEPS):
        even[i] = jnp.where(near, turned[i], kept[0, i])
    for i in range(half):
        even[STEPS + i] = jnp.where(near, turned[STEPS + i], kept[2, i])


def signs(mask, sign):
    sign[...] = jnp.where(jnp.broadcast_to(mask[...], TILE) > 0, -GROW, GROW)


def prepare(field, sat, sign, kept, turned, odd):
    near = toward_odd()
    half = STEPS // 2
    rows = [pl.ds(i, CHUNKS, stride=STEPS) for i in range(STEPS)]
    sign = sign[...]
    for i in range(STEPS):
        f1 = field[1, rows[i], :] * (1.0 / SCALE)
        kept[1, i] = f1
        turned[i] = roll(f1, XS, 1)
    for i in range(STEPS):
        s = sat[rows[i], :] * sign
        kept[2, i] = s
        if i >= half:
            high = roll(s, XS, 1)
            turned[STEPS + i - half] = high
            odd[STEPS + i - half] = jnp.where(near, kept[2, i - half], high)
    for i in range(STEPS):
        f0 = field[0, rows[i], :]
        kept[0, i] = f0
        odd[i] = jnp.where(near, f0, turned[i])


def tile():
    return lax.axis_index("tile")


def at_row_end():
    place = lax.rem(lax.axis_index("tile"), ROW)
    return jnp.logical_or(place == 0, place == ROW - 1)


def inner(field_hbm, sat_hbm, mask_hbm, kept, turned, odd, even, fbuf, sbuf, mbuf, gbuf, sems):
    @pl.when(jnp.logical_not(at_row_end()))
    def _():
        copies = [
            pltpu.make_async_copy(field_hbm, fbuf, sems.at[0]),
            pltpu.make_async_copy(sat_hbm, sbuf, sems.at[1]),
            pltpu.make_async_copy(mask_hbm, mbuf, sems.at[2]),
        ]
        for copy in copies:
            copy.start()
        for copy in copies:
            copy.wait()
        signs(mbuf, gbuf)
        prepare(fbuf, sbuf, gbuf, kept, turned, odd)
        pack_even(kept, turned, even)

    @pl.when(jnp.logical_and(tile() >= 1, tile() <= 2))
    def _():
        for i in range(PACK):
            odd[i], even[i] = even[i], odd[i]


def ends(field, sat, sign, kept_in, turned_in, odd_in, kept, turned, odd):
    @pl.when(at_row_end())
    def _():
        prepare(field, sat, sign, kept, turned, odd)

    @pl.when(tile() == 0)
    def _():
        pack_even(kept, turned, odd)


def third(kept, turned, first, arrived, out):
    @pl.when(tile() != 1)
    def _():
        pack_even(kept, turned, out)

    @pl.when(tile() == 1)
    def _():
        for i in range(PACK):
            out[i] = first[i]


def local(kept, turned, k_all, rhs, ab, dinv, ring, final, answer, share):
    line = lax.axis_index("line")
    first, last = chunks() == 0, chunks() == CHUNKS - 1
    low_line, high_line = line == 0, line == 1
    column = lax.rem(lanes(), XS)
    west_end, east_end = column == 0, column == XS - 1
    half = STEPS // 2

    k = []
    for i in range(STEPS):
        s = kept[2, i]
        ki = conduct(s)
        k.append(ki)
        store(k_all, (i,), ki)
        f = (kept[0, i], kept[1, i])
        far = (roll(f[0], XS, 1), turned[i])
        far_s = turned[STEPS + i - half] if i >= half else roll(s, XS, 1)
        total = flux(add(ki, conduct(far_s)), (far[0] - f[0], far[1] - f[1]))
        west_k = conduct(roll(s, 1, 1))
        west = flux(add(ki, west_k), (roll(f[0], 1, 1) - f[0], roll(f[1], 1, 1) - f[1]))
        edge = flux(ki, f)
        west = tuple(jnp.where(west_end, -e, w) for e, w in zip(edge, west))
        east = tuple(jnp.where(east_end, e, roll(w, -1, 1)) for e, w in zip(edge, west))
        for j in range(2):
            rhs[j, i] = f[j] + (total[j] + (west[j] - east[j]))

    upper = {i: wide(add(k[i], k[i + 1])) for i in range(STEPS - 1)}
    upper[STEPS - 1] = wide(tuple(jnp.where(last, 0.0, x) for x in add(k[-1], down(k[0], -1))))
    bottom = jnp.logical_and(first, low_line)
    top = jnp.logical_and(last, high_line)
    bottom = tuple(jnp.where(bottom, x, 0.0) for x in k[0])
    top = tuple(jnp.where(top, x, 0.0) for x in k[-1])
    excess = {}

    for stride, keep, drop in levels():
        lower = {}
        for i in (*keep, *drop):
            left = i - stride
            lower[i] = turn(upper[left] if left >= 0 else down(upper[left + STEPS], 1))
        inv = {}
        for i in drop:
            if stride == 1:
                d = symmetric(lower[i], upper[i])
                d = (d[0] + 1.0, d[1], d[2] + 1.0)
                if i == STEPS - 1:
                    d = add(d, top)
            else:
                d = symmetric(excess[i], lower[i], upper[i])
            inv[i] = inverse(d)
            store(dinv, (i,), inv[i])
        for i in keep:
            right, left = i + stride, i - stride
            if left < 0:
                before = wide(down(inv[left + STEPS], 1))
            else:
                before = wide(inv[left])
            a = mul(lower[i], before)
            b = mul(upper[i], wide(inv[right]))
            store(ab, (PLACE[stride, i],), (*a, *b))
            if stride == 1:
                more = add(a, b)
                more = (more[0] + 1.0, more[1], more[2], more[3] + 1.0)
                if i == 0:
                    more = add(more, wide(bottom))
                if right == STEPS - 1:
                    more = add(more, mul(b, wide(top)))
            else:
                prev = excess[left] if left >= 0 else down(excess[left + STEPS], 1)
                more = add(excess[i], mul(a, prev), mul(b, excess[right]))
            excess[i] = more
            upper[i] = mul(b, upper[right])

    start = jnp.where(jnp.logical_and(high_line, first), 1.0, 0.0)
    end = jnp.logical_and(low_line, last)
    one = jnp.where(end, 1.0, 0.0)
    none = jnp.zeros(TILE, jnp.float32)
    source = (one, none, none, one)
    sides = {STEPS - 1: source}
    for stride, keep, _ in levels():
        b = load(ab, PLACE[stride, keep[-1]])[4:8]
        source = tuple(jnp.where(end, x, 0.0) for x in b) if stride == 1 else mul(b, source)
        sides[keep[-1]] = source
    vec = (source[0] + start, source[1], source[2], source[3] + start)

    up, ex = upper[0], excess[0]
    low = turn(down(up, 1))
    shift, place = 1, 0
    while shift < CHUNKS:
        inv = inverse(symmetric(ex, low, up))
        a = mul(low, wide(down(inv, shift)))
        b = mul(up, wide(down(inv, -shift)))
        store(ring, (place,), (*a, *b))
        vec = add(vec, mul(a, down(vec, shift)), mul(b, down(vec, -shift)))
        ex = add(ex, mul(a, down(ex, shift)), mul(b, down(ex, -shift)))
        up = mul(b, down(up, -shift))
        shift *= 2
        place += 1
        low = turn(down(up, shift))
    inv = inverse((ex[0], ex[1], ex[3]))
    store(final, (), inv)
    w = {0: mul(wide(inv), vec)}
    for stride, keep, drop in reversed(list(levels())):
        for i in drop:
            left, right = i - stride, i + stride
            prev = turn(load(ab, PLACE[stride, left])[4:8])
            if right < STEPS:
                after, later = turn(load(ab, PLACE[stride, right])[0:4]), w[right]
            else:
                after, later = turn(down(load(ab, PLACE[stride, 0])[0:4], -1)), down(w[0], -1)
            w[i] = add(mul(prev, w[left]), mul(after, later))
            if i in sides:
                w[i] = add(w[i], mul(wide(load(dinv, i)), sides[i]))
    for i in range(STEPS):
        for j, x in enumerate((w[i][0], w[i][1], SCALE * w[i][2], SCALE * w[i][3])):
            answer[j, pl.ds(i, CHUNKS, stride=STEPS), :] = x

    tail = down((w[STEPS - 1][0], w[STEPS - 1][1], w[STEPS - 1][3], kept[2, STEPS - 1]), 1)
    head = (w[0][0], w[0][1], w[0][3], kept[2, 0])
    for j, (x, y) in enumerate(zip(head, tail)):
        share[pl.ds(2 + j, 1), :] = jnp.where(low_line, y, x)[0:1]
    share[pl.ds(0, 2), :] = none[0:2]
    share[pl.ds(6, 2), :] = none[0:2]


def finish(k_all, rhs, kept, ab, dinv, ring, final, share, one, two, four, three, local_x, message):
    rest = (k_all, rhs, kept, ab, dinv, ring, final, share, local_x, message)

    @pl.when(tile() >= ROW)
    def _():
        end = at_row_end()
        solve(lambda i: (two[i], jnp.where(end, one[i], three[i])), *rest)

    @pl.when(tile() < ROW)
    def _():
        at = tile()

        def halo(i):
            odd = jnp.where(at <= 1, one[i], jnp.where(at == 2, three[i], two[i]))
            return odd, jnp.where(at <= 1, two[i], four[i])

        solve(halo, *rest)


def solve(halo, k_all, rhs, kept, ab, dinv, ring, final, share, local_x, message):
    line = lax.axis_index("line")
    near = toward_odd()
    alone = jnp.logical_or(tile() == 0, tile() == lax.axis_size("tile") - 1)
    inside = jnp.logical_not(jnp.logical_and(near, alone))
    half = STEPS // 2
    far_s, far_0, far_1 = [None] * STEPS, [], []
    for i in range(half):
        o, e = halo(STEPS + i)
        far_s[i] = roll(jnp.where(near, e, o), XS, 1)
        far_s[i + half] = jnp.where(near, o, e)
    for i in range(STEPS):
        o, e = halo(i)
        far_0.append(roll(jnp.where(near, e, o), XS, 1))
        far_1.append(jnp.where(near, o, e))
    b = {}
    for i in range(STEPS):
        drop = (far_0[i] - kept[0, i], far_1[i] - kept[1, i])
        total = flux(add(load(k_all, i), conduct(far_s[i], inside)), drop)
        b[i] = (rhs[0, i] + total[0], rhs[1, i] + total[1])
    for stride, keep, drop in levels():
        for i in keep:
            left = i - stride
            prev = b[left] if left >= 0 else down(b[left + STEPS], 1)
            c = load(ab, PLACE[stride, i])
            b[i] = add(b[i], apply(c[0:4], prev), apply(c[4:8], b[i + stride]))
    vec = b[0]
    shift, place = 1, 0
    while shift < CHUNKS:
        c = load(ring, place)
        vec = add(vec, apply(c[0:4], down(vec, shift)), apply(c[4:8], down(vec, -shift)))
        shift *= 2
        place += 1
    x = {0: apply(wide(load(final)), vec)}
    for stride, keep, drop in reversed(list(levels())):
        for i in drop:
            left, right = i - stride, i + stride
            prev = turn(load(ab, PLACE[stride, left])[4:8])
            if right < STEPS:
                after, later = turn(load(ab, PLACE[stride, right])[0:4]), x[right]
            else:
                after, later = turn(down(load(ab, PLACE[stride, 0])[0:4], -1)), down(x[0], -1)
            x[i] = add(apply(wide(load(dinv, i)), b[i]), apply(prev, x[left]), apply(after, later))
    message[...] = share[...]
    tail = down(x[STEPS - 1], 1)
    for j in range(2):
        message[pl.ds(j, 1), :] = jnp.where(line == 0, tail[j], x[0][j])[0:1]
    for i in range(STEPS):
        here = pl.ds(i, CHUNKS, stride=STEPS)
        local_x[0, here, :] = x[i][0]
        local_x[1, here, :] = SCALE * x[i][1]


def join(local_x, answer, both, out_hbm, out, sems):
    line = lax.axis_index("line")

    def row(who, j):
        return jnp.broadcast_to(both[who, pl.ds(j, 1), :], TILE)

    sign = jnp.where(line == 0, 1.0, -1.0)
    drop = tuple(sign * (row(1, j) - row(0, j)) for j in range(2))
    reach = wide(tuple(row(0, 2 + j) + row(1, 2 + j) for j in range(3)))
    face = add(conduct(row(0, 5)), conduct(row(1, 5)))
    m = mul(wide(face), reach)
    m = (m[0] + 1.0, m[1], m[2], m[3] + 1.0)
    push = flux(face, drop)
    scale = 1.0 / (m[0] * m[3] - m[1] * m[2])
    through = ((m[3] * push[0] - m[1] * push[1]) * scale, (m[0] * push[1] - m[2] * push[0]) * scale)

    copies = [pltpu.make_async_copy(out.at[j], out_hbm.at[j], sems.at[j]) for j in range(2)]
    for j in range(2):
        for i in range(STEPS):
            here = pl.ds(i * CHUNKS, CHUNKS)
            change = answer[2 * j, here, :] * through[0] + answer[2 * j + 1, here, :] * through[1]
            out[j, here, :] = local_x[j, here, :] + change
        copies[j].start()
    for copy in copies:
        copy.wait()


def tiles(*lead):
    return jax.ShapeDtypeStruct((*lead, *TILE), jnp.float32)


def call(kernel, outs, args, name, flops, **more):
    vmem = pl.BlockSpec(memory_space=pltpu.VMEM)
    more.setdefault("in_specs", [vmem] * len(args))
    if "out_specs" not in more:
        more["out_specs"] = [vmem] * len(outs)
    return pl.pallas_call(
        kernel,
        out_shape=outs,
        compiler_params=pltpu.CompilerParams(vmem_limit_bytes=LIMIT),
        cost_estimate=pl.CostEstimate(flops=flops, bytes_accessed=1 << 20, transcendentals=0),
        name=name,
        **more,
    )(*args)


def moves(count):
    first, second, third = [(2, 1)], [(0, 1), (1, 0)], [(1, 2)]
    for t in range(ROW, count, ROW):
        first += [(t + 1, t), (t + 2, t + 3)]
        second += [(t - 1, t), (t, t - 1), (t + 1, t + 2), (t + 2, t + 1)]
        third += [(t, t + 1), (t + 3, t + 2)]
    return first, second, third, [(2, 3), (3, 2)]


def body(field, saturation, solid_mask):
    first, second, third_moves, fourth_moves = moves(lax.axis_size("tile"))
    cells = STEPS * CHUNKS
    in_hbm = [pltpu.with_memory_space_constraint(x, pltpu.HBM) for x in (field, saturation, solid_mask)]
    kept, turned, two, one = call(
        inner,
        [tiles(3, STEPS), tiles(PACK), tiles(PACK), tiles(PACK)],
        in_hbm,
        "inner",
        1 << 16,
        in_specs=[pl.BlockSpec(memory_space=pltpu.HBM)] * 3,
        scratch_shapes=[
            pltpu.VMEM((2, cells, LANES), jnp.float32),
            pltpu.VMEM((cells, LANES), jnp.float32),
            pltpu.VMEM((1, LANES), jnp.int32),
            pltpu.VMEM(TILE, jnp.float32),
            pltpu.SemaphoreType.DMA((3,)),
        ],
    )
    from_one = lax.ppermute(one, "tile", first)
    (sign,) = call(signs, [tiles()], (solid_mask,), "signs", 1 << 8)
    kept, turned, two = call(
        ends,
        [tiles(3, STEPS), tiles(PACK), tiles(PACK)],
        (field, saturation, sign, kept, turned, two),
        "ends",
        1 << 16,
        input_output_aliases={3: 0, 4: 1, 5: 2},
    )
    from_two = lax.ppermute(two, "tile", second)
    (three,) = call(third, [tiles(PACK)], (kept, turned, one, from_one), "third", 1 << 12)
    from_three = lax.ppermute(three, "tile", third_moves)
    from_four = lax.ppermute(three, "tile", fourth_moves)
    k_all, rhs, ab, dinv, ring, final, answer, share = call(
        local,
        [
            tiles(STEPS, 3),
            tiles(2, STEPS),
            tiles(STEPS - 1, 8),
            tiles(STEPS, 3),
            tiles(3, 8),
            tiles(3),
            jax.ShapeDtypeStruct((4, cells, LANES), jnp.float32),
            jax.ShapeDtypeStruct((8, LANES), jnp.float32),
        ],
        (kept, turned),
        "local",
        1 << 23,
    )
    local_x, message = call(
        finish,
        [jax.ShapeDtypeStruct((2, cells, LANES), jnp.float32), jax.ShapeDtypeStruct((8, LANES), jnp.float32)],
        (k_all, rhs, kept, ab, dinv, ring, final, share, from_one, from_two, from_four, from_three),
        "finish",
        1 << 21,
    )
    both = lax.all_gather(message, "line", axis=0)
    return call(
        join,
        jax.ShapeDtypeStruct((2, cells, LANES), jnp.float32),
        (local_x, answer, both),
        "join",
        1 << 18,
        out_specs=pl.BlockSpec(memory_space=pltpu.HBM),
        scratch_shapes=[pltpu.VMEM((2, cells, LANES), jnp.float32), pltpu.SemaphoreType.DMA((2,))],
    )


def solution(mesh):
    in_specs = (P(None, "line", "tile"), P("line", "tile"), P("line", "tile"))
    out_specs = P(None, "line", "tile")
    return jax.shard_map(body, mesh=mesh, in_specs=in_specs, out_specs=out_specs, check_vma=False)
```

```python
import jax
import jax.numpy as jnp
from jax import lax
from jax.experimental import pallas as pl
from jax.experimental.pallas import tpu as pltpu
from jax.sharding import PartitionSpec as P

XS = 64
ZSTIFF = 2048
HALF = 0.5 * ZSTIFF
STEPS = 16
CHUNKS = 8
LANES = 128
TILE = (CHUNKS, LANES)
ROW = 4
SCALE = 0.4**0.5
CROSS = 0.1**0.5
GROW = HALF ** (1.0 / 3.0)
PACK = STEPS + STEPS // 2
LIMIT = 12 * 1024 * 1024


def mul(a, b):
    return (
        a[0] * b[0] + a[1] * b[2],
        a[0] * b[1] + a[1] * b[3],
        a[2] * b[0] + a[3] * b[2],
        a[2] * b[1] + a[3] * b[3],
    )


def wide(s):
    return (s[0], s[1], s[1], s[2])


def turn(a):
    return (a[0], a[2], a[1], a[3])


def apply(a, v):
    return (a[0] * v[0] + a[1] * v[1], a[2] * v[0] + a[3] * v[1])


def add(*items):
    total = items[0]
    for item in items[1:]:
        total = tuple(x + y for x, y in zip(total, item))
    return total


def symmetric(a, *more):
    return add(*((m[0], m[1], m[3]) for m in (a, *more)))


def inverse(s):
    scale = 1.0 / (s[0] * s[2] - s[1] * s[1])
    return (s[2] * scale, -s[1] * scale, s[0] * scale)


def conduct(signed, inside=None):
    dry = jnp.maximum(signed, 0.0)
    moist = HALF * 0.004 + dry * dry * dry
    pore = signed > 0.0
    heat = jnp.where(pore, HALF + (2.0 * HALF / GROW) * signed, 3.0 * HALF)
    cross = jnp.where(pore, CROSS * moist, 0.0)
    if inside is None:
        return (heat, cross, moist)
    return (jnp.where(inside, heat, 0.0), cross, jnp.where(inside, moist, 0.0))


def flux(k, drop):
    return (k[0] * drop[0] + k[1] * drop[1], k[1] * drop[0] + k[2] * drop[1])


def roll(x, shift, axis):
    return pltpu.roll(x, shift % x.shape[axis], axis)


def down(items, shift):
    return tuple(roll(x, shift, 0) for x in items)


def lanes():
    return lax.broadcasted_iota(jnp.int32, TILE, 1)


def chunks():
    return lax.broadcasted_iota(jnp.int32, TILE, 0)


def toward_odd():
    parity = lax.rem(lax.axis_index("tile"), 2)
    return (lanes() >= XS) == (parity == 1)


def load(ref, *index):
    return tuple(ref[(*index, j)] for j in range(ref.shape[len(index)]))


def store(ref, index, items):
    for j, item in enumerate(items):
        ref[(*index, j)] = item


def levels():
    stride = 1
    while stride < STEPS:
        yield stride, range(0, STEPS, 2 * stride), range(stride, STEPS, 2 * stride)
        stride *= 2


def rows_of():
    place, at = {}, 0
    for stride, kept, _ in levels():
        for step in kept:
            place[stride, step] = at
            at += 1
    return place


PLACE = rows_of()


def pack_even(kept, turned, even):
    near = toward_odd()
    half = STEPS // 2
    for i in range(STEPS):
        even[i] = jnp.where(near, turned[i], kept[0, i])
    for i in range(half):
        even[STEPS + i] = jnp.where(near, turned[STEPS + i], kept[2, i])


def signs(mask, sign):
    sign[...] = jnp.where(jnp.broadcast_to(mask[...], TILE) > 0, -GROW, GROW)


def prepare(field, sat, sign, kept, turned, odd):
    near = toward_odd()
    half = STEPS // 2
    rows = [pl.ds(i, CHUNKS, stride=STEPS) for i in range(STEPS)]
    sign = sign[...]
    for i in range(STEPS):
        f1 = field[1, rows[i], :] * (1.0 / SCALE)
        kept[1, i] = f1
        turned[i] = roll(f1, XS, 1)
    for i in range(STEPS):
        s = sat[rows[i], :] * sign
        kept[2, i] = s
        if i >= half:
            high = roll(s, XS, 1)
            turned[STEPS + i - half] = high
            odd[STEPS + i - half] = jnp.where(near, kept[2, i - half], high)
    for i in range(STEPS):
        f0 = field[0, rows[i], :]
        kept[0, i] = f0
        odd[i] = jnp.where(near, f0, turned[i])


def tile():
    return lax.axis_index("tile")


def line():
    return lax.axis_index("line")


def at_row_end():
    place = lax.rem(lax.axis_index("tile"), ROW)
    return jnp.logical_or(place == 0, place == ROW - 1)


def inner(field_hbm, sat_hbm, mask_hbm, kept, turned, odd, even, fbuf, sbuf, mbuf, gbuf, sems):
    @pl.when(jnp.logical_not(at_row_end()))
    def _():
        copies = [
            pltpu.make_async_copy(field_hbm, fbuf, sems.at[0]),
            pltpu.make_async_copy(sat_hbm, sbuf, sems.at[1]),
            pltpu.make_async_copy(mask_hbm, mbuf, sems.at[2]),
        ]
        for copy in copies:
            copy.start()
        for copy in copies:
            copy.wait()
        signs(mbuf, gbuf)
        prepare(fbuf, sbuf, gbuf, kept, turned, odd)
        pack_even(kept, turned, even)

    @pl.when(jnp.logical_or(tile() == 2, jnp.logical_and(tile() == 1, line() == 1)))
    def _():
        for i in range(PACK):
            odd[i], even[i] = even[i], odd[i]


def ends(field, sat, sign, kept_in, turned_in, odd_in, kept, turned, odd):
    @pl.when(at_row_end())
    def _():
        prepare(field, sat, sign, kept, turned, odd)

    @pl.when(tile() == 0)
    def _():
        pack_even(kept, turned, odd)


def third(kept, turned, arrived, out):
    relay = jnp.logical_and(tile() == 0, line() == 1)

    @pl.when(jnp.logical_not(relay))
    def _():
        pack_even(kept, turned, out)

    @pl.when(relay)
    def _():
        for i in range(PACK):
            out[i] = arrived[i]


def local(kept, turned, k_all, rhs, ab, dinv, ring, final, answer, share):
    first, last = chunks() == 0, chunks() == CHUNKS - 1
    low_line, high_line = line() == 0, line() == 1
    column = lax.rem(lanes(), XS)
    west_end, east_end = column == 0, column == XS - 1
    half = STEPS // 2

    k = []
    for i in range(STEPS):
        s = kept[2, i]
        ki = conduct(s)
        k.append(ki)
        store(k_all, (i,), ki)
        f = (kept[0, i], kept[1, i])
        far = (roll(f[0], XS, 1), turned[i])
        far_s = turned[STEPS + i - half] if i >= half else roll(s, XS, 1)
        total = flux(add(ki, conduct(far_s)), (far[0] - f[0], far[1] - f[1]))
        west_k = conduct(roll(s, 1, 1))
        west = flux(add(ki, west_k), (roll(f[0], 1, 1) - f[0], roll(f[1], 1, 1) - f[1]))
        edge = flux(ki, f)
        west = tuple(jnp.where(west_end, -e, w) for e, w in zip(edge, west))
        east = tuple(jnp.where(east_end, e, roll(w, -1, 1)) for e, w in zip(edge, west))
        for j in range(2):
            rhs[j, i] = f[j] + (total[j] + (west[j] - east[j]))

    upper = {i: wide(add(k[i], k[i + 1])) for i in range(STEPS - 1)}
    upper[STEPS - 1] = wide(tuple(jnp.where(last, 0.0, x) for x in add(k[-1], down(k[0], -1))))
    bottom = jnp.logical_and(first, low_line)
    top = jnp.logical_and(last, high_line)
    bottom = tuple(jnp.where(bottom, x, 0.0) for x in k[0])
    top = tuple(jnp.where(top, x, 0.0) for x in k[-1])
    excess = {}

    for stride, keep, drop in levels():
        lower = {}
        for i in (*keep, *drop):
            left = i - stride
            lower[i] = turn(upper[left] if left >= 0 else down(upper[left + STEPS], 1))
        inv = {}
        for i in drop:
            if stride == 1:
                d = symmetric(lower[i], upper[i])
                d = (d[0] + 1.0, d[1], d[2] + 1.0)
                if i == STEPS - 1:
                    d = add(d, top)
            else:
                d = symmetric(excess[i], lower[i], upper[i])
            inv[i] = inverse(d)
            store(dinv, (i,), inv[i])
        for i in keep:
            right, left = i + stride, i - stride
            if left < 0:
                before = wide(down(inv[left + STEPS], 1))
            else:
                before = wide(inv[left])
            a = mul(lower[i], before)
            b = mul(upper[i], wide(inv[right]))
            store(ab, (PLACE[stride, i],), (*a, *b))
            if stride == 1:
                more = add(a, b)
                more = (more[0] + 1.0, more[1], more[2], more[3] + 1.0)
                if i == 0:
                    more = add(more, wide(bottom))
                if right == STEPS - 1:
                    more = add(more, mul(b, wide(top)))
            else:
                prev = excess[left] if left >= 0 else down(excess[left + STEPS], 1)
                more = add(excess[i], mul(a, prev), mul(b, excess[right]))
            excess[i] = more
            upper[i] = mul(b, upper[right])

    start = jnp.where(jnp.logical_and(high_line, first), 1.0, 0.0)
    end = jnp.logical_and(low_line, last)
    one = jnp.where(end, 1.0, 0.0)
    none = jnp.zeros(TILE, jnp.float32)
    source = (one, none, none, one)
    sides = {STEPS - 1: source}
    for stride, keep, _ in levels():
        b = load(ab, PLACE[stride, keep[-1]])[4:8]
        source = tuple(jnp.where(end, x, 0.0) for x in b) if stride == 1 else mul(b, source)
        sides[keep[-1]] = source
    vec = (source[0] + start, source[1], source[2], source[3] + start)

    up, ex = upper[0], excess[0]
    low = turn(down(up, 1))
    shift, place = 1, 0
    while shift < CHUNKS:
        inv = inverse(symmetric(ex, low, up))
        a = mul(low, wide(down(inv, shift)))
        b = mul(up, wide(down(inv, -shift)))
        store(ring, (place,), (*a, *b))
        vec = add(vec, mul(a, down(vec, shift)), mul(b, down(vec, -shift)))
        ex = add(ex, mul(a, down(ex, shift)), mul(b, down(ex, -shift)))
        up = mul(b, down(up, -shift))
        shift *= 2
        place += 1
        low = turn(down(up, shift))
    inv = inverse((ex[0], ex[1], ex[3]))
    store(final, (), inv)
    w = {0: mul(wide(inv), vec)}
    for stride, keep, drop in reversed(list(levels())):
        for i in drop:
            left, right = i - stride, i + stride
            prev = turn(load(ab, PLACE[stride, left])[4:8])
            if right < STEPS:
                after, later = turn(load(ab, PLACE[stride, right])[0:4]), w[right]
            else:
                after, later = turn(down(load(ab, PLACE[stride, 0])[0:4], -1)), down(w[0], -1)
            w[i] = add(mul(prev, w[left]), mul(after, later))
            if i in sides:
                w[i] = add(w[i], mul(wide(load(dinv, i)), sides[i]))
    for i in range(STEPS):
        for j, x in enumerate((w[i][0], w[i][1], SCALE * w[i][2], SCALE * w[i][3])):
            answer[j, pl.ds(i, CHUNKS, stride=STEPS), :] = x

    tail = down((w[STEPS - 1][0], w[STEPS - 1][1], w[STEPS - 1][3], kept[2, STEPS - 1]), 1)
    head = (w[0][0], w[0][1], w[0][3], kept[2, 0])
    for j, (x, y) in enumerate(zip(head, tail)):
        share[pl.ds(2 + j, 1), :] = jnp.where(low_line, y, x)[0:1]
    share[pl.ds(0, 2), :] = none[0:2]
    share[pl.ds(6, 2), :] = none[0:2]


def finish(k_all, rhs, kept, ab, dinv, ring, final, share, one, two, three, local_x, message):
    rest = (k_all, rhs, kept, ab, dinv, ring, final, share, local_x, message)

    @pl.when(tile() >= ROW)
    def _():
        place = lax.rem(tile(), ROW)
        solve(lambda i: (two[i], jnp.where(place == 0, one[i], three[i])), *rest)

    @pl.when(tile() < ROW)
    def _():
        at, high = tile(), line() == 1

        def halo(i):
            odd = jnp.where(at == 1, one[i], two[i])
            odd = jnp.where(jnp.logical_and(high, at == 2), one[i], odd)
            odd = jnp.where(jnp.logical_and(high, at == 0), three[i], odd)
            even = jnp.where(jnp.logical_or(at == 1, jnp.logical_and(high, at == 0)), two[i], three[i])
            return odd, even

        solve(halo, *rest)


def solve(halo, k_all, rhs, kept, ab, dinv, ring, final, share, local_x, message):
    near = toward_odd()
    alone = jnp.logical_or(tile() == 0, tile() == lax.axis_size("tile") - 1)
    inside = jnp.logical_not(jnp.logical_and(near, alone))
    half = STEPS // 2
    far_s, far_0, far_1 = [None] * STEPS, [], []
    for i in range(half):
        o, e = halo(STEPS + i)
        far_s[i] = roll(jnp.where(near, e, o), XS, 1)
        far_s[i + half] = jnp.where(near, o, e)
    for i in range(STEPS):
        o, e = halo(i)
        far_0.append(roll(jnp.where(near, e, o), XS, 1))
        far_1.append(jnp.where(near, o, e))
    b = {}
    for i in range(STEPS):
        drop = (far_0[i] - kept[0, i], far_1[i] - kept[1, i])
        total = flux(add(load(k_all, i), conduct(far_s[i], inside)), drop)
        b[i] = (rhs[0, i] + total[0], rhs[1, i] + total[1])
    for stride, keep, drop in levels():
        for i in keep:
            left = i - stride
            prev = b[left] if left >= 0 else down(b[left + STEPS], 1)
            c = load(ab, PLACE[stride, i])
            b[i] = add(b[i], apply(c[0:4], prev), apply(c[4:8], b[i + stride]))
    vec = b[0]
    shift, place = 1, 0
    while shift < CHUNKS:
        c = load(ring, place)
        vec = add(vec, apply(c[0:4], down(vec, shift)), apply(c[4:8], down(vec, -shift)))
        shift *= 2
        place += 1
    x = {0: apply(wide(load(final)), vec)}
    for stride, keep, drop in reversed(list(levels())):
        for i in drop:
            left, right = i - stride, i + stride
            prev = turn(load(ab, PLACE[stride, left])[4:8])
            if right < STEPS:
                after, later = turn(load(ab, PLACE[stride, right])[0:4]), x[right]
            else:
                after, later = turn(down(load(ab, PLACE[stride, 0])[0:4], -1)), down(x[0], -1)
            x[i] = add(apply(wide(load(dinv, i)), b[i]), apply(prev, x[left]), apply(after, later))
    message[...] = share[...]
    tail = down(x[STEPS - 1], 1)
    for j in range(2):
        message[pl.ds(j, 1), :] = jnp.where(line() == 0, tail[j], x[0][j])[0:1]
    for i in range(STEPS):
        here = pl.ds(i, CHUNKS, stride=STEPS)
        local_x[0, here, :] = x[i][0]
        local_x[1, here, :] = SCALE * x[i][1]


def join(local_x, answer, both, out_hbm, out, sems):
    def row(who, j):
        return jnp.broadcast_to(both[who, pl.ds(j, 1), :], TILE)

    sign = jnp.where(line() == 0, 1.0, -1.0)
    drop = tuple(sign * (row(1, j) - row(0, j)) for j in range(2))
    reach = wide(tuple(row(0, 2 + j) + row(1, 2 + j) for j in range(3)))
    face = add(conduct(row(0, 5)), conduct(row(1, 5)))
    m = mul(wide(face), reach)
    m = (m[0] + 1.0, m[1], m[2], m[3] + 1.0)
    push = flux(face, drop)
    scale = 1.0 / (m[0] * m[3] - m[1] * m[2])
    through = ((m[3] * push[0] - m[1] * push[1]) * scale, (m[0] * push[1] - m[2] * push[0]) * scale)

    copies = [pltpu.make_async_copy(out.at[j], out_hbm.at[j], sems.at[j]) for j in range(2)]
    for j in range(2):
        for i in range(STEPS):
            here = pl.ds(i * CHUNKS, CHUNKS)
            change = answer[2 * j, here, :] * through[0] + answer[2 * j + 1, here, :] * through[1]
            out[j, here, :] = local_x[j, here, :] + change
        copies[j].start()
    for copy in copies:
        copy.wait()


def tiles(*lead):
    return jax.ShapeDtypeStruct((*lead, *TILE), jnp.float32)


def call(kernel, outs, args, name, flops, **more):
    vmem = pl.BlockSpec(memory_space=pltpu.VMEM)
    more.setdefault("in_specs", [vmem] * len(args))
    if "out_specs" not in more:
        more["out_specs"] = [vmem] * len(outs)
    return pl.pallas_call(
        kernel,
        out_shape=outs,
        compiler_params=pltpu.CompilerParams(vmem_limit_bytes=LIMIT),
        cost_estimate=pl.CostEstimate(flops=flops, bytes_accessed=1 << 20, transcendentals=0),
        name=name,
        **more,
    )(*args)


def moves(count):
    ops = [[], [], []]
    for base in (0, count):
        for t in range(base, base + count, ROW):
            ops[2] += [(t + 2, t + 3), (t + 3, t + 2)]
            if t > base:
                ops[0].append((t + 1, t))
                ops[1] += [(t - 1, t), (t, t - 1), (t + 1, t + 2), (t + 2, t + 1)]
                ops[2].append((t, t + 1))
    ops[0] += [(1, count), (2, 1), (count + 1, count + 2), (count + 2, count + 1)]
    ops[1] += [(0, 1), (1, 2), (count, count + 1), (count + 1, count)]
    ops[2].append((count, 0))
    return ops


def body(field, saturation, solid_mask):
    ops = moves(lax.axis_size("tile"))
    both_axes = ("line", "tile")
    cells = STEPS * CHUNKS
    in_hbm = [pltpu.with_memory_space_constraint(x, pltpu.HBM) for x in (field, saturation, solid_mask)]
    kept, turned, two, one = call(
        inner,
        [tiles(3, STEPS), tiles(PACK), tiles(PACK), tiles(PACK)],
        in_hbm,
        "inner",
        1 << 16,
        in_specs=[pl.BlockSpec(memory_space=pltpu.HBM)] * 3,
        scratch_shapes=[
            pltpu.VMEM((2, cells, LANES), jnp.float32),
            pltpu.VMEM((cells, LANES), jnp.float32),
            pltpu.VMEM((1, LANES), jnp.int32),
            pltpu.VMEM(TILE, jnp.float32),
            pltpu.SemaphoreType.DMA((3,)),
        ],
    )
    from_one = lax.ppermute(one, both_axes, ops[0])
    (sign,) = call(signs, [tiles()], (solid_mask,), "signs", 1 << 8)
    kept, turned, two = call(
        ends,
        [tiles(3, STEPS), tiles(PACK), tiles(PACK)],
        (field, saturation, sign, kept, turned, two),
        "ends",
        1 << 16,
        input_output_aliases={3: 0, 4: 1, 5: 2},
    )
    from_two = lax.ppermute(two, both_axes, ops[1])
    (three,) = call(third, [tiles(PACK)], (kept, turned, from_one), "third", 1 << 12)
    from_three = lax.ppermute(three, both_axes, ops[2])
    k_all, rhs, ab, dinv, ring, final, answer, share = call(
        local,
        [
            tiles(STEPS, 3),
            tiles(2, STEPS),
            tiles(STEPS - 1, 8),
            tiles(STEPS, 3),
            tiles(3, 8),
            tiles(3),
            jax.ShapeDtypeStruct((4, cells, LANES), jnp.float32),
            jax.ShapeDtypeStruct((8, LANES), jnp.float32),
        ],
        (kept, turned),
        "local",
        1 << 23,
    )
    local_x, message = call(
        finish,
        [jax.ShapeDtypeStruct((2, cells, LANES), jnp.float32), jax.ShapeDtypeStruct((8, LANES), jnp.float32)],
        (k_all, rhs, kept, ab, dinv, ring, final, share, from_one, from_two, from_three),
        "finish",
        1 << 21,
    )
    both = lax.all_gather(message, "line", axis=0)
    return call(
        join,
        jax.ShapeDtypeStruct((2, cells, LANES), jnp.float32),
        (local_x, answer, both),
        "join",
        1 << 18,
        out_specs=pl.BlockSpec(memory_space=pltpu.HBM),
        scratch_shapes=[pltpu.VMEM((2, cells, LANES), jnp.float32), pltpu.SemaphoreType.DMA((2,))],
    )


def solution(mesh):
    in_specs = (P(None, "line", "tile"), P("line", "tile"), P("line", "tile"))
    out_specs = P(None, "line", "tile")
    return jax.shard_map(body, mesh=mesh, in_specs=in_specs, out_specs=out_specs, check_vma=False)
```

```python
import jax
import jax.numpy as jnp
from jax import lax
from jax.experimental import pallas as pl
from jax.experimental.pallas import tpu as pltpu
from jax.sharding import PartitionSpec as P

XS = 64
ZSTIFF = 2048
HALF = 0.5 * ZSTIFF
STEPS = 16
CHUNKS = 8
LANES = 128
TILE = (CHUNKS, LANES)
ROW = 4
SCALE = 0.4**0.5
CROSS = 0.1**0.5
GROW = HALF ** (1.0 / 3.0)
PACK = STEPS + STEPS // 2
LIMIT = 12 * 1024 * 1024


def mul(a, b):
    return (
        a[0] * b[0] + a[1] * b[2],
        a[0] * b[1] + a[1] * b[3],
        a[2] * b[0] + a[3] * b[2],
        a[2] * b[1] + a[3] * b[3],
    )


def wide(s):
    return (s[0], s[1], s[1], s[2])


def turn(a):
    return (a[0], a[2], a[1], a[3])


def apply(a, v):
    return (a[0] * v[0] + a[1] * v[1], a[2] * v[0] + a[3] * v[1])


def add(*items):
    total = items[0]
    for item in items[1:]:
        total = tuple(x + y for x, y in zip(total, item))
    return total


def symmetric(a, *more):
    return add(*((m[0], m[1], m[3]) for m in (a, *more)))


def inverse(s):
    scale = 1.0 / (s[0] * s[2] - s[1] * s[1])
    return (s[2] * scale, -s[1] * scale, s[0] * scale)


def conduct(signed, inside=None):
    dry = jnp.maximum(signed, 0.0)
    moist = HALF * 0.004 + dry * dry * dry
    pore = signed > 0.0
    heat = jnp.where(pore, HALF + (2.0 * HALF / GROW) * signed, 3.0 * HALF)
    cross = jnp.where(pore, CROSS * moist, 0.0)
    if inside is None:
        return (heat, cross, moist)
    return (jnp.where(inside, heat, 0.0), cross, jnp.where(inside, moist, 0.0))


def flux(k, drop):
    return (k[0] * drop[0] + k[1] * drop[1], k[1] * drop[0] + k[2] * drop[1])


def roll(x, shift, axis):
    return pltpu.roll(x, shift % x.shape[axis], axis)


def down(items, shift):
    return tuple(roll(x, shift, 0) for x in items)


def lanes():
    return lax.broadcasted_iota(jnp.int32, TILE, 1)


def chunks():
    return lax.broadcasted_iota(jnp.int32, TILE, 0)


def toward_odd():
    parity = lax.rem(lax.axis_index("tile"), 2)
    return (lanes() >= XS) == (parity == 1)


def load(ref, *index):
    return tuple(ref[(*index, j)] for j in range(ref.shape[len(index)]))


def store(ref, index, items):
    for j, item in enumerate(items):
        ref[(*index, j)] = item


def levels():
    stride = 1
    while stride < STEPS:
        yield stride, range(0, STEPS, 2 * stride), range(stride, STEPS, 2 * stride)
        stride *= 2


def rows_of():
    place, at = {}, 0
    for stride, kept, _ in levels():
        for step in kept:
            place[stride, step] = at
            at += 1
    return place


PLACE = rows_of()


def pack_even(kept, turned, even):
    near = toward_odd()
    half = STEPS // 2
    for j in range(3):
        for i in range(half):
            even[j * half + i] = jnp.where(near, turned[j * half + i], kept[j, i])


def signs(mask, sign):
    sign[...] = jnp.where(jnp.broadcast_to(mask[...], TILE) > 0, -GROW, GROW)


def prepare(field, sat, sign, kept, turned, odd):
    near = toward_odd()
    half = STEPS // 2
    rows = [pl.ds(i, CHUNKS, stride=STEPS) for i in range(STEPS)]
    sign = sign[...]
    for i in (*range(half, STEPS), *range(half)):
        for j, x in enumerate((field[0, rows[i], :], field[1, rows[i], :] * (1.0 / SCALE), sat[rows[i], :] * sign)):
            kept[j, i] = x
            if i >= half:
                turned[(j - 1) * half + i] = roll(x, XS, 1)
            else:
                odd[j * half + i] = jnp.where(near, x, turned[j * half + i])


def tile():
    return lax.axis_index("tile")


def line():
    return lax.axis_index("line")


def at_row_end():
    place = lax.rem(lax.axis_index("tile"), ROW)
    return jnp.logical_or(place == 0, place == ROW - 1)


def inner(field_hbm, sat_hbm, mask_hbm, kept, turned, odd, even, fbuf, sbuf, mbuf, gbuf, sems):
    @pl.when(jnp.logical_not(at_row_end()))
    def _():
        copies = [
            pltpu.make_async_copy(field_hbm, fbuf, sems.at[0]),
            pltpu.make_async_copy(sat_hbm, sbuf, sems.at[1]),
            pltpu.make_async_copy(mask_hbm, mbuf, sems.at[2]),
        ]
        for copy in copies:
            copy.start()
        for copy in copies:
            copy.wait()
        signs(mbuf, gbuf)
        prepare(fbuf, sbuf, gbuf, kept, turned, odd)
        pack_even(kept, turned, even)

    @pl.when(jnp.logical_or(tile() == 2, jnp.logical_and(tile() == 1, line() == 1)))
    def _():
        for i in range(PACK):
            odd[i], even[i] = even[i], odd[i]


def ends(field, sat, sign, kept_in, turned_in, odd_in, kept, turned, odd):
    @pl.when(at_row_end())
    def _():
        prepare(field, sat, sign, kept, turned, odd)

    @pl.when(tile() == 0)
    def _():
        pack_even(kept, turned, odd)


def third(kept, turned, arrived, out):
    relay = jnp.logical_and(tile() == 0, line() == 1)

    @pl.when(jnp.logical_not(relay))
    def _():
        pack_even(kept, turned, out)

    @pl.when(relay)
    def _():
        for i in range(PACK):
            out[i] = arrived[i]


def local(kept, turned, one, k_all, rhs, ab, dinv, ring, final, answer, share, own):
    first, last = chunks() == 0, chunks() == CHUNKS - 1
    low_line, high_line = line() == 0, line() == 1
    column = lax.rem(lanes(), XS)
    west_end, east_end = column == 0, column == XS - 1
    half = STEPS // 2

    near = toward_odd()
    k = []
    for i in range(STEPS):
        s = kept[2, i]
        ki = conduct(s)
        k.append(ki)
        store(k_all, (i,), ki)
        f = (kept[0, i], kept[1, i])
        if i < half:
            far, far_s = (roll(f[0], XS, 1), roll(f[1], XS, 1)), roll(s, XS, 1)
        else:
            far, far_s = (turned[i - half], turned[i]), turned[i + half]
        far_k = conduct(far_s)
        if i < half:
            store(own, (i,), (*far_k, *far))
        else:
            held = load(own, i - half)
            store(own, (i - half,), tuple(jnp.where(near, x, y) for x, y in zip((*ki, *f), held)))
        total = flux(add(ki, far_k), (far[0] - f[0], far[1] - f[1]))
        west_k = conduct(roll(s, 1, 1))
        west = flux(add(ki, west_k), (roll(f[0], 1, 1) - f[0], roll(f[1], 1, 1) - f[1]))
        edge = flux(ki, f)
        west = tuple(jnp.where(west_end, -e, w) for e, w in zip(edge, west))
        east = tuple(jnp.where(east_end, e, roll(w, -1, 1)) for e, w in zip(edge, west))
        for j in range(2):
            rhs[j, i] = f[j] + (total[j] + (west[j] - east[j]))

    @pl.when(from_first())
    def _():
        for i in range(STEPS):
            pack = [one[j * half + i % half] for j in range(3)]
            far = pack if i >= half else [roll(x, XS, 1) for x in pack]
            total = flux(add(load(k_all, i), conduct(far[2])), (far[0] - kept[0, i], far[1] - kept[1, i]))
            for j in range(2):
                rhs[j, i] = rhs[j, i] + jnp.where(near, 0.0, total[j])

    upper = {i: wide(add(k[i], k[i + 1])) for i in range(STEPS - 1)}
    upper[STEPS - 1] = wide(tuple(jnp.where(last, 0.0, x) for x in add(k[-1], down(k[0], -1))))
    bottom = jnp.logical_and(first, low_line)
    top = jnp.logical_and(last, high_line)
    bottom = tuple(jnp.where(bottom, x, 0.0) for x in k[0])
    top = tuple(jnp.where(top, x, 0.0) for x in k[-1])
    excess = {}

    for stride, keep, drop in levels():
        lower = {}
        for i in (*keep, *drop):
            left = i - stride
            lower[i] = turn(upper[left] if left >= 0 else down(upper[left + STEPS], 1))
        inv = {}
        for i in drop:
            if stride == 1:
                d = symmetric(lower[i], upper[i])
                d = (d[0] + 1.0, d[1], d[2] + 1.0)
                if i == STEPS - 1:
                    d = add(d, top)
            else:
                d = symmetric(excess[i], lower[i], upper[i])
            inv[i] = inverse(d)
            store(dinv, (i,), inv[i])
        for i in keep:
            right, left = i + stride, i - stride
            if left < 0:
                before = wide(down(inv[left + STEPS], 1))
            else:
                before = wide(inv[left])
            a = mul(lower[i], before)
            b = mul(upper[i], wide(inv[right]))
            store(ab, (PLACE[stride, i],), (*a, *b))
            if stride == 1:
                more = add(a, b)
                more = (more[0] + 1.0, more[1], more[2], more[3] + 1.0)
                if i == 0:
                    more = add(more, wide(bottom))
                if right == STEPS - 1:
                    more = add(more, mul(b, wide(top)))
            else:
                prev = excess[left] if left >= 0 else down(excess[left + STEPS], 1)
                more = add(excess[i], mul(a, prev), mul(b, excess[right]))
            excess[i] = more
            upper[i] = mul(b, upper[right])

    start = jnp.where(jnp.logical_and(high_line, first), 1.0, 0.0)
    end = jnp.logical_and(low_line, last)
    one = jnp.where(end, 1.0, 0.0)
    none = jnp.zeros(TILE, jnp.float32)
    source = (one, none, none, one)
    sides = {STEPS - 1: source}
    for stride, keep, _ in levels():
        b = load(ab, PLACE[stride, keep[-1]])[4:8]
        source = tuple(jnp.where(end, x, 0.0) for x in b) if stride == 1 else mul(b, source)
        sides[keep[-1]] = source
    vec = (source[0] + start, source[1], source[2], source[3] + start)

    up, ex = upper[0], excess[0]
    low = turn(down(up, 1))
    shift, place = 1, 0
    while shift < CHUNKS:
        inv = inverse(symmetric(ex, low, up))
        a = mul(low, wide(down(inv, shift)))
        b = mul(up, wide(down(inv, -shift)))
        store(ring, (place,), (*a, *b))
        vec = add(vec, mul(a, down(vec, shift)), mul(b, down(vec, -shift)))
        ex = add(ex, mul(a, down(ex, shift)), mul(b, down(ex, -shift)))
        up = mul(b, down(up, -shift))
        shift *= 2
        place += 1
        low = turn(down(up, shift))
    inv = inverse((ex[0], ex[1], ex[3]))
    store(final, (), inv)
    w = {0: mul(wide(inv), vec)}
    for stride, keep, drop in reversed(list(levels())):
        for i in drop:
            left, right = i - stride, i + stride
            prev = turn(load(ab, PLACE[stride, left])[4:8])
            if right < STEPS:
                after, later = turn(load(ab, PLACE[stride, right])[0:4]), w[right]
            else:
                after, later = turn(down(load(ab, PLACE[stride, 0])[0:4], -1)), down(w[0], -1)
            w[i] = add(mul(prev, w[left]), mul(after, later))
            if i in sides:
                w[i] = add(w[i], mul(wide(load(dinv, i)), sides[i]))
    for i in range(STEPS):
        for j, x in enumerate((w[i][0], w[i][1], SCALE * w[i][2], SCALE * w[i][3])):
            answer[j, pl.ds(i, CHUNKS, stride=STEPS), :] = x

    tail = down((w[STEPS - 1][0], w[STEPS - 1][1], w[STEPS - 1][3], kept[2, STEPS - 1]), 1)
    head = (w[0][0], w[0][1], w[0][3], kept[2, 0])
    for j, (x, y) in enumerate(zip(head, tail)):
        share[pl.ds(2 + j, 1), :] = jnp.where(low_line, y, x)[0:1]
    share[pl.ds(0, 2), :] = none[0:2]
    share[pl.ds(6, 2), :] = none[0:2]


def from_first():
    return jnp.logical_and(tile() >= ROW, lax.rem(tile(), ROW) == 0)


def finish(k_all, rhs, kept, own, ab, dinv, ring, final, share, one, two, three, local_x, message):
    half = STEPS // 2
    at, high = tile(), line() == 1
    near = toward_odd()
    rest = (ab, dinv, ring, final, share, local_x, message)

    @pl.when(from_first())
    def _():
        b = {i: (rhs[0, i], rhs[1, i]) for i in range(STEPS)}
        for i in range(half):
            mine = load(own, i)
            total = flux(add(mine[:3], conduct(two[2 * half + i])), (two[i] - mine[3], two[half + i] - mine[4]))
            b[i + half] = add(b[i + half], tuple(jnp.where(near, x, 0.0) for x in total))
            b[i] = add(b[i], tuple(jnp.where(near, roll(x, XS, 1), 0.0) for x in total))
        solve(b, *rest)

    def both(halo):
        alone = jnp.logical_or(at == 0, at == lax.axis_size("tile") - 1)
        inside = jnp.logical_not(jnp.logical_and(near, alone))
        far = {}
        for j in range(3):
            for i in range(half):
                o, e = halo(j * half + i)
                far[j, i] = roll(jnp.where(near, e, o), XS, 1)
                far[j, i + half] = jnp.where(near, o, e)
        b = {}
        for i in range(STEPS):
            drop = (far[0, i] - kept[0, i], far[1, i] - kept[1, i])
            total = flux(add(load(k_all, i), conduct(far[2, i], inside)), drop)
            b[i] = (rhs[0, i] + total[0], rhs[1, i] + total[1])
        solve(b, *rest)

    @pl.when(jnp.logical_and(at >= ROW, jnp.logical_not(from_first())))
    def _():
        both(lambda i: (two[i], three[i]))

    @pl.when(at < ROW)
    def _():
        def halo(i):
            odd = jnp.where(at == 1, one[i], two[i])
            odd = jnp.where(jnp.logical_and(high, at == 2), one[i], odd)
            odd = jnp.where(jnp.logical_and(high, at == 0), three[i], odd)
            even = jnp.where(jnp.logical_or(at == 1, jnp.logical_and(high, at == 0)), two[i], three[i])
            return odd, even

        both(halo)


def solve(b, ab, dinv, ring, final, share, local_x, message):
    for stride, keep, drop in levels():
        for i in keep:
            left = i - stride
            prev = b[left] if left >= 0 else down(b[left + STEPS], 1)
            c = load(ab, PLACE[stride, i])
            b[i] = add(b[i], apply(c[0:4], prev), apply(c[4:8], b[i + stride]))
    vec = b[0]
    shift, place = 1, 0
    while shift < CHUNKS:
        c = load(ring, place)
        vec = add(vec, apply(c[0:4], down(vec, shift)), apply(c[4:8], down(vec, -shift)))
        shift *= 2
        place += 1
    x = {0: apply(wide(load(final)), vec)}
    for stride, keep, drop in reversed(list(levels())):
        for i in drop:
            left, right = i - stride, i + stride
            prev = turn(load(ab, PLACE[stride, left])[4:8])
            if right < STEPS:
                after, later = turn(load(ab, PLACE[stride, right])[0:4]), x[right]
            else:
                after, later = turn(down(load(ab, PLACE[stride, 0])[0:4], -1)), down(x[0], -1)
            x[i] = add(apply(wide(load(dinv, i)), b[i]), apply(prev, x[left]), apply(after, later))
    message[...] = share[...]
    tail = down(x[STEPS - 1], 1)
    for j in range(2):
        message[pl.ds(j, 1), :] = jnp.where(line() == 0, tail[j], x[0][j])[0:1]
    for i in range(STEPS):
        here = pl.ds(i, CHUNKS, stride=STEPS)
        local_x[0, here, :] = x[i][0]
        local_x[1, here, :] = SCALE * x[i][1]


def join(local_x, answer, both, out_hbm, out, sems):
    def row(who, j):
        return jnp.broadcast_to(both[who, pl.ds(j, 1), :], TILE)

    sign = jnp.where(line() == 0, 1.0, -1.0)
    drop = tuple(sign * (row(1, j) - row(0, j)) for j in range(2))
    reach = wide(tuple(row(0, 2 + j) + row(1, 2 + j) for j in range(3)))
    face = add(conduct(row(0, 5)), conduct(row(1, 5)))
    m = mul(wide(face), reach)
    m = (m[0] + 1.0, m[1], m[2], m[3] + 1.0)
    push = flux(face, drop)
    scale = 1.0 / (m[0] * m[3] - m[1] * m[2])
    through = ((m[3] * push[0] - m[1] * push[1]) * scale, (m[0] * push[1] - m[2] * push[0]) * scale)

    copies = [pltpu.make_async_copy(out.at[j], out_hbm.at[j], sems.at[j]) for j in range(2)]
    for j in range(2):
        for i in range(STEPS):
            here = pl.ds(i * CHUNKS, CHUNKS)
            change = answer[2 * j, here, :] * through[0] + answer[2 * j + 1, here, :] * through[1]
            out[j, here, :] = local_x[j, here, :] + change
        copies[j].start()
    for copy in copies:
        copy.wait()


def tiles(*lead):
    return jax.ShapeDtypeStruct((*lead, *TILE), jnp.float32)


def call(kernel, outs, args, name, flops, **more):
    vmem = pl.BlockSpec(memory_space=pltpu.VMEM)
    more.setdefault("in_specs", [vmem] * len(args))
    if "out_specs" not in more:
        more["out_specs"] = [vmem] * len(outs)
    return pl.pallas_call(
        kernel,
        out_shape=outs,
        compiler_params=pltpu.CompilerParams(vmem_limit_bytes=LIMIT),
        cost_estimate=pl.CostEstimate(flops=flops, bytes_accessed=1 << 20, transcendentals=0),
        name=name,
        **more,
    )(*args)


def moves(count):
    ops = [[], [], []]
    for base in (0, count):
        for t in range(base, base + count, ROW):
            ops[2] += [(t + 2, t + 3), (t + 3, t + 2)]
            if t > base:
                ops[0].append((t + 1, t))
                ops[1] += [(t - 1, t), (t, t - 1), (t + 1, t + 2), (t + 2, t + 1)]
                ops[2].append((t, t + 1))
    ops[0] += [(1, count), (2, 1), (count + 1, count + 2), (count + 2, count + 1)]
    ops[1] += [(0, 1), (1, 2), (count, count + 1), (count + 1, count)]
    ops[2].append((count, 0))
    return ops


def body(field, saturation, solid_mask):
    ops = moves(lax.axis_size("tile"))
    both_axes = ("line", "tile")
    cells = STEPS * CHUNKS
    in_hbm = [pltpu.with_memory_space_constraint(x, pltpu.HBM) for x in (field, saturation, solid_mask)]
    kept, turned, two, one = call(
        inner,
        [tiles(3, STEPS), tiles(PACK), tiles(PACK), tiles(PACK)],
        in_hbm,
        "inner",
        1 << 16,
        in_specs=[pl.BlockSpec(memory_space=pltpu.HBM)] * 3,
        scratch_shapes=[
            pltpu.VMEM((2, cells, LANES), jnp.float32),
            pltpu.VMEM((cells, LANES), jnp.float32),
            pltpu.VMEM((1, LANES), jnp.int32),
            pltpu.VMEM(TILE, jnp.float32),
            pltpu.SemaphoreType.DMA((3,)),
        ],
    )
    from_one = lax.ppermute(one, both_axes, ops[0])
    (sign,) = call(signs, [tiles()], (solid_mask,), "signs", 1 << 8)
    kept, turned, two = call(
        ends,
        [tiles(3, STEPS), tiles(PACK), tiles(PACK)],
        (field, saturation, sign, kept, turned, two),
        "ends",
        1 << 16,
        input_output_aliases={3: 0, 4: 1, 5: 2},
    )
    from_two = lax.ppermute(two, both_axes, ops[1])
    (three,) = call(third, [tiles(PACK)], (kept, turned, from_one), "third", 1 << 12)
    from_three = lax.ppermute(three, both_axes, ops[2])
    k_all, rhs, ab, dinv, ring, final, answer, share, own = call(
        local,
        [
            tiles(STEPS, 3),
            tiles(2, STEPS),
            tiles(STEPS - 1, 8),
            tiles(STEPS, 3),
            tiles(3, 8),
            tiles(3),
            jax.ShapeDtypeStruct((4, cells, LANES), jnp.float32),
            jax.ShapeDtypeStruct((8, LANES), jnp.float32),
            tiles(STEPS // 2, 5),
        ],
        (kept, turned, from_one),
        "local",
        1 << 23,
    )
    local_x, message = call(
        finish,
        [jax.ShapeDtypeStruct((2, cells, LANES), jnp.float32), jax.ShapeDtypeStruct((8, LANES), jnp.float32)],
        (k_all, rhs, kept, own, ab, dinv, ring, final, share, from_one, from_two, from_three),
        "finish",
        1 << 21,
    )
    both = lax.all_gather(message, "line", axis=0)
    return call(
        join,
        jax.ShapeDtypeStruct((2, cells, LANES), jnp.float32),
        (local_x, answer, both),
        "join",
        1 << 18,
        out_specs=pl.BlockSpec(memory_space=pltpu.HBM),
        scratch_shapes=[pltpu.VMEM((2, cells, LANES), jnp.float32), pltpu.SemaphoreType.DMA((2,))],
    )


def solution(mesh):
    in_specs = (P(None, "line", "tile"), P("line", "tile"), P("line", "tile"))
    out_specs = P(None, "line", "tile")
    return jax.shard_map(body, mesh=mesh, in_specs=in_specs, out_specs=out_specs, check_vma=False)
```

```python
import jax
import jax.numpy as jnp
from jax import lax
from jax.experimental import pallas as pl
from jax.experimental.pallas import tpu as pltpu
from jax.sharding import PartitionSpec as P

XS = 64
ZSTIFF = 2048
HALF = 0.5 * ZSTIFF
STEPS = 16
CHUNKS = 8
LANES = 128
TILE = (CHUNKS, LANES)
ROW = 4
SCALE = 0.4**0.5
CROSS = 0.1**0.5
GROW = HALF ** (1.0 / 3.0)
PACK = STEPS + STEPS // 2
LIMIT = 12 * 1024 * 1024


def mul(a, b):
    return (
        a[0] * b[0] + a[1] * b[2],
        a[0] * b[1] + a[1] * b[3],
        a[2] * b[0] + a[3] * b[2],
        a[2] * b[1] + a[3] * b[3],
    )


def wide(s):
    return (s[0], s[1], s[1], s[2])


def turn(a):
    return (a[0], a[2], a[1], a[3])


def apply(a, v):
    return (a[0] * v[0] + a[1] * v[1], a[2] * v[0] + a[3] * v[1])


def add(*items):
    total = items[0]
    for item in items[1:]:
        total = tuple(x + y for x, y in zip(total, item))
    return total


def symmetric(a, *more):
    return add(*((m[0], m[1], m[3]) for m in (a, *more)))


def inverse(s):
    scale = 1.0 / (s[0] * s[2] - s[1] * s[1])
    return (s[2] * scale, -s[1] * scale, s[0] * scale)


def conduct(signed, inside=None):
    dry = jnp.maximum(signed, 0.0)
    moist = HALF * 0.004 + dry * dry * dry
    pore = signed > 0.0
    heat = jnp.where(pore, HALF + (2.0 * HALF / GROW) * signed, 3.0 * HALF)
    cross = jnp.where(pore, CROSS * moist, 0.0)
    if inside is None:
        return (heat, cross, moist)
    return (jnp.where(inside, heat, 0.0), cross, jnp.where(inside, moist, 0.0))


def flux(k, drop):
    return (k[0] * drop[0] + k[1] * drop[1], k[1] * drop[0] + k[2] * drop[1])


def roll(x, shift, axis):
    return pltpu.roll(x, shift % x.shape[axis], axis)


def down(items, shift):
    return tuple(roll(x, shift, 0) for x in items)


def lanes():
    return lax.broadcasted_iota(jnp.int32, TILE, 1)


def chunks():
    return lax.broadcasted_iota(jnp.int32, TILE, 0)


def toward_odd():
    parity = lax.rem(lax.axis_index("tile"), 2)
    return (lanes() >= XS) == (parity == 1)


def load(ref, *index):
    return tuple(ref[(*index, j)] for j in range(ref.shape[len(index)]))


def store(ref, index, items):
    for j, item in enumerate(items):
        ref[(*index, j)] = item


def levels():
    stride = 1
    while stride < STEPS:
        yield stride, range(0, STEPS, 2 * stride), range(stride, STEPS, 2 * stride)
        stride *= 2


def rows_of():
    place, at = {}, 0
    for stride, kept, _ in levels():
        for step in kept:
            place[stride, step] = at
            at += 1
    return place


PLACE = rows_of()


def pack_even(kept, turned, even):
    near = toward_odd()
    half = STEPS // 2
    for j in range(3):
        for i in range(half):
            even[j * half + i] = jnp.where(near, turned[j * half + i], kept[j, i])


def signs(mask, sign):
    sign[...] = jnp.where(jnp.broadcast_to(mask[...], TILE) > 0, -GROW, GROW)


def prepare(field, sat, sign, kept, turned, odd):
    near = toward_odd()
    half = STEPS // 2
    rows = [pl.ds(i, CHUNKS, stride=STEPS) for i in range(STEPS)]
    sign = sign[...]
    low, high = [None] * PACK, [None] * PACK
    for i in (*range(half, STEPS), *range(half)):
        for j, x in reversed(list(enumerate((field[0, rows[i], :], field[1, rows[i], :] * (1.0 / SCALE), sat[rows[i], :] * sign)))):
            if i >= half:
                high[(j - 1) * half + i] = roll(x, XS, 1)
            else:
                low[j * half + i] = x
            kept[j, i] = x
    for i in range(PACK):
        odd[i] = jnp.where(near, low[i], high[i])
    for i in range(PACK):
        turned[i] = high[i]


def tile():
    return lax.axis_index("tile")


def line():
    return lax.axis_index("line")


def at_row_end():
    place = lax.rem(lax.axis_index("tile"), ROW)
    return jnp.logical_or(place == 0, place == ROW - 1)


def inner(field_hbm, sat_hbm, mask_hbm, kept, turned, odd, even, fbuf, sbuf, mbuf, gbuf, sems):
    @pl.when(jnp.logical_not(at_row_end()))
    def _():
        copies = [
            pltpu.make_async_copy(field_hbm, fbuf, sems.at[0]),
            pltpu.make_async_copy(sat_hbm, sbuf, sems.at[1]),
            pltpu.make_async_copy(mask_hbm, mbuf, sems.at[2]),
        ]
        for copy in copies:
            copy.start()
        for copy in copies:
            copy.wait()
        signs(mbuf, gbuf)
        prepare(fbuf, sbuf, gbuf, kept, turned, odd)
        pack_even(kept, turned, even)

    @pl.when(jnp.logical_or(tile() == 2, jnp.logical_and(tile() == 1, line() == 1)))
    def _():
        for i in range(PACK):
            odd[i], even[i] = even[i], odd[i]


def ends(field, sat, sign, kept_in, turned_in, odd_in, kept, turned, odd):
    @pl.when(at_row_end())
    def _():
        prepare(field, sat, sign, kept, turned, odd)

    @pl.when(tile() == 0)
    def _():
        pack_even(kept, turned, odd)


def third(kept, turned, arrived, out):
    relay = jnp.logical_and(tile() == 0, line() == 1)

    @pl.when(jnp.logical_not(relay))
    def _():
        pack_even(kept, turned, out)

    @pl.when(relay)
    def _():
        for i in range(PACK):
            out[i] = arrived[i]


def local(kept, turned, one, k_all, rhs, ab, dinv, ring, final, answer, share, own):
    first, last = chunks() == 0, chunks() == CHUNKS - 1
    low_line, high_line = line() == 0, line() == 1
    column = lax.rem(lanes(), XS)
    west_end, east_end = column == 0, column == XS - 1
    half = STEPS // 2

    near = toward_odd()
    k = []
    for i in range(STEPS):
        s = kept[2, i]
        ki = conduct(s)
        k.append(ki)
        store(k_all, (i,), ki)
        f = (kept[0, i], kept[1, i])
        if i < half:
            far, far_s = (roll(f[0], XS, 1), roll(f[1], XS, 1)), roll(s, XS, 1)
        else:
            far, far_s = (turned[i - half], turned[i]), turned[i + half]
        far_k = conduct(far_s)
        if i < half:
            store(own, (i,), (*far_k, *far))
        else:
            held = load(own, i - half)
            store(own, (i - half,), tuple(jnp.where(near, x, y) for x, y in zip((*ki, *f), held)))
        total = flux(add(ki, far_k), (far[0] - f[0], far[1] - f[1]))
        west_k = conduct(roll(s, 1, 1))
        west = flux(add(ki, west_k), (roll(f[0], 1, 1) - f[0], roll(f[1], 1, 1) - f[1]))
        edge = flux(ki, f)
        west = tuple(jnp.where(west_end, -e, w) for e, w in zip(edge, west))
        east = tuple(jnp.where(east_end, e, roll(w, -1, 1)) for e, w in zip(edge, west))
        for j in range(2):
            rhs[j, i] = f[j] + (total[j] + (west[j] - east[j]))

    @pl.when(from_first())
    def _():
        for i in range(STEPS):
            pack = [one[j * half + i % half] for j in range(3)]
            far = pack if i >= half else [roll(x, XS, 1) for x in pack]
            total = flux(add(load(k_all, i), conduct(far[2])), (far[0] - kept[0, i], far[1] - kept[1, i]))
            for j in range(2):
                rhs[j, i] = rhs[j, i] + jnp.where(near, 0.0, total[j])

    upper = {i: wide(add(k[i], k[i + 1])) for i in range(STEPS - 1)}
    upper[STEPS - 1] = wide(tuple(jnp.where(last, 0.0, x) for x in add(k[-1], down(k[0], -1))))
    bottom = jnp.logical_and(first, low_line)
    top = jnp.logical_and(last, high_line)
    bottom = tuple(jnp.where(bottom, x, 0.0) for x in k[0])
    top = tuple(jnp.where(top, x, 0.0) for x in k[-1])
    excess = {}

    for stride, keep, drop in levels():
        lower = {}
        for i in (*keep, *drop):
            left = i - stride
            lower[i] = turn(upper[left] if left >= 0 else down(upper[left + STEPS], 1))
        inv = {}
        for i in drop:
            if stride == 1:
                d = symmetric(lower[i], upper[i])
                d = (d[0] + 1.0, d[1], d[2] + 1.0)
                if i == STEPS - 1:
                    d = add(d, top)
            else:
                d = symmetric(excess[i], lower[i], upper[i])
            inv[i] = inverse(d)
            store(dinv, (i,), inv[i])
        for i in keep:
            right, left = i + stride, i - stride
            if left < 0:
                before = wide(down(inv[left + STEPS], 1))
            else:
                before = wide(inv[left])
            a = mul(lower[i], before)
            b = mul(upper[i], wide(inv[right]))
            store(ab, (PLACE[stride, i],), (*a, *b))
            if stride == 1:
                more = add(a, b)
                more = (more[0] + 1.0, more[1], more[2], more[3] + 1.0)
                if i == 0:
                    more = add(more, wide(bottom))
                if right == STEPS - 1:
                    more = add(more, mul(b, wide(top)))
            else:
                prev = excess[left] if left >= 0 else down(excess[left + STEPS], 1)
                more = add(excess[i], mul(a, prev), mul(b, excess[right]))
            excess[i] = more
            upper[i] = mul(b, upper[right])

    start = jnp.where(jnp.logical_and(high_line, first), 1.0, 0.0)
    end = jnp.logical_and(low_line, last)
    one = jnp.where(end, 1.0, 0.0)
    none = jnp.zeros(TILE, jnp.float32)
    source = (one, none, none, one)
    sides = {STEPS - 1: source}
    for stride, keep, _ in levels():
        b = load(ab, PLACE[stride, keep[-1]])[4:8]
        source = tuple(jnp.where(end, x, 0.0) for x in b) if stride == 1 else mul(b, source)
        sides[keep[-1]] = source
    vec = (source[0] + start, source[1], source[2], source[3] + start)

    up, ex = upper[0], excess[0]
    low = turn(down(up, 1))
    shift, place = 1, 0
    while shift < CHUNKS:
        inv = inverse(symmetric(ex, low, up))
        a = mul(low, wide(down(inv, shift)))
        b = mul(up, wide(down(inv, -shift)))
        store(ring, (place,), (*a, *b))
        vec = add(vec, mul(a, down(vec, shift)), mul(b, down(vec, -shift)))
        ex = add(ex, mul(a, down(ex, shift)), mul(b, down(ex, -shift)))
        up = mul(b, down(up, -shift))
        shift *= 2
        place += 1
        low = turn(down(up, shift))
    inv = inverse((ex[0], ex[1], ex[3]))
    store(final, (), inv)
    w = {0: mul(wide(inv), vec)}
    for stride, keep, drop in reversed(list(levels())):
        for i in drop:
            left, right = i - stride, i + stride
            prev = turn(load(ab, PLACE[stride, left])[4:8])
            if right < STEPS:
                after, later = turn(load(ab, PLACE[stride, right])[0:4]), w[right]
            else:
                after, later = turn(down(load(ab, PLACE[stride, 0])[0:4], -1)), down(w[0], -1)
            w[i] = add(mul(prev, w[left]), mul(after, later))
            if i in sides:
                w[i] = add(w[i], mul(wide(load(dinv, i)), sides[i]))
    for i in range(STEPS):
        for j, x in enumerate((w[i][0], w[i][1], SCALE * w[i][2], SCALE * w[i][3])):
            answer[j, pl.ds(i, CHUNKS, stride=STEPS), :] = x

    tail = down((w[STEPS - 1][0], w[STEPS - 1][1], w[STEPS - 1][3], kept[2, STEPS - 1]), 1)
    head = (w[0][0], w[0][1], w[0][3], kept[2, 0])
    for j, (x, y) in enumerate(zip(head, tail)):
        share[pl.ds(2 + j, 1), :] = jnp.where(low_line, y, x)[0:1]
    share[pl.ds(0, 2), :] = none[0:2]
    share[pl.ds(6, 2), :] = none[0:2]


def from_first():
    return jnp.logical_and(tile() >= ROW, lax.rem(tile(), ROW) == 0)


def finish(k_all, rhs, kept, own, ab, dinv, ring, final, share, one, two, three, local_x, message):
    half = STEPS // 2
    at, high = tile(), line() == 1
    near = toward_odd()
    rest = (ab, dinv, ring, final, share, local_x, message)

    @pl.when(from_first())
    def _():
        b = {i: (rhs[0, i], rhs[1, i]) for i in range(STEPS)}
        for i in range(half):
            mine = load(own, i)
            total = flux(add(mine[:3], conduct(two[2 * half + i])), (two[i] - mine[3], two[half + i] - mine[4]))
            b[i + half] = add(b[i + half], tuple(jnp.where(near, x, 0.0) for x in total))
            b[i] = add(b[i], tuple(jnp.where(near, roll(x, XS, 1), 0.0) for x in total))
        solve(b, *rest)

    def both(halo):
        alone = jnp.logical_or(at == 0, at == lax.axis_size("tile") - 1)
        inside = jnp.logical_not(jnp.logical_and(near, alone))
        far = {}
        for j in range(3):
            for i in range(half):
                o, e = halo(j * half + i)
                far[j, i] = roll(jnp.where(near, e, o), XS, 1)
                far[j, i + half] = jnp.where(near, o, e)
        b = {}
        for i in range(STEPS):
            drop = (far[0, i] - kept[0, i], far[1, i] - kept[1, i])
            total = flux(add(load(k_all, i), conduct(far[2, i], inside)), drop)
            b[i] = (rhs[0, i] + total[0], rhs[1, i] + total[1])
        solve(b, *rest)

    @pl.when(jnp.logical_and(at >= ROW, jnp.logical_not(from_first())))
    def _():
        both(lambda i: (two[i], three[i]))

    @pl.when(at < ROW)
    def _():
        def halo(i):
            odd = jnp.where(at == 1, one[i], two[i])
            odd = jnp.where(jnp.logical_and(high, at == 2), one[i], odd)
            odd = jnp.where(jnp.logical_and(high, at == 0), three[i], odd)
            even = jnp.where(jnp.logical_or(at == 1, jnp.logical_and(high, at == 0)), two[i], three[i])
            return odd, even

        both(halo)


def solve(b, ab, dinv, ring, final, share, local_x, message):
    for stride, keep, drop in levels():
        for i in keep:
            left = i - stride
            prev = b[left] if left >= 0 else down(b[left + STEPS], 1)
            c = load(ab, PLACE[stride, i])
            b[i] = add(b[i], apply(c[0:4], prev), apply(c[4:8], b[i + stride]))
    vec = b[0]
    shift, place = 1, 0
    while shift < CHUNKS:
        c = load(ring, place)
        vec = add(vec, apply(c[0:4], down(vec, shift)), apply(c[4:8], down(vec, -shift)))
        shift *= 2
        place += 1
    x = {0: apply(wide(load(final)), vec)}
    for stride, keep, drop in reversed(list(levels())):
        for i in drop:
            left, right = i - stride, i + stride
            prev = turn(load(ab, PLACE[stride, left])[4:8])
            if right < STEPS:
                after, later = turn(load(ab, PLACE[stride, right])[0:4]), x[right]
            else:
                after, later = turn(down(load(ab, PLACE[stride, 0])[0:4], -1)), down(x[0], -1)
            x[i] = add(apply(wide(load(dinv, i)), b[i]), apply(prev, x[left]), apply(after, later))
    message[...] = share[...]
    tail = down(x[STEPS - 1], 1)
    for j in range(2):
        message[pl.ds(j, 1), :] = jnp.where(line() == 0, tail[j], x[0][j])[0:1]
    for i in range(STEPS):
        here = pl.ds(i, CHUNKS, stride=STEPS)
        local_x[0, here, :] = x[i][0]
        local_x[1, here, :] = SCALE * x[i][1]


def join(local_x, answer, both, out_hbm, out, sems):
    def row(who, j):
        return jnp.broadcast_to(both[who, pl.ds(j, 1), :], TILE)

    sign = jnp.where(line() == 0, 1.0, -1.0)
    drop = tuple(sign * (row(1, j) - row(0, j)) for j in range(2))
    reach = wide(tuple(row(0, 2 + j) + row(1, 2 + j) for j in range(3)))
    face = add(conduct(row(0, 5)), conduct(row(1, 5)))
    m = mul(wide(face), reach)
    m = (m[0] + 1.0, m[1], m[2], m[3] + 1.0)
    push = flux(face, drop)
    scale = 1.0 / (m[0] * m[3] - m[1] * m[2])
    through = ((m[3] * push[0] - m[1] * push[1]) * scale, (m[0] * push[1] - m[2] * push[0]) * scale)

    copies = [pltpu.make_async_copy(out.at[j], out_hbm.at[j], sems.at[j]) for j in range(2)]
    for j in range(2):
        for i in range(STEPS):
            here = pl.ds(i * CHUNKS, CHUNKS)
            change = answer[2 * j, here, :] * through[0] + answer[2 * j + 1, here, :] * through[1]
            out[j, here, :] = local_x[j, here, :] + change
        copies[j].start()
    for copy in copies:
        copy.wait()


def tiles(*lead):
    return jax.ShapeDtypeStruct((*lead, *TILE), jnp.float32)


def call(kernel, outs, args, name, flops, **more):
    vmem = pl.BlockSpec(memory_space=pltpu.VMEM)
    more.setdefault("in_specs", [vmem] * len(args))
    if "out_specs" not in more:
        more["out_specs"] = [vmem] * len(outs)
    return pl.pallas_call(
        kernel,
        out_shape=outs,
        compiler_params=pltpu.CompilerParams(vmem_limit_bytes=LIMIT),
        cost_estimate=pl.CostEstimate(flops=flops, bytes_accessed=1 << 20, transcendentals=0),
        name=name,
        **more,
    )(*args)


def moves(count):
    ops = [[], [], []]
    for base in (0, count):
        for t in range(base, base + count, ROW):
            ops[2] += [(t + 2, t + 3), (t + 3, t + 2)]
            if t > base:
                ops[0].append((t + 1, t))
                ops[1] += [(t - 1, t), (t, t - 1), (t + 1, t + 2), (t + 2, t + 1)]
                ops[2].append((t, t + 1))
    ops[0] += [(1, count), (2, 1), (count + 1, count + 2), (count + 2, count + 1)]
    ops[1] += [(0, 1), (1, 2), (count, count + 1), (count + 1, count)]
    ops[2].append((count, 0))
    return ops


def body(field, saturation, solid_mask):
    ops = moves(lax.axis_size("tile"))
    both_axes = ("line", "tile")
    cells = STEPS * CHUNKS
    in_hbm = [pltpu.with_memory_space_constraint(x, pltpu.HBM) for x in (field, saturation, solid_mask)]
    kept, turned, two, one = call(
        inner,
        [tiles(3, STEPS), tiles(PACK), tiles(PACK), tiles(PACK)],
        in_hbm,
        "inner",
        1 << 16,
        in_specs=[pl.BlockSpec(memory_space=pltpu.HBM)] * 3,
        scratch_shapes=[
            pltpu.VMEM((2, cells, LANES), jnp.float32),
            pltpu.VMEM((cells, LANES), jnp.float32),
            pltpu.VMEM((1, LANES), jnp.int32),
            pltpu.VMEM(TILE, jnp.float32),
            pltpu.SemaphoreType.DMA((3,)),
        ],
    )
    from_one = lax.ppermute(one, both_axes, ops[0])
    (sign,) = call(signs, [tiles()], (solid_mask,), "signs", 1 << 8)
    kept, turned, two = call(
        ends,
        [tiles(3, STEPS), tiles(PACK), tiles(PACK)],
        (field, saturation, sign, kept, turned, two),
        "ends",
        1 << 16,
        input_output_aliases={3: 0, 4: 1, 5: 2},
    )
    from_two = lax.ppermute(two, both_axes, ops[1])
    (three,) = call(third, [tiles(PACK)], (kept, turned, from_one), "third", 1 << 12)
    from_three = lax.ppermute(three, both_axes, ops[2])
    k_all, rhs, ab, dinv, ring, final, answer, share, own = call(
        local,
        [
            tiles(STEPS, 3),
            tiles(2, STEPS),
            tiles(STEPS - 1, 8),
            tiles(STEPS, 3),
            tiles(3, 8),
            tiles(3),
            jax.ShapeDtypeStruct((4, cells, LANES), jnp.float32),
            jax.ShapeDtypeStruct((8, LANES), jnp.float32),
            tiles(STEPS // 2, 5),
        ],
        (kept, turned, from_one),
        "local",
        1 << 23,
    )
    local_x, message = call(
        finish,
        [jax.ShapeDtypeStruct((2, cells, LANES), jnp.float32), jax.ShapeDtypeStruct((8, LANES), jnp.float32)],
        (k_all, rhs, kept, own, ab, dinv, ring, final, share, from_one, from_two, from_three),
        "finish",
        1 << 21,
    )
    both = lax.all_gather(message, "line", axis=0)
    return call(
        join,
        jax.ShapeDtypeStruct((2, cells, LANES), jnp.float32),
        (local_x, answer, both),
        "join",
        1 << 18,
        out_specs=pl.BlockSpec(memory_space=pltpu.HBM),
        scratch_shapes=[pltpu.VMEM((2, cells, LANES), jnp.float32), pltpu.SemaphoreType.DMA((2,))],
    )


def solution(mesh):
    in_specs = (P(None, "line", "tile"), P("line", "tile"), P("line", "tile"))
    out_specs = P(None, "line", "tile")
    return jax.shard_map(body, mesh=mesh, in_specs=in_specs, out_specs=out_specs, check_vma=False)
```

```python
import jax
import jax.numpy as jnp
from jax import lax
from jax.experimental import pallas as pl
from jax.experimental.pallas import tpu as pltpu
from jax.sharding import PartitionSpec as P

XS = 64
ZSTIFF = 2048
HALF = 0.5 * ZSTIFF
STEPS = 16
CHUNKS = 8
LANES = 128
TILE = (CHUNKS, LANES)
ROW = 4
SCALE = 0.4**0.5
CROSS = 0.1**0.5
GROW = HALF ** (1.0 / 3.0)
PACK = STEPS + STEPS // 2
LIMIT = 12 * 1024 * 1024


def mul(a, b):
    return (
        a[0] * b[0] + a[1] * b[2],
        a[0] * b[1] + a[1] * b[3],
        a[2] * b[0] + a[3] * b[2],
        a[2] * b[1] + a[3] * b[3],
    )


def wide(s):
    return (s[0], s[1], s[1], s[2])


def turn(a):
    return (a[0], a[2], a[1], a[3])


def apply(a, v):
    return (a[0] * v[0] + a[1] * v[1], a[2] * v[0] + a[3] * v[1])


def add(*items):
    total = items[0]
    for item in items[1:]:
        total = tuple(x + y for x, y in zip(total, item))
    return total


def symmetric(a, *more):
    return add(*((m[0], m[1], m[3]) for m in (a, *more)))


def inverse(s):
    scale = 1.0 / (s[0] * s[2] - s[1] * s[1])
    return (s[2] * scale, -s[1] * scale, s[0] * scale)


def conduct(signed, inside=None):
    dry = jnp.maximum(signed, 0.0)
    moist = HALF * 0.004 + dry * dry * dry
    pore = signed > 0.0
    heat = jnp.where(pore, HALF + (2.0 * HALF / GROW) * signed, 3.0 * HALF)
    cross = jnp.where(pore, CROSS * moist, 0.0)
    if inside is None:
        return (heat, cross, moist)
    return (jnp.where(inside, heat, 0.0), cross, jnp.where(inside, moist, 0.0))


def flux(k, drop):
    return (k[0] * drop[0] + k[1] * drop[1], k[1] * drop[0] + k[2] * drop[1])


def roll(x, shift, axis):
    return pltpu.roll(x, shift % x.shape[axis], axis)


def down(items, shift):
    return tuple(roll(x, shift, 0) for x in items)


def lanes():
    return lax.broadcasted_iota(jnp.int32, TILE, 1)


def chunks():
    return lax.broadcasted_iota(jnp.int32, TILE, 0)


def toward_odd():
    parity = lax.rem(lax.axis_index("tile"), 2)
    return (lanes() >= XS) == (parity == 1)


def load(ref, *index):
    return tuple(ref[(*index, j)] for j in range(ref.shape[len(index)]))


def store(ref, index, items):
    for j, item in enumerate(items):
        ref[(*index, j)] = item


def levels():
    stride = 1
    while stride < STEPS:
        yield stride, range(0, STEPS, 2 * stride), range(stride, STEPS, 2 * stride)
        stride *= 2


def rows_of():
    place, at = {}, 0
    for stride, kept, _ in levels():
        for step in kept:
            place[stride, step] = at
            at += 1
    return place


PLACE = rows_of()


def pack_even(kept, turned, even):
    near = toward_odd()
    half = STEPS // 2
    for j in range(3):
        for i in range(half):
            even[j * half + i] = jnp.where(near, turned[j * half + i], kept[j, i])


def signs(mask, sign):
    sign[...] = jnp.where(jnp.broadcast_to(mask[...], TILE) > 0, -GROW, GROW)


def prepare(field, sat, sign, kept, turned, odd):
    near = toward_odd()
    half = STEPS // 2
    rows = [pl.ds(i, CHUNKS, stride=STEPS) for i in range(STEPS)]
    sign = sign[...]
    low, high = [None] * PACK, [None] * PACK
    for i in (*range(half, STEPS), *range(half)):
        for j, x in reversed(list(enumerate((field[0, rows[i], :], field[1, rows[i], :] * (1.0 / SCALE), sat[rows[i], :] * sign)))):
            if i >= half:
                high[(j - 1) * half + i] = roll(x, XS, 1)
            else:
                low[j * half + i] = x
            kept[j, i] = x
    for i in range(PACK):
        odd[i] = jnp.where(near, low[i], high[i])
    for i in range(PACK):
        turned[i] = high[i]


def tile():
    return lax.axis_index("tile")


def line():
    return lax.axis_index("line")


def at_row_end():
    place = lax.rem(lax.axis_index("tile"), ROW)
    return jnp.logical_or(place == 0, place == ROW - 1)


def inner(field_hbm, sat_hbm, mask_hbm, kept, turned, odd, even, fbuf, sbuf, mbuf, gbuf, sems):
    @pl.when(jnp.logical_not(at_row_end()))
    def _():
        copies = [
            pltpu.make_async_copy(field_hbm, fbuf, sems.at[0]),
            pltpu.make_async_copy(sat_hbm, sbuf, sems.at[1]),
            pltpu.make_async_copy(mask_hbm, mbuf, sems.at[2]),
        ]
        for copy in copies:
            copy.start()
        for copy in copies:
            copy.wait()
        signs(mbuf, gbuf)
        prepare(fbuf, sbuf, gbuf, kept, turned, odd)
        pack_even(kept, turned, even)

    @pl.when(jnp.logical_or(tile() == 2, jnp.logical_and(tile() == 1, line() == 1)))
    def _():
        for i in range(PACK):
            odd[i], even[i] = even[i], odd[i]


def ends(field, sat, sign, kept_in, turned_in, odd_in, kept, turned, odd):
    @pl.when(at_row_end())
    def _():
        prepare(field, sat, sign, kept, turned, odd)

    @pl.when(tile() == 0)
    def _():
        pack_even(kept, turned, odd)


def third(kept, turned, arrived, out):
    relay = jnp.logical_and(tile() == 0, line() == 1)

    @pl.when(jnp.logical_not(relay))
    def _():
        pack_even(kept, turned, out)

    @pl.when(relay)
    def _():
        for i in range(PACK):
            out[i] = arrived[i]


def local(kept, turned, one, k_all, rhs, ab, dinv, ring, final, answer, share, own, green):
    first, last = chunks() == 0, chunks() == CHUNKS - 1
    low_line, high_line = line() == 0, line() == 1
    column = lax.rem(lanes(), XS)
    west_end, east_end = column == 0, column == XS - 1
    half = STEPS // 2

    near = toward_odd()
    k = []
    for i in range(STEPS):
        s = kept[2, i]
        ki = conduct(s)
        k.append(ki)
        store(k_all, (i,), ki)
        f = (kept[0, i], kept[1, i])
        if i < half:
            far, far_s = (roll(f[0], XS, 1), roll(f[1], XS, 1)), roll(s, XS, 1)
        else:
            far, far_s = (turned[i - half], turned[i]), turned[i + half]
        far_k = conduct(far_s)
        if i < half:
            store(own, (i,), (*far_k, *far))
        else:
            held = load(own, i - half)
            store(own, (i - half,), tuple(jnp.where(near, x, y) for x, y in zip((*ki, *f), held)))
        total = flux(add(ki, far_k), (far[0] - f[0], far[1] - f[1]))
        west_k = conduct(roll(s, 1, 1))
        west = flux(add(ki, west_k), (roll(f[0], 1, 1) - f[0], roll(f[1], 1, 1) - f[1]))
        edge = flux(ki, f)
        west = tuple(jnp.where(west_end, -e, w) for e, w in zip(edge, west))
        east = tuple(jnp.where(east_end, e, roll(w, -1, 1)) for e, w in zip(edge, west))
        for j in range(2):
            rhs[j, i] = f[j] + (total[j] + (west[j] - east[j]))

    @pl.when(from_first())
    def _():
        for i in range(STEPS):
            pack = [one[j * half + i % half] for j in range(3)]
            far = pack if i >= half else [roll(x, XS, 1) for x in pack]
            total = flux(add(load(k_all, i), conduct(far[2])), (far[0] - kept[0, i], far[1] - kept[1, i]))
            for j in range(2):
                rhs[j, i] = rhs[j, i] + jnp.where(near, 0.0, total[j])

    upper = {i: wide(add(k[i], k[i + 1])) for i in range(STEPS - 1)}
    upper[STEPS - 1] = wide(tuple(jnp.where(last, 0.0, x) for x in add(k[-1], down(k[0], -1))))
    bottom = jnp.logical_and(first, low_line)
    top = jnp.logical_and(last, high_line)
    bottom = tuple(jnp.where(bottom, x, 0.0) for x in k[0])
    top = tuple(jnp.where(top, x, 0.0) for x in k[-1])
    excess = {}

    for stride, keep, drop in levels():
        lower = {}
        for i in (*keep, *drop):
            left = i - stride
            lower[i] = turn(upper[left] if left >= 0 else down(upper[left + STEPS], 1))
        inv = {}
        for i in drop:
            if stride == 1:
                d = symmetric(lower[i], upper[i])
                d = (d[0] + 1.0, d[1], d[2] + 1.0)
                if i == STEPS - 1:
                    d = add(d, top)
            else:
                d = symmetric(excess[i], lower[i], upper[i])
            inv[i] = inverse(d)
            store(dinv, (i,), inv[i])
        for i in keep:
            right, left = i + stride, i - stride
            if left < 0:
                before = wide(down(inv[left + STEPS], 1))
            else:
                before = wide(inv[left])
            a = mul(lower[i], before)
            b = mul(upper[i], wide(inv[right]))
            store(ab, (PLACE[stride, i],), (*a, *b))
            if stride == 1:
                more = add(a, b)
                more = (more[0] + 1.0, more[1], more[2], more[3] + 1.0)
                if i == 0:
                    more = add(more, wide(bottom))
                if right == STEPS - 1:
                    more = add(more, mul(b, wide(top)))
            else:
                prev = excess[left] if left >= 0 else down(excess[left + STEPS], 1)
                more = add(excess[i], mul(a, prev), mul(b, excess[right]))
            excess[i] = more
            upper[i] = mul(b, upper[right])

    start = jnp.where(jnp.logical_and(high_line, first), 1.0, 0.0)
    end = jnp.logical_and(low_line, last)
    one = jnp.where(end, 1.0, 0.0)
    none = jnp.zeros(TILE, jnp.float32)
    source = (one, none, none, one)
    sides = {STEPS - 1: source}
    for stride, keep, _ in levels():
        b = load(ab, PLACE[stride, keep[-1]])[4:8]
        source = tuple(jnp.where(end, x, 0.0) for x in b) if stride == 1 else mul(b, source)
        sides[keep[-1]] = source
    vec = (source[0] + start, source[1], source[2], source[3] + start)

    up, ex = upper[0], excess[0]
    low = turn(down(up, 1))
    shift, place = 1, 0
    while shift < CHUNKS:
        inv = inverse(symmetric(ex, low, up))
        a = mul(low, wide(down(inv, shift)))
        b = mul(up, wide(down(inv, -shift)))
        store(ring, (place,), (*a, *b))
        vec = add(vec, mul(a, down(vec, shift)), mul(b, down(vec, -shift)))
        ex = add(ex, mul(a, down(ex, shift)), mul(b, down(ex, -shift)))
        up = mul(b, down(up, -shift))
        shift *= 2
        place += 1
        low = turn(down(up, shift))
    inv = inverse((ex[0], ex[1], ex[3]))
    store(final, (), inv)
    w = {0: mul(wide(inv), vec)}
    for stride, keep, drop in reversed(list(levels())):
        for i in drop:
            left, right = i - stride, i + stride
            prev = turn(load(ab, PLACE[stride, left])[4:8])
            if right < STEPS:
                after, later = turn(load(ab, PLACE[stride, right])[0:4]), w[right]
            else:
                after, later = turn(down(load(ab, PLACE[stride, 0])[0:4], -1)), down(w[0], -1)
            w[i] = add(mul(prev, w[left]), mul(after, later))
            if i in sides:
                w[i] = add(w[i], mul(wide(load(dinv, i)), sides[i]))
    for i in range(STEPS):
        store(green, (i,), w[i])
        for j, x in enumerate((w[i][0], w[i][1], SCALE * w[i][2], SCALE * w[i][3])):
            answer[j, pl.ds(i, CHUNKS, stride=STEPS), :] = x

    tail = down((w[STEPS - 1][0], w[STEPS - 1][1], w[STEPS - 1][3], kept[2, STEPS - 1]), 1)
    head = (w[0][0], w[0][1], w[0][3], kept[2, 0])
    for j, (x, y) in enumerate(zip(head, tail)):
        share[pl.ds(2 + j, 1), :] = jnp.where(low_line, y, x)[0:1]
    share[pl.ds(0, 2), :] = none[0:2]
    share[pl.ds(6, 2), :] = none[0:2]


def from_first():
    return jnp.logical_and(tile() >= ROW, lax.rem(tile(), ROW) == 0)


def finish(k_all, rhs, kept, own, ab, dinv, ring, final, share, green, one, two, three, local_x, message, pending):
    half = STEPS // 2
    at, high = tile(), line() == 1
    near = toward_odd()
    rest = (ab, dinv, ring, final, share, green, local_x, message, pending)

    @pl.when(from_first())
    def _():
        b = {i: (rhs[0, i], rhs[1, i]) for i in range(STEPS)}
        for i in range(half):
            mine = load(own, i)
            total = flux(add(mine[:3], conduct(two[2 * half + i])), (two[i] - mine[3], two[half + i] - mine[4]))
            b[i + half] = add(b[i + half], tuple(jnp.where(near, x, 0.0) for x in total))
            b[i] = add(b[i], tuple(jnp.where(near, roll(x, XS, 1), 0.0) for x in total))
        conclude(b, *rest)

    def both(halo):
        alone = jnp.logical_or(at == 0, at == lax.axis_size("tile") - 1)
        inside = jnp.logical_not(jnp.logical_and(near, alone))
        far = {}
        for j in range(3):
            for i in range(half):
                o, e = halo(j * half + i)
                far[j, i] = roll(jnp.where(near, e, o), XS, 1)
                far[j, i + half] = jnp.where(near, o, e)
        b = {}
        for i in range(STEPS):
            drop = (far[0, i] - kept[0, i], far[1, i] - kept[1, i])
            total = flux(add(load(k_all, i), conduct(far[2, i], inside)), drop)
            b[i] = (rhs[0, i] + total[0], rhs[1, i] + total[1])
        conclude(b, *rest)

    @pl.when(jnp.logical_and(at >= ROW, jnp.logical_not(from_first())))
    def _():
        both(lambda i: (two[i], three[i]))

    @pl.when(at < ROW)
    def _():
        def halo(i):
            odd = jnp.where(at == 1, one[i], two[i])
            odd = jnp.where(jnp.logical_and(high, at == 2), one[i], odd)
            odd = jnp.where(jnp.logical_and(high, at == 0), three[i], odd)
            even = jnp.where(jnp.logical_or(at == 1, jnp.logical_and(high, at == 0)), two[i], three[i])
            return odd, even

        both(halo)


def conclude(b, ab, dinv, ring, final, share, green, local_x, message, pending):
    message[...] = share[...]

    @pl.when(line() == 0)
    def _():
        parts = []
        for i in range(STEPS):
            w = load(green, i)
            parts.append((w[0] * b[i][0] + w[2] * b[i][1], w[1] * b[i][0] + w[3] * b[i][1]))
            store(pending, (i,), b[i])
        while len(parts) > 1:
            parts = [add(x, y) for x, y in zip(parts[::2], parts[1::2])]
        d = parts[0]
        for shift in (4, 2, 1):
            d = add(d, down(d, shift))
        for j in range(2):
            message[pl.ds(j, 1), :] = d[j][0:1]

    @pl.when(line() == 1)
    def _():
        x = solve(b, ab, dinv, ring, final)
        for j in range(2):
            message[pl.ds(j, 1), :] = x[0][j][0:1]
        for i in range(STEPS):
            here = pl.ds(i, CHUNKS, stride=STEPS)
            local_x[0, here, :] = x[i][0]
            local_x[1, here, :] = SCALE * x[i][1]


def solve(b, ab, dinv, ring, final):
    b = dict(b)
    for stride, keep, drop in levels():
        for i in keep:
            left = i - stride
            prev = b[left] if left >= 0 else down(b[left + STEPS], 1)
            c = load(ab, PLACE[stride, i])
            b[i] = add(b[i], apply(c[0:4], prev), apply(c[4:8], b[i + stride]))
    vec = b[0]
    shift, place = 1, 0
    while shift < CHUNKS:
        c = load(ring, place)
        vec = add(vec, apply(c[0:4], down(vec, shift)), apply(c[4:8], down(vec, -shift)))
        shift *= 2
        place += 1
    x = {0: apply(wide(load(final)), vec)}
    for stride, keep, drop in reversed(list(levels())):
        for i in drop:
            left, right = i - stride, i + stride
            prev = turn(load(ab, PLACE[stride, left])[4:8])
            if right < STEPS:
                after, later = turn(load(ab, PLACE[stride, right])[0:4]), x[right]
            else:
                after, later = turn(down(load(ab, PLACE[stride, 0])[0:4], -1)), down(x[0], -1)
            x[i] = add(apply(wide(load(dinv, i)), b[i]), apply(prev, x[left]), apply(after, later))
    return x


def join(local_x, answer, both, pending, ab, dinv, ring, final, out_hbm, out, sems):
    def row(who, j):
        return jnp.broadcast_to(both[who, pl.ds(j, 1), :], TILE)

    sign = jnp.where(line() == 0, 1.0, -1.0)
    drop = tuple(sign * (row(1, j) - row(0, j)) for j in range(2))
    reach = wide(tuple(row(0, 2 + j) + row(1, 2 + j) for j in range(3)))
    face = add(conduct(row(0, 5)), conduct(row(1, 5)))
    m = mul(wide(face), reach)
    m = (m[0] + 1.0, m[1], m[2], m[3] + 1.0)
    push = flux(face, drop)
    scale = 1.0 / (m[0] * m[3] - m[1] * m[2])
    through = ((m[3] * push[0] - m[1] * push[1]) * scale, (m[0] * push[1] - m[2] * push[0]) * scale)

    copies = [pltpu.make_async_copy(out.at[j], out_hbm.at[j], sems.at[j]) for j in range(2)]

    @pl.when(line() == 0)
    def _():
        b = {i: load(pending, i) for i in range(STEPS)}
        last = chunks() == CHUNKS - 1
        b[STEPS - 1] = add(b[STEPS - 1], tuple(jnp.where(last, x, 0.0) for x in through))
        x = solve(b, ab, dinv, ring, final)
        for i in range(STEPS):
            here = pl.ds(i, CHUNKS, stride=STEPS)
            out[0, here, :] = x[i][0]
            out[1, here, :] = SCALE * x[i][1]
        for copy in copies:
            copy.start()

    @pl.when(line() == 1)
    def _():
        for j in range(2):
            for i in range(STEPS):
                here = pl.ds(i * CHUNKS, CHUNKS)
                change = answer[2 * j, here, :] * through[0] + answer[2 * j + 1, here, :] * through[1]
                out[j, here, :] = local_x[j, here, :] + change
            copies[j].start()

    for copy in copies:
        copy.wait()


def tiles(*lead):
    return jax.ShapeDtypeStruct((*lead, *TILE), jnp.float32)


def call(kernel, outs, args, name, flops, **more):
    vmem = pl.BlockSpec(memory_space=pltpu.VMEM)
    more.setdefault("in_specs", [vmem] * len(args))
    if "out_specs" not in more:
        more["out_specs"] = [vmem] * len(outs)
    return pl.pallas_call(
        kernel,
        out_shape=outs,
        compiler_params=pltpu.CompilerParams(vmem_limit_bytes=LIMIT),
        cost_estimate=pl.CostEstimate(flops=flops, bytes_accessed=1 << 20, transcendentals=0),
        name=name,
        **more,
    )(*args)


def moves(count):
    ops = [[], [], []]
    for base in (0, count):
        for t in range(base, base + count, ROW):
            ops[2] += [(t + 2, t + 3), (t + 3, t + 2)]
            if t > base:
                ops[0].append((t + 1, t))
                ops[1] += [(t - 1, t), (t, t - 1), (t + 1, t + 2), (t + 2, t + 1)]
                ops[2].append((t, t + 1))
    ops[0] += [(1, count), (2, 1), (count + 1, count + 2), (count + 2, count + 1)]
    ops[1] += [(0, 1), (1, 2), (count, count + 1), (count + 1, count)]
    ops[2].append((count, 0))
    return ops


def body(field, saturation, solid_mask):
    ops = moves(lax.axis_size("tile"))
    both_axes = ("line", "tile")
    cells = STEPS * CHUNKS
    in_hbm = [pltpu.with_memory_space_constraint(x, pltpu.HBM) for x in (field, saturation, solid_mask)]
    kept, turned, two, one = call(
        inner,
        [tiles(3, STEPS), tiles(PACK), tiles(PACK), tiles(PACK)],
        in_hbm,
        "inner",
        1 << 16,
        in_specs=[pl.BlockSpec(memory_space=pltpu.HBM)] * 3,
        scratch_shapes=[
            pltpu.VMEM((2, cells, LANES), jnp.float32),
            pltpu.VMEM((cells, LANES), jnp.float32),
            pltpu.VMEM((1, LANES), jnp.int32),
            pltpu.VMEM(TILE, jnp.float32),
            pltpu.SemaphoreType.DMA((3,)),
        ],
    )
    from_one = lax.ppermute(one, both_axes, ops[0])
    (sign,) = call(signs, [tiles()], (solid_mask,), "signs", 1 << 8)
    kept, turned, two = call(
        ends,
        [tiles(3, STEPS), tiles(PACK), tiles(PACK)],
        (field, saturation, sign, kept, turned, two),
        "ends",
        1 << 16,
        input_output_aliases={3: 0, 4: 1, 5: 2},
    )
    from_two = lax.ppermute(two, both_axes, ops[1])
    (three,) = call(third, [tiles(PACK)], (kept, turned, from_one), "third", 1 << 12)
    from_three = lax.ppermute(three, both_axes, ops[2])
    k_all, rhs, ab, dinv, ring, final, answer, share, own, green = call(
        local,
        [
            tiles(STEPS, 3),
            tiles(2, STEPS),
            tiles(STEPS - 1, 8),
            tiles(STEPS, 3),
            tiles(3, 8),
            tiles(3),
            jax.ShapeDtypeStruct((4, cells, LANES), jnp.float32),
            jax.ShapeDtypeStruct((8, LANES), jnp.float32),
            tiles(STEPS // 2, 5),
            tiles(STEPS, 4),
        ],
        (kept, turned, from_one),
        "local",
        1 << 23,
    )
    local_x, message, pending = call(
        finish,
        [jax.ShapeDtypeStruct((2, cells, LANES), jnp.float32), jax.ShapeDtypeStruct((8, LANES), jnp.float32), tiles(STEPS, 2)],
        (k_all, rhs, kept, own, ab, dinv, ring, final, share, green, from_one, from_two, from_three),
        "finish",
        1 << 21,
    )
    both = lax.all_gather(message, "line", axis=0)
    return call(
        join,
        jax.ShapeDtypeStruct((2, cells, LANES), jnp.float32),
        (local_x, answer, both, pending, ab, dinv, ring, final),
        "join",
        1 << 18,
        out_specs=pl.BlockSpec(memory_space=pltpu.HBM),
        scratch_shapes=[pltpu.VMEM((2, cells, LANES), jnp.float32), pltpu.SemaphoreType.DMA((2,))],
    )


def solution(mesh):
    in_specs = (P(None, "line", "tile"), P("line", "tile"), P("line", "tile"))
    out_specs = P(None, "line", "tile")
    return jax.shard_map(body, mesh=mesh, in_specs=in_specs, out_specs=out_specs, check_vma=False)
```

```python
import jax
import jax.numpy as jnp
from jax import lax
from jax.experimental import pallas as pl
from jax.experimental.pallas import tpu as pltpu
from jax.sharding import PartitionSpec as P

XS = 64
ZSTIFF = 2048
HALF = 0.5 * ZSTIFF
STEPS = 16
CHUNKS = 8
LANES = 128
TILE = (CHUNKS, LANES)
ROW = 4
SCALE = 0.4**0.5
CROSS = 0.1**0.5
GROW = HALF ** (1.0 / 3.0)
PACK = STEPS + STEPS // 2
LIMIT = 12 * 1024 * 1024


def mul(a, b):
    return (
        a[0] * b[0] + a[1] * b[2],
        a[0] * b[1] + a[1] * b[3],
        a[2] * b[0] + a[3] * b[2],
        a[2] * b[1] + a[3] * b[3],
    )


def wide(s):
    return (s[0], s[1], s[1], s[2])


def turn(a):
    return (a[0], a[2], a[1], a[3])


def apply(a, v):
    return (a[0] * v[0] + a[1] * v[1], a[2] * v[0] + a[3] * v[1])


def add(*items):
    total = items[0]
    for item in items[1:]:
        total = tuple(x + y for x, y in zip(total, item))
    return total


def symmetric(a, *more):
    return add(*((m[0], m[1], m[3]) for m in (a, *more)))


def inverse(s):
    scale = 1.0 / (s[0] * s[2] - s[1] * s[1])
    return (s[2] * scale, -s[1] * scale, s[0] * scale)


def conduct(signed, inside=None):
    dry = jnp.maximum(signed, 0.0)
    moist = HALF * 0.004 + dry * dry * dry
    pore = signed > 0.0
    heat = jnp.where(pore, HALF + (2.0 * HALF / GROW) * signed, 3.0 * HALF)
    cross = jnp.where(pore, CROSS * moist, 0.0)
    if inside is None:
        return (heat, cross, moist)
    return (jnp.where(inside, heat, 0.0), cross, jnp.where(inside, moist, 0.0))


def flux(k, drop):
    return (k[0] * drop[0] + k[1] * drop[1], k[1] * drop[0] + k[2] * drop[1])


def roll(x, shift, axis):
    return pltpu.roll(x, shift % x.shape[axis], axis)


def down(items, shift):
    return tuple(roll(x, shift, 0) for x in items)


def over_chunks(items):
    for shift in (4, 2, 1):
        items = add(items, down(items, shift))
    return items


def lanes():
    return lax.broadcasted_iota(jnp.int32, TILE, 1)


def chunks():
    return lax.broadcasted_iota(jnp.int32, TILE, 0)


def toward_odd():
    parity = lax.rem(lax.axis_index("tile"), 2)
    return (lanes() >= XS) == (parity == 1)


def load(ref, *index):
    return tuple(ref[(*index, j)] for j in range(ref.shape[len(index)]))


def store(ref, index, items):
    for j, item in enumerate(items):
        ref[(*index, j)] = item


def levels():
    stride = 1
    while stride < STEPS:
        yield stride, range(0, STEPS, 2 * stride), range(stride, STEPS, 2 * stride)
        stride *= 2


def rows_of():
    place, at = {}, 0
    for stride, kept, _ in levels():
        for step in kept:
            place[stride, step] = at
            at += 1
    return place


PLACE = rows_of()


def pack_even(kept, turned, even):
    near = toward_odd()
    half = STEPS // 2
    for j in range(3):
        for i in range(half):
            even[j * half + i] = jnp.where(near, turned[j * half + i], kept[j, i])


def signs(mask, sign):
    sign[...] = jnp.where(jnp.broadcast_to(mask[...], TILE) > 0, -GROW, GROW)


def prepare(field, sat, sign, kept, turned, odd):
    near = toward_odd()
    half = STEPS // 2
    rows = [pl.ds(i, CHUNKS, stride=STEPS) for i in range(STEPS)]
    sign = sign[...]
    low, high = [None] * PACK, [None] * PACK
    for i in (*range(half, STEPS), *range(half)):
        for j, x in reversed(list(enumerate((field[0, rows[i], :], field[1, rows[i], :] * (1.0 / SCALE), sat[rows[i], :] * sign)))):
            if i >= half:
                high[(j - 1) * half + i] = roll(x, XS, 1)
            else:
                low[j * half + i] = x
            kept[j, i] = x
    for i in range(PACK):
        odd[i] = jnp.where(near, low[i], high[i])
    for i in range(PACK):
        turned[i] = high[i]


def tile():
    return lax.axis_index("tile")


def line():
    return lax.axis_index("line")


def at_row_end():
    place = lax.rem(lax.axis_index("tile"), ROW)
    return jnp.logical_or(place == 0, place == ROW - 1)


def inner(field_hbm, sat_hbm, mask_hbm, kept, turned, odd, even, fbuf, sbuf, mbuf, gbuf, sems):
    @pl.when(jnp.logical_not(at_row_end()))
    def _():
        copies = [
            pltpu.make_async_copy(field_hbm, fbuf, sems.at[0]),
            pltpu.make_async_copy(sat_hbm, sbuf, sems.at[1]),
            pltpu.make_async_copy(mask_hbm, mbuf, sems.at[2]),
        ]
        for copy in copies:
            copy.start()
        for copy in copies:
            copy.wait()
        signs(mbuf, gbuf)
        prepare(fbuf, sbuf, gbuf, kept, turned, odd)
        pack_even(kept, turned, even)

    @pl.when(jnp.logical_or(tile() == 2, jnp.logical_and(tile() == 1, line() == 1)))
    def _():
        for i in range(PACK):
            odd[i], even[i] = even[i], odd[i]


def ends(field, sat, sign, kept_in, turned_in, odd_in, kept, turned, odd):
    @pl.when(at_row_end())
    def _():
        prepare(field, sat, sign, kept, turned, odd)

    @pl.when(tile() == 0)
    def _():
        pack_even(kept, turned, odd)


def third(kept, turned, arrived, out):
    relay = jnp.logical_and(tile() == 0, line() == 1)

    @pl.when(jnp.logical_not(relay))
    def _():
        pack_even(kept, turned, out)

    @pl.when(relay)
    def _():
        for i in range(PACK):
            out[i] = arrived[i]


def local(kept, turned, one, k_all, rhs, ab, dinv, ring, final, answer, share, own, green, own_green, known):
    first, last = chunks() == 0, chunks() == CHUNKS - 1
    low_line, high_line = line() == 0, line() == 1
    column = lax.rem(lanes(), XS)
    west_end, east_end = column == 0, column == XS - 1
    half = STEPS // 2

    near = toward_odd()
    k = []
    for i in range(STEPS):
        s = kept[2, i]
        ki = conduct(s)
        k.append(ki)
        store(k_all, (i,), ki)
        f = (kept[0, i], kept[1, i])
        if i < half:
            far, far_s = (roll(f[0], XS, 1), roll(f[1], XS, 1)), roll(s, XS, 1)
        else:
            far, far_s = (turned[i - half], turned[i]), turned[i + half]
        far_k = conduct(far_s)
        if i < half:
            store(own, (i,), (*far_k, *far))
        else:
            held = load(own, i - half)
            store(own, (i - half,), tuple(jnp.where(near, x, y) for x, y in zip((*ki, *f), held)))
        total = flux(add(ki, far_k), (far[0] - f[0], far[1] - f[1]))
        west_k = conduct(roll(s, 1, 1))
        west = flux(add(ki, west_k), (roll(f[0], 1, 1) - f[0], roll(f[1], 1, 1) - f[1]))
        edge = flux(ki, f)
        west = tuple(jnp.where(west_end, -e, w) for e, w in zip(edge, west))
        east = tuple(jnp.where(east_end, e, roll(w, -1, 1)) for e, w in zip(edge, west))
        for j in range(2):
            rhs[j, i] = f[j] + (total[j] + (west[j] - east[j]))

    @pl.when(from_first())
    def _():
        for i in range(STEPS):
            pack = [one[j * half + i % half] for j in range(3)]
            far = pack if i >= half else [roll(x, XS, 1) for x in pack]
            total = flux(add(load(k_all, i), conduct(far[2])), (far[0] - kept[0, i], far[1] - kept[1, i]))
            for j in range(2):
                rhs[j, i] = rhs[j, i] + jnp.where(near, 0.0, total[j])

    upper = {i: wide(add(k[i], k[i + 1])) for i in range(STEPS - 1)}
    upper[STEPS - 1] = wide(tuple(jnp.where(last, 0.0, x) for x in add(k[-1], down(k[0], -1))))
    bottom = jnp.logical_and(first, low_line)
    top = jnp.logical_and(last, high_line)
    bottom = tuple(jnp.where(bottom, x, 0.0) for x in k[0])
    top = tuple(jnp.where(top, x, 0.0) for x in k[-1])
    excess = {}

    for stride, keep, drop in levels():
        lower = {}
        for i in (*keep, *drop):
            left = i - stride
            lower[i] = turn(upper[left] if left >= 0 else down(upper[left + STEPS], 1))
        inv = {}
        for i in drop:
            if stride == 1:
                d = symmetric(lower[i], upper[i])
                d = (d[0] + 1.0, d[1], d[2] + 1.0)
                if i == STEPS - 1:
                    d = add(d, top)
            else:
                d = symmetric(excess[i], lower[i], upper[i])
            inv[i] = inverse(d)
            store(dinv, (i,), inv[i])
        for i in keep:
            right, left = i + stride, i - stride
            if left < 0:
                before = wide(down(inv[left + STEPS], 1))
            else:
                before = wide(inv[left])
            a = mul(lower[i], before)
            b = mul(upper[i], wide(inv[right]))
            store(ab, (PLACE[stride, i],), (*a, *b))
            if stride == 1:
                more = add(a, b)
                more = (more[0] + 1.0, more[1], more[2], more[3] + 1.0)
                if i == 0:
                    more = add(more, wide(bottom))
                if right == STEPS - 1:
                    more = add(more, mul(b, wide(top)))
            else:
                prev = excess[left] if left >= 0 else down(excess[left + STEPS], 1)
                more = add(excess[i], mul(a, prev), mul(b, excess[right]))
            excess[i] = more
            upper[i] = mul(b, upper[right])

    start = jnp.where(jnp.logical_and(high_line, first), 1.0, 0.0)
    end = jnp.logical_and(low_line, last)
    one = jnp.where(end, 1.0, 0.0)
    none = jnp.zeros(TILE, jnp.float32)
    source = (one, none, none, one)
    sides = {STEPS - 1: source}
    for stride, keep, _ in levels():
        b = load(ab, PLACE[stride, keep[-1]])[4:8]
        source = tuple(jnp.where(end, x, 0.0) for x in b) if stride == 1 else mul(b, source)
        sides[keep[-1]] = source
    vec = (source[0] + start, source[1], source[2], source[3] + start)

    up, ex = upper[0], excess[0]
    low = turn(down(up, 1))
    shift, place = 1, 0
    while shift < CHUNKS:
        inv = inverse(symmetric(ex, low, up))
        a = mul(low, wide(down(inv, shift)))
        b = mul(up, wide(down(inv, -shift)))
        store(ring, (place,), (*a, *b))
        vec = add(vec, mul(a, down(vec, shift)), mul(b, down(vec, -shift)))
        ex = add(ex, mul(a, down(ex, shift)), mul(b, down(ex, -shift)))
        up = mul(b, down(up, -shift))
        shift *= 2
        place += 1
        low = turn(down(up, shift))
    inv = inverse((ex[0], ex[1], ex[3]))
    store(final, (), inv)
    w = {0: mul(wide(inv), vec)}
    for stride, keep, drop in reversed(list(levels())):
        for i in drop:
            left, right = i - stride, i + stride
            prev = turn(load(ab, PLACE[stride, left])[4:8])
            if right < STEPS:
                after, later = turn(load(ab, PLACE[stride, right])[0:4]), w[right]
            else:
                after, later = turn(down(load(ab, PLACE[stride, 0])[0:4], -1)), down(w[0], -1)
            w[i] = add(mul(prev, w[left]), mul(after, later))
            if i in sides:
                w[i] = add(w[i], mul(wide(load(dinv, i)), sides[i]))
    for i in range(STEPS):
        store(green, (i,), w[i])
        for j, x in enumerate((w[i][0], w[i][1], SCALE * w[i][2], SCALE * w[i][3])):
            answer[j, pl.ds(i, CHUNKS, stride=STEPS), :] = x

    @pl.when(from_first())
    def _():
        total = apply(turn(w[0]), (rhs[0, 0], rhs[1, 0]))
        for i in range(1, STEPS):
            total = add(total, apply(turn(w[i]), (rhs[0, i], rhs[1, i])))
        store(known, (), over_chunks(total))
        for i in range(half):
            store(own_green, (i,), tuple(jnp.where(near, x, roll(y, XS, 1)) for x, y in zip(w[i + half], w[i])))

    tail = down((w[STEPS - 1][0], w[STEPS - 1][1], w[STEPS - 1][3], kept[2, STEPS - 1]), 1)
    head = (w[0][0], w[0][1], w[0][3], kept[2, 0])
    for j, (x, y) in enumerate(zip(head, tail)):
        share[pl.ds(2 + j, 1), :] = jnp.where(low_line, y, x)[0:1]
    share[pl.ds(0, 2), :] = none[0:2]
    share[pl.ds(6, 2), :] = none[0:2]


def from_first():
    return jnp.logical_and(tile() >= ROW, lax.rem(tile(), ROW) == 0)


def finish(k_all, rhs, kept, own, ab, dinv, ring, final, share, green, own_green, known, one, two, three, local_x, message, pending):
    half = STEPS // 2
    at, high = tile(), line() == 1
    near = toward_odd()
    rest = (ab, dinv, ring, final, share, green, local_x, message, pending)

    @pl.when(from_first())
    def _():
        through = []
        for i in range(half):
            mine = load(own, i)
            drop = (two[i] - mine[3], two[half + i] - mine[4])
            through.append(flux(add(mine[:3], conduct(two[2 * half + i])), drop))

        @pl.when(line() == 0)
        def _():
            parts = [apply(turn(load(own_green, i)), through[i]) for i in range(half)]
            while len(parts) > 1:
                parts = [add(x, y) for x, y in zip(parts[::2], parts[1::2])]
            d = over_chunks(parts[0])
            message[...] = share[...]
            for j in range(2):
                x = known[j] + jnp.where(near, d[j] + roll(d[j], XS, 1), 0.0)
                message[pl.ds(j, 1), :] = x[0:1]
            for i in range(half):
                store(pending, (i,), through[i])

        @pl.when(line() == 1)
        def _():
            b = {}
            for i in range(half):
                b[i + half] = tuple(rhs[j, i + half] + jnp.where(near, through[i][j], 0.0) for j in range(2))
                b[i] = tuple(rhs[j, i] + jnp.where(near, roll(through[i][j], XS, 1), 0.0) for j in range(2))
            conclude(b, *rest)

    def both(halo):
        alone = jnp.logical_or(at == 0, at == lax.axis_size("tile") - 1)
        inside = jnp.logical_not(jnp.logical_and(near, alone))
        far = {}
        for j in range(3):
            for i in range(half):
                o, e = halo(j * half + i)
                far[j, i] = roll(jnp.where(near, e, o), XS, 1)
                far[j, i + half] = jnp.where(near, o, e)
        b = {}
        for i in range(STEPS):
            drop = (far[0, i] - kept[0, i], far[1, i] - kept[1, i])
            total = flux(add(load(k_all, i), conduct(far[2, i], inside)), drop)
            b[i] = (rhs[0, i] + total[0], rhs[1, i] + total[1])
        conclude(b, *rest)

    @pl.when(jnp.logical_and(at >= ROW, jnp.logical_not(from_first())))
    def _():
        both(lambda i: (two[i], three[i]))

    @pl.when(at < ROW)
    def _():
        def halo(i):
            odd = jnp.where(at == 1, one[i], two[i])
            odd = jnp.where(jnp.logical_and(high, at == 2), one[i], odd)
            odd = jnp.where(jnp.logical_and(high, at == 0), three[i], odd)
            even = jnp.where(jnp.logical_or(at == 1, jnp.logical_and(high, at == 0)), two[i], three[i])
            return odd, even

        both(halo)


def conclude(b, ab, dinv, ring, final, share, green, local_x, message, pending):
    message[...] = share[...]

    @pl.when(line() == 0)
    def _():
        parts = []
        for i in range(STEPS):
            w = load(green, i)
            parts.append((w[0] * b[i][0] + w[2] * b[i][1], w[1] * b[i][0] + w[3] * b[i][1]))
            store(pending, (i,), b[i])
        while len(parts) > 1:
            parts = [add(x, y) for x, y in zip(parts[::2], parts[1::2])]
        d = over_chunks(parts[0])
        for j in range(2):
            message[pl.ds(j, 1), :] = d[j][0:1]

    @pl.when(line() == 1)
    def _():
        x = solve(b, ab, dinv, ring, final)
        for j in range(2):
            message[pl.ds(j, 1), :] = x[0][j][0:1]
        for i in range(STEPS):
            here = pl.ds(i, CHUNKS, stride=STEPS)
            local_x[0, here, :] = x[i][0]
            local_x[1, here, :] = SCALE * x[i][1]


def solve(b, ab, dinv, ring, final):
    b = dict(b)
    for stride, keep, drop in levels():
        for i in keep:
            left = i - stride
            prev = b[left] if left >= 0 else down(b[left + STEPS], 1)
            c = load(ab, PLACE[stride, i])
            b[i] = add(b[i], apply(c[0:4], prev), apply(c[4:8], b[i + stride]))
    vec = b[0]
    shift, place = 1, 0
    while shift < CHUNKS:
        c = load(ring, place)
        vec = add(vec, apply(c[0:4], down(vec, shift)), apply(c[4:8], down(vec, -shift)))
        shift *= 2
        place += 1
    x = {0: apply(wide(load(final)), vec)}
    for stride, keep, drop in reversed(list(levels())):
        for i in drop:
            left, right = i - stride, i + stride
            prev = turn(load(ab, PLACE[stride, left])[4:8])
            if right < STEPS:
                after, later = turn(load(ab, PLACE[stride, right])[0:4]), x[right]
            else:
                after, later = turn(down(load(ab, PLACE[stride, 0])[0:4], -1)), down(x[0], -1)
            x[i] = add(apply(wide(load(dinv, i)), b[i]), apply(prev, x[left]), apply(after, later))
    return x


def join(local_x, answer, both, rhs, pending, ab, dinv, ring, final, out_hbm, out, sems):
    def row(who, j):
        return jnp.broadcast_to(both[who, pl.ds(j, 1), :], TILE)

    sign = jnp.where(line() == 0, 1.0, -1.0)
    drop = tuple(sign * (row(1, j) - row(0, j)) for j in range(2))
    reach = wide(tuple(row(0, 2 + j) + row(1, 2 + j) for j in range(3)))
    face = add(conduct(row(0, 5)), conduct(row(1, 5)))
    m = mul(wide(face), reach)
    m = (m[0] + 1.0, m[1], m[2], m[3] + 1.0)
    push = flux(face, drop)
    scale = 1.0 / (m[0] * m[3] - m[1] * m[2])
    through = ((m[3] * push[0] - m[1] * push[1]) * scale, (m[0] * push[1] - m[2] * push[0]) * scale)

    copies = [pltpu.make_async_copy(out.at[j], out_hbm.at[j], sems.at[j]) for j in range(2)]

    @pl.when(line() == 0)
    def _():
        half = STEPS // 2
        near = toward_odd()
        packed = from_first()
        b = {}
        for i in range(half):
            low, high = load(pending, i), load(pending, i + half)
            for step, left, flow in ((i, low, tuple(roll(x, XS, 1) for x in low)), (i + half, high, low)):
                b[step] = tuple(
                    jnp.where(packed, rhs[j, step] + jnp.where(near, flow[j], 0.0), left[j]) for j in range(2)
                )
        last = chunks() == CHUNKS - 1
        b[STEPS - 1] = add(b[STEPS - 1], tuple(jnp.where(last, x, 0.0) for x in through))
        x = solve(b, ab, dinv, ring, final)
        for i in range(STEPS):
            here = pl.ds(i, CHUNKS, stride=STEPS)
            out[0, here, :] = x[i][0]
            out[1, here, :] = SCALE * x[i][1]
        for copy in copies:
            copy.start()

    @pl.when(line() == 1)
    def _():
        for j in range(2):
            for i in range(STEPS):
                here = pl.ds(i * CHUNKS, CHUNKS)
                change = answer[2 * j, here, :] * through[0] + answer[2 * j + 1, here, :] * through[1]
                out[j, here, :] = local_x[j, here, :] + change
            copies[j].start()

    for copy in copies:
        copy.wait()


def tiles(*lead):
    return jax.ShapeDtypeStruct((*lead, *TILE), jnp.float32)


def call(kernel, outs, args, name, flops, **more):
    vmem = pl.BlockSpec(memory_space=pltpu.VMEM)
    more.setdefault("in_specs", [vmem] * len(args))
    if "out_specs" not in more:
        more["out_specs"] = [vmem] * len(outs)
    return pl.pallas_call(
        kernel,
        out_shape=outs,
        compiler_params=pltpu.CompilerParams(vmem_limit_bytes=LIMIT),
        cost_estimate=pl.CostEstimate(flops=flops, bytes_accessed=1 << 20, transcendentals=0),
        name=name,
        **more,
    )(*args)


def moves(count):
    ops = [[], [], []]
    for base in (0, count):
        for t in range(base, base + count, ROW):
            ops[2] += [(t + 2, t + 3), (t + 3, t + 2)]
            if t > base:
                ops[0].append((t + 1, t))
                ops[1] += [(t - 1, t), (t, t - 1), (t + 1, t + 2), (t + 2, t + 1)]
                ops[2].append((t, t + 1))
    ops[0] += [(1, count), (2, 1), (count + 1, count + 2), (count + 2, count + 1)]
    ops[1] += [(0, 1), (1, 2), (count, count + 1), (count + 1, count)]
    ops[2].append((count, 0))
    return ops


def body(field, saturation, solid_mask):
    ops = moves(lax.axis_size("tile"))
    both_axes = ("line", "tile")
    cells = STEPS * CHUNKS
    in_hbm = [pltpu.with_memory_space_constraint(x, pltpu.HBM) for x in (field, saturation, solid_mask)]
    kept, turned, two, one = call(
        inner,
        [tiles(3, STEPS), tiles(PACK), tiles(PACK), tiles(PACK)],
        in_hbm,
        "inner",
        1 << 16,
        in_specs=[pl.BlockSpec(memory_space=pltpu.HBM)] * 3,
        scratch_shapes=[
            pltpu.VMEM((2, cells, LANES), jnp.float32),
            pltpu.VMEM((cells, LANES), jnp.float32),
            pltpu.VMEM((1, LANES), jnp.int32),
            pltpu.VMEM(TILE, jnp.float32),
            pltpu.SemaphoreType.DMA((3,)),
        ],
    )
    from_one = lax.ppermute(one, both_axes, ops[0])
    (sign,) = call(signs, [tiles()], (solid_mask,), "signs", 1 << 8)
    kept, turned, two = call(
        ends,
        [tiles(3, STEPS), tiles(PACK), tiles(PACK)],
        (field, saturation, sign, kept, turned, two),
        "ends",
        1 << 16,
        input_output_aliases={3: 0, 4: 1, 5: 2},
    )
    from_two = lax.ppermute(two, both_axes, ops[1])
    (three,) = call(third, [tiles(PACK)], (kept, turned, from_one), "third", 1 << 12)
    from_three = lax.ppermute(three, both_axes, ops[2])
    k_all, rhs, ab, dinv, ring, final, answer, share, own, green, own_green, known = call(
        local,
        [
            tiles(STEPS, 3),
            tiles(2, STEPS),
            tiles(STEPS - 1, 8),
            tiles(STEPS, 3),
            tiles(3, 8),
            tiles(3),
            jax.ShapeDtypeStruct((4, cells, LANES), jnp.float32),
            jax.ShapeDtypeStruct((8, LANES), jnp.float32),
            tiles(STEPS // 2, 5),
            tiles(STEPS, 4),
            tiles(STEPS // 2, 4),
            tiles(2),
        ],
        (kept, turned, from_one),
        "local",
        1 << 23,
    )
    local_x, message, pending = call(
        finish,
        [jax.ShapeDtypeStruct((2, cells, LANES), jnp.float32), jax.ShapeDtypeStruct((8, LANES), jnp.float32), tiles(STEPS, 2)],
        (k_all, rhs, kept, own, ab, dinv, ring, final, share, green, own_green, known, from_one, from_two, from_three),
        "finish",
        1 << 21,
    )
    both = lax.all_gather(message, "line", axis=0)
    return call(
        join,
        jax.ShapeDtypeStruct((2, cells, LANES), jnp.float32),
        (local_x, answer, both, rhs, pending, ab, dinv, ring, final),
        "join",
        1 << 18,
        out_specs=pl.BlockSpec(memory_space=pltpu.HBM),
        scratch_shapes=[pltpu.VMEM((2, cells, LANES), jnp.float32), pltpu.SemaphoreType.DMA((2,))],
    )


def solution(mesh):
    in_specs = (P(None, "line", "tile"), P("line", "tile"), P("line", "tile"))
    out_specs = P(None, "line", "tile")
    return jax.shard_map(body, mesh=mesh, in_specs=in_specs, out_specs=out_specs, check_vma=False)
```

```python
import jax
import jax.numpy as jnp
from jax import lax
from jax.experimental import pallas as pl
from jax.experimental.pallas import tpu as pltpu
from jax.sharding import PartitionSpec as P

XS = 64
ZSTIFF = 2048
HALF = 0.5 * ZSTIFF
STEPS = 16
CHUNKS = 8
LANES = 128
TILE = (CHUNKS, LANES)
ROW = 4
SCALE = 0.4**0.5
CROSS = 0.1**0.5
GROW = HALF ** (1.0 / 3.0)
PACK = STEPS + STEPS // 2
LIMIT = 12 * 1024 * 1024


def mul(a, b):
    return (
        a[0] * b[0] + a[1] * b[2],
        a[0] * b[1] + a[1] * b[3],
        a[2] * b[0] + a[3] * b[2],
        a[2] * b[1] + a[3] * b[3],
    )


def wide(s):
    return (s[0], s[1], s[1], s[2])


def turn(a):
    return (a[0], a[2], a[1], a[3])


def apply(a, v):
    return (a[0] * v[0] + a[1] * v[1], a[2] * v[0] + a[3] * v[1])


def add(*items):
    total = items[0]
    for item in items[1:]:
        total = tuple(x + y for x, y in zip(total, item))
    return total


def symmetric(a, *more):
    return add(*((m[0], m[1], m[3]) for m in (a, *more)))


def inverse(s):
    scale = 1.0 / (s[0] * s[2] - s[1] * s[1])
    return (s[2] * scale, -s[1] * scale, s[0] * scale)


def conduct(signed, inside=None):
    dry = jnp.maximum(signed, 0.0)
    moist = HALF * 0.004 + dry * dry * dry
    pore = signed > 0.0
    heat = jnp.where(pore, HALF + (2.0 * HALF / GROW) * signed, 3.0 * HALF)
    cross = jnp.where(pore, CROSS * moist, 0.0)
    if inside is None:
        return (heat, cross, moist)
    return (jnp.where(inside, heat, 0.0), cross, jnp.where(inside, moist, 0.0))


def flux(k, drop):
    return (k[0] * drop[0] + k[1] * drop[1], k[1] * drop[0] + k[2] * drop[1])


def roll(x, shift, axis):
    return pltpu.roll(x, shift % x.shape[axis], axis)


def down(items, shift):
    return tuple(roll(x, shift, 0) for x in items)


def over_chunks(items):
    for shift in (4, 2, 1):
        items = add(items, down(items, shift))
    return items


def lanes():
    return lax.broadcasted_iota(jnp.int32, TILE, 1)


def chunks():
    return lax.broadcasted_iota(jnp.int32, TILE, 0)


def toward_odd():
    parity = lax.rem(lax.axis_index("tile"), 2)
    return (lanes() >= XS) == (parity == 1)


def load(ref, *index):
    return tuple(ref[(*index, j)] for j in range(ref.shape[len(index)]))


def store(ref, index, items):
    for j, item in enumerate(items):
        ref[(*index, j)] = item


def levels():
    stride = 1
    while stride < STEPS:
        yield stride, range(0, STEPS, 2 * stride), range(stride, STEPS, 2 * stride)
        stride *= 2


def rows_of():
    place, at = {}, 0
    for stride, kept, _ in levels():
        for step in kept:
            place[stride, step] = at
            at += 1
    return place


PLACE = rows_of()


def pack_even(kept, turned, even):
    near = toward_odd()
    half = STEPS // 2
    for j in range(3):
        for i in range(half):
            even[j * half + i] = jnp.where(near, turned[j * half + i], kept[j, i])


def signs(mask, sign):
    sign[...] = jnp.where(jnp.broadcast_to(mask[...], TILE) > 0, -GROW, GROW)


def prepare(field, sat, sign, kept, turned, odd):
    near = toward_odd()
    half = STEPS // 2
    rows = [pl.ds(i, CHUNKS, stride=STEPS) for i in range(STEPS)]
    sign = sign[...]
    low, high = [None] * PACK, [None] * PACK
    for i in (*range(half, STEPS), *range(half)):
        for j, x in reversed(list(enumerate((field[0, rows[i], :], field[1, rows[i], :] * (1.0 / SCALE), sat[rows[i], :] * sign)))):
            if i >= half:
                high[(j - 1) * half + i] = roll(x, XS, 1)
            else:
                low[j * half + i] = x
            kept[j, i] = x
    for i in range(PACK):
        odd[i] = jnp.where(near, low[i], high[i])
    for i in range(PACK):
        turned[i] = high[i]


def tile():
    return lax.axis_index("tile")


def line():
    return lax.axis_index("line")


def at_row_end():
    place = lax.rem(lax.axis_index("tile"), ROW)
    return jnp.logical_or(place == 0, place == ROW - 1)


def inner(field_hbm, sat_hbm, mask_hbm, kept, turned, odd, even, fbuf, sbuf, mbuf, gbuf, sems):
    @pl.when(jnp.logical_not(at_row_end()))
    def _():
        copies = [
            pltpu.make_async_copy(field_hbm, fbuf, sems.at[0]),
            pltpu.make_async_copy(sat_hbm, sbuf, sems.at[1]),
            pltpu.make_async_copy(mask_hbm, mbuf, sems.at[2]),
        ]
        for copy in copies:
            copy.start()
        for copy in copies:
            copy.wait()
        signs(mbuf, gbuf)
        prepare(fbuf, sbuf, gbuf, kept, turned, odd)
        pack_even(kept, turned, even)

    @pl.when(jnp.logical_or(tile() == 2, jnp.logical_and(tile() == 1, line() == 1)))
    def _():
        for i in range(PACK):
            odd[i], even[i] = even[i], odd[i]


def ends(field, sat, sign, kept_in, turned_in, odd_in, kept, turned, odd):
    @pl.when(at_row_end())
    def _():
        prepare(field, sat, sign, kept, turned, odd)

    @pl.when(tile() == 0)
    def _():
        pack_even(kept, turned, odd)


def third(kept, turned, arrived, out):
    relay = jnp.logical_and(tile() == 0, line() == 1)

    @pl.when(jnp.logical_not(relay))
    def _():
        pack_even(kept, turned, out)

    @pl.when(relay)
    def _():
        for i in range(PACK):
            out[i] = arrived[i]


def local(kept, turned, one, k_all, rhs, ab, dinv, ring, final, answer, share, own, green, own_green, known):
    first, last = chunks() == 0, chunks() == CHUNKS - 1
    low_line, high_line = line() == 0, line() == 1
    column = lax.rem(lanes(), XS)
    west_end, east_end = column == 0, column == XS - 1
    half = STEPS // 2

    near = toward_odd()
    k = []
    for i in range(STEPS):
        s = kept[2, i]
        ki = conduct(s)
        k.append(ki)
        store(k_all, (i,), ki)
        f = (kept[0, i], kept[1, i])
        if i < half:
            far, far_s = (roll(f[0], XS, 1), roll(f[1], XS, 1)), roll(s, XS, 1)
        else:
            far, far_s = (turned[i - half], turned[i]), turned[i + half]
        far_k = conduct(far_s)
        if i < half:
            store(own, (i,), (*far_k, *far))
        else:
            held = load(own, i - half)
            store(own, (i - half,), tuple(jnp.where(near, x, y) for x, y in zip((*ki, *f), held)))
        total = flux(add(ki, far_k), (far[0] - f[0], far[1] - f[1]))
        west_k = conduct(roll(s, 1, 1))
        west = flux(add(ki, west_k), (roll(f[0], 1, 1) - f[0], roll(f[1], 1, 1) - f[1]))
        edge = flux(ki, f)
        west = tuple(jnp.where(west_end, -e, w) for e, w in zip(edge, west))
        east = tuple(jnp.where(east_end, e, roll(w, -1, 1)) for e, w in zip(edge, west))
        for j in range(2):
            rhs[j, i] = f[j] + (total[j] + (west[j] - east[j]))

    @pl.when(from_first())
    def _():
        for i in range(STEPS):
            pack = [one[j * half + i % half] for j in range(3)]
            far = pack if i >= half else [roll(x, XS, 1) for x in pack]
            total = flux(add(load(k_all, i), conduct(far[2])), (far[0] - kept[0, i], far[1] - kept[1, i]))
            for j in range(2):
                rhs[j, i] = rhs[j, i] + jnp.where(near, 0.0, total[j])

    upper = {i: wide(add(k[i], k[i + 1])) for i in range(STEPS - 1)}
    upper[STEPS - 1] = wide(tuple(jnp.where(last, 0.0, x) for x in add(k[-1], down(k[0], -1))))
    bottom = jnp.logical_and(first, low_line)
    top = jnp.logical_and(last, high_line)
    bottom = tuple(jnp.where(bottom, x, 0.0) for x in k[0])
    top = tuple(jnp.where(top, x, 0.0) for x in k[-1])
    excess = {}

    for stride, keep, drop in levels():
        lower = {}
        for i in (*keep, *drop):
            left = i - stride
            lower[i] = turn(upper[left] if left >= 0 else down(upper[left + STEPS], 1))
        inv = {}
        for i in drop:
            if stride == 1:
                d = symmetric(lower[i], upper[i])
                d = (d[0] + 1.0, d[1], d[2] + 1.0)
                if i == STEPS - 1:
                    d = add(d, top)
            else:
                d = symmetric(excess[i], lower[i], upper[i])
            inv[i] = inverse(d)
            store(dinv, (i,), inv[i])
        for i in keep:
            right, left = i + stride, i - stride
            if left < 0:
                before = wide(down(inv[left + STEPS], 1))
            else:
                before = wide(inv[left])
            a = mul(lower[i], before)
            b = mul(upper[i], wide(inv[right]))
            store(ab, (PLACE[stride, i],), (*a, *b))
            if stride == 1:
                more = add(a, b)
                more = (more[0] + 1.0, more[1], more[2], more[3] + 1.0)
                if i == 0:
                    more = add(more, wide(bottom))
                if right == STEPS - 1:
                    more = add(more, mul(b, wide(top)))
            else:
                prev = excess[left] if left >= 0 else down(excess[left + STEPS], 1)
                more = add(excess[i], mul(a, prev), mul(b, excess[right]))
            excess[i] = more
            upper[i] = mul(b, upper[right])

    start = jnp.where(jnp.logical_and(high_line, first), 1.0, 0.0)
    end = jnp.logical_and(low_line, last)
    one = jnp.where(end, 1.0, 0.0)
    none = jnp.zeros(TILE, jnp.float32)
    source = (one, none, none, one)
    sides = {STEPS - 1: source}
    for stride, keep, _ in levels():
        b = load(ab, PLACE[stride, keep[-1]])[4:8]
        source = tuple(jnp.where(end, x, 0.0) for x in b) if stride == 1 else mul(b, source)
        sides[keep[-1]] = source
    vec = (source[0] + start, source[1], source[2], source[3] + start)

    up, ex = upper[0], excess[0]
    low = turn(down(up, 1))
    shift, place = 1, 0
    while shift < CHUNKS:
        inv = inverse(symmetric(ex, low, up))
        a = mul(low, wide(down(inv, shift)))
        b = mul(up, wide(down(inv, -shift)))
        store(ring, (place,), (*a, *b))
        vec = add(vec, mul(a, down(vec, shift)), mul(b, down(vec, -shift)))
        ex = add(ex, mul(a, down(ex, shift)), mul(b, down(ex, -shift)))
        up = mul(b, down(up, -shift))
        shift *= 2
        place += 1
        low = turn(down(up, shift))
    inv = inverse((ex[0], ex[1], ex[3]))
    store(final, (), inv)
    w = {0: mul(wide(inv), vec)}
    for stride, keep, drop in reversed(list(levels())):
        for i in drop:
            left, right = i - stride, i + stride
            prev = turn(load(ab, PLACE[stride, left])[4:8])
            if right < STEPS:
                after, later = turn(load(ab, PLACE[stride, right])[0:4]), w[right]
            else:
                after, later = turn(down(load(ab, PLACE[stride, 0])[0:4], -1)), down(w[0], -1)
            w[i] = add(mul(prev, w[left]), mul(after, later))
            if i in sides:
                w[i] = add(w[i], mul(wide(load(dinv, i)), sides[i]))
    for i in range(STEPS):
        store(green, (i,), w[i])
        for j, x in enumerate((w[i][0], w[i][1], SCALE * w[i][2], SCALE * w[i][3])):
            answer[j, pl.ds(i, CHUNKS, stride=STEPS), :] = x

    @pl.when(from_first())
    def _():
        total = apply(turn(w[0]), (rhs[0, 0], rhs[1, 0]))
        for i in range(1, STEPS):
            total = add(total, apply(turn(w[i]), (rhs[0, i], rhs[1, i])))
        store(known, (), over_chunks(total))
        for i in range(half):
            store(own_green, (i,), tuple(jnp.where(near, x, roll(y, XS, 1)) for x, y in zip(w[i + half], w[i])))

    tail = down((w[STEPS - 1][0], w[STEPS - 1][1], w[STEPS - 1][3], kept[2, STEPS - 1]), 1)
    head = (w[0][0], w[0][1], w[0][3], kept[2, 0])
    for j, (x, y) in enumerate(zip(head, tail)):
        share[pl.ds(2 + j, 1), :] = jnp.where(low_line, y, x)[0:1]
    share[pl.ds(0, 2), :] = none[0:2]
    share[pl.ds(6, 2), :] = none[0:2]


def from_first():
    return jnp.logical_and(tile() >= ROW, lax.rem(tile(), ROW) == 0)


def finish(k_all, rhs, kept, own, ab, dinv, ring, final, share, green, own_green, known, one, two, three, local_x, message, pending):
    half = STEPS // 2
    at, high = tile(), line() == 1
    near = toward_odd()
    rest = (ab, dinv, ring, final, share, green, local_x, message, pending)

    @pl.when(from_first())
    def _():
        through = []
        for i in range(half):
            mine = load(own, i)
            drop = (two[i] - mine[3], two[half + i] - mine[4])
            through.append(flux(add(mine[:3], conduct(two[2 * half + i])), drop))

        @pl.when(line() == 0)
        def _():
            parts = [apply(turn(load(own_green, i)), through[i]) for i in range(half)]
            while len(parts) > 1:
                parts = [add(x, y) for x, y in zip(parts[::2], parts[1::2])]
            d = over_chunks(parts[0])
            message[...] = share[...]
            for j in range(2):
                x = known[j] + jnp.where(near, d[j] + roll(d[j], XS, 1), 0.0)
                message[pl.ds(j, 1), :] = x[0:1]
            for i in range(half):
                store(pending, (i,), through[i])

        @pl.when(line() == 1)
        def _():
            b = {}
            for i in range(half):
                b[i + half] = tuple(rhs[j, i + half] + jnp.where(near, through[i][j], 0.0) for j in range(2))
                b[i] = tuple(rhs[j, i] + jnp.where(near, roll(through[i][j], XS, 1), 0.0) for j in range(2))
            conclude(b, *rest)

    def both(halo):
        alone = jnp.logical_or(at == 0, at == lax.axis_size("tile") - 1)
        inside = jnp.logical_not(jnp.logical_and(near, alone))
        far = {}
        for j in range(3):
            for i in range(half):
                o, e = halo(j * half + i)
                far[j, i] = roll(jnp.where(near, e, o), XS, 1)
                far[j, i + half] = jnp.where(near, o, e)
        b = {}
        for i in range(STEPS):
            drop = (far[0, i] - kept[0, i], far[1, i] - kept[1, i])
            total = flux(add(load(k_all, i), conduct(far[2, i], inside)), drop)
            b[i] = (rhs[0, i] + total[0], rhs[1, i] + total[1])
        conclude(b, *rest)

    @pl.when(jnp.logical_and(at >= ROW, jnp.logical_not(from_first())))
    def _():
        both(lambda i: (two[i], three[i]))

    @pl.when(at < ROW)
    def _():
        def halo(i):
            odd = jnp.where(at == 1, one[i], two[i])
            odd = jnp.where(jnp.logical_and(high, at == 2), one[i], odd)
            odd = jnp.where(jnp.logical_and(high, at == 0), three[i], odd)
            even = jnp.where(jnp.logical_or(at == 1, jnp.logical_and(high, at == 0)), two[i], three[i])
            return odd, even

        both(halo)


def conclude(b, ab, dinv, ring, final, share, green, local_x, message, pending):
    message[...] = share[...]

    @pl.when(line() == 0)
    def _():
        parts = []
        for i in range(STEPS):
            w = load(green, i)
            parts.append((w[0] * b[i][0] + w[2] * b[i][1], w[1] * b[i][0] + w[3] * b[i][1]))
            store(pending, (i,), b[i])
        while len(parts) > 1:
            parts = [add(x, y) for x, y in zip(parts[::2], parts[1::2])]
        d = over_chunks(parts[0])
        for j in range(2):
            message[pl.ds(j, 1), :] = d[j][0:1]

    @pl.when(line() == 1)
    def _():
        x = solve(b, ab, dinv, ring, final)
        for j in range(2):
            message[pl.ds(j, 1), :] = x[0][j][0:1]
        for i in range(STEPS):
            here = pl.ds(i, CHUNKS, stride=STEPS)
            local_x[0, here, :] = x[i][0]
            local_x[1, here, :] = SCALE * x[i][1]


def solve(b, ab, dinv, ring, final):
    b = dict(b)
    for stride, keep, drop in levels():
        for i in keep:
            left = i - stride
            prev = b[left] if left >= 0 else down(b[left + STEPS], 1)
            c = load(ab, PLACE[stride, i])
            b[i] = add(b[i], apply(c[0:4], prev), apply(c[4:8], b[i + stride]))
    vec = b[0]
    shift, place = 1, 0
    while shift < CHUNKS:
        c = load(ring, place)
        vec = add(vec, apply(c[0:4], down(vec, shift)), apply(c[4:8], down(vec, -shift)))
        shift *= 2
        place += 1
    x = {0: apply(wide(load(final)), vec)}
    for stride, keep, drop in reversed(list(levels())):
        for i in drop:
            left, right = i - stride, i + stride
            prev = turn(load(ab, PLACE[stride, left])[4:8])
            if right < STEPS:
                after, later = turn(load(ab, PLACE[stride, right])[0:4]), x[right]
            else:
                after, later = turn(down(load(ab, PLACE[stride, 0])[0:4], -1)), down(x[0], -1)
            x[i] = add(apply(wide(load(dinv, i)), b[i]), apply(prev, x[left]), apply(after, later))
    return x


def join(local_x, answer, both, rhs, pending, ab, dinv, ring, final, out_hbm, out, sems):
    def row(who, j):
        return jnp.broadcast_to(both[who, pl.ds(j, 1), :], TILE)

    sign = jnp.where(line() == 0, 1.0, -1.0)
    drop = tuple(sign * (row(1, j) - row(0, j)) for j in range(2))
    reach = wide(tuple(row(0, 2 + j) + row(1, 2 + j) for j in range(3)))
    face = add(conduct(row(0, 5)), conduct(row(1, 5)))
    m = mul(wide(face), reach)
    m = (m[0] + 1.0, m[1], m[2], m[3] + 1.0)
    push = flux(face, drop)
    scale = 1.0 / (m[0] * m[3] - m[1] * m[2])
    through = ((m[3] * push[0] - m[1] * push[1]) * scale, (m[0] * push[1] - m[2] * push[0]) * scale)

    copies = [pltpu.make_async_copy(out.at[j], out_hbm.at[j], sems.at[j]) for j in range(2)]

    @pl.when(line() == 0)
    def _():
        half = STEPS // 2
        near = toward_odd()
        packed = from_first()
        b = {}
        for i in range(half):
            low, high = load(pending, i), load(pending, i + half)
            for step, left, flow in ((i, low, tuple(roll(x, XS, 1) for x in low)), (i + half, high, low)):
                b[step] = tuple(
                    jnp.where(packed, rhs[j, step] + jnp.where(near, flow[j], 0.0), left[j]) for j in range(2)
                )
        last = chunks() == CHUNKS - 1
        b[STEPS - 1] = add(b[STEPS - 1], tuple(jnp.where(last, x, 0.0) for x in through))
        x = solve(b, ab, dinv, ring, final)
        for i in range(STEPS):
            here = pl.ds(i, CHUNKS, stride=STEPS)
            out[0, here, :] = x[i][0]
            out[1, here, :] = SCALE * x[i][1]
        whole = pltpu.make_async_copy(out, out_hbm, sems.at[0])
        whole.start()
        whole.wait()

    @pl.when(line() == 1)
    def _():
        for j in range(2):
            for i in range(STEPS):
                here = pl.ds(i * CHUNKS, CHUNKS)
                change = answer[2 * j, here, :] * through[0] + answer[2 * j + 1, here, :] * through[1]
                out[j, here, :] = local_x[j, here, :] + change
            copies[j].start()
        for copy in copies:
            copy.wait()


def tiles(*lead):
    return jax.ShapeDtypeStruct((*lead, *TILE), jnp.float32)


def call(kernel, outs, args, name, flops, **more):
    vmem = pl.BlockSpec(memory_space=pltpu.VMEM)
    more.setdefault("in_specs", [vmem] * len(args))
    if "out_specs" not in more:
        more["out_specs"] = [vmem] * len(outs)
    return pl.pallas_call(
        kernel,
        out_shape=outs,
        compiler_params=pltpu.CompilerParams(vmem_limit_bytes=LIMIT),
        cost_estimate=pl.CostEstimate(flops=flops, bytes_accessed=1 << 20, transcendentals=0),
        name=name,
        **more,
    )(*args)


def moves(count):
    ops = [[], [], []]
    for base in (0, count):
        for t in range(base, base + count, ROW):
            ops[2] += [(t + 2, t + 3), (t + 3, t + 2)]
            if t > base:
                ops[0].append((t + 1, t))
                ops[1] += [(t - 1, t), (t, t - 1), (t + 1, t + 2), (t + 2, t + 1)]
                ops[2].append((t, t + 1))
    ops[0] += [(1, count), (2, 1), (count + 1, count + 2), (count + 2, count + 1)]
    ops[1] += [(0, 1), (1, 2), (count, count + 1), (count + 1, count)]
    ops[2].append((count, 0))
    return ops


def body(field, saturation, solid_mask):
    ops = moves(lax.axis_size("tile"))
    both_axes = ("line", "tile")
    cells = STEPS * CHUNKS
    in_hbm = [pltpu.with_memory_space_constraint(x, pltpu.HBM) for x in (field, saturation, solid_mask)]
    kept, turned, two, one = call(
        inner,
        [tiles(3, STEPS), tiles(PACK), tiles(PACK), tiles(PACK)],
        in_hbm,
        "inner",
        1 << 16,
        in_specs=[pl.BlockSpec(memory_space=pltpu.HBM)] * 3,
        scratch_shapes=[
            pltpu.VMEM((2, cells, LANES), jnp.float32),
            pltpu.VMEM((cells, LANES), jnp.float32),
            pltpu.VMEM((1, LANES), jnp.int32),
            pltpu.VMEM(TILE, jnp.float32),
            pltpu.SemaphoreType.DMA((3,)),
        ],
    )
    from_one = lax.ppermute(one, both_axes, ops[0])
    (sign,) = call(signs, [tiles()], (solid_mask,), "signs", 1 << 8)
    kept, turned, two = call(
        ends,
        [tiles(3, STEPS), tiles(PACK), tiles(PACK)],
        (field, saturation, sign, kept, turned, two),
        "ends",
        1 << 16,
        input_output_aliases={3: 0, 4: 1, 5: 2},
    )
    from_two = lax.ppermute(two, both_axes, ops[1])
    (three,) = call(third, [tiles(PACK)], (kept, turned, from_one), "third", 1 << 12)
    from_three = lax.ppermute(three, both_axes, ops[2])
    k_all, rhs, ab, dinv, ring, final, answer, share, own, green, own_green, known = call(
        local,
        [
            tiles(STEPS, 3),
            tiles(2, STEPS),
            tiles(STEPS - 1, 8),
            tiles(STEPS, 3),
            tiles(3, 8),
            tiles(3),
            jax.ShapeDtypeStruct((4, cells, LANES), jnp.float32),
            jax.ShapeDtypeStruct((8, LANES), jnp.float32),
            tiles(STEPS // 2, 5),
            tiles(STEPS, 4),
            tiles(STEPS // 2, 4),
            tiles(2),
        ],
        (kept, turned, from_one),
        "local",
        1 << 23,
    )
    local_x, message, pending = call(
        finish,
        [jax.ShapeDtypeStruct((2, cells, LANES), jnp.float32), jax.ShapeDtypeStruct((8, LANES), jnp.float32), tiles(STEPS, 2)],
        (k_all, rhs, kept, own, ab, dinv, ring, final, share, green, own_green, known, from_one, from_two, from_three),
        "finish",
        1 << 21,
    )
    both = lax.all_gather(message, "line", axis=0)
    return call(
        join,
        jax.ShapeDtypeStruct((2, cells, LANES), jnp.float32),
        (local_x, answer, both, rhs, pending, ab, dinv, ring, final),
        "join",
        1 << 18,
        out_specs=pl.BlockSpec(memory_space=pltpu.HBM),
        scratch_shapes=[pltpu.VMEM((2, cells, LANES), jnp.float32), pltpu.SemaphoreType.DMA((2,))],
    )


def solution(mesh):
    in_specs = (P(None, "line", "tile"), P("line", "tile"), P("line", "tile"))
    out_specs = P(None, "line", "tile")
    return jax.shard_map(body, mesh=mesh, in_specs=in_specs, out_specs=out_specs, check_vma=False)
```

```python
import jax
import jax.numpy as jnp
from jax import lax
from jax.experimental import pallas as pl
from jax.experimental.pallas import tpu as pltpu
from jax.sharding import PartitionSpec as P

XS = 64
ZSTIFF = 2048
HALF = 0.5 * ZSTIFF
STEPS = 16
CHUNKS = 8
LANES = 128
TILE = (CHUNKS, LANES)
ROW = 4
SCALE = 0.4**0.5
CROSS = 0.1**0.5
GROW = HALF ** (1.0 / 3.0)
PACK = STEPS + STEPS // 2
LIMIT = 12 * 1024 * 1024


def mul(a, b):
    return (
        a[0] * b[0] + a[1] * b[2],
        a[0] * b[1] + a[1] * b[3],
        a[2] * b[0] + a[3] * b[2],
        a[2] * b[1] + a[3] * b[3],
    )


def wide(s):
    return (s[0], s[1], s[1], s[2])


def turn(a):
    return (a[0], a[2], a[1], a[3])


def apply(a, v):
    return (a[0] * v[0] + a[1] * v[1], a[2] * v[0] + a[3] * v[1])


def add(*items):
    total = items[0]
    for item in items[1:]:
        total = tuple(x + y for x, y in zip(total, item))
    return total


def symmetric(a, *more):
    return add(*((m[0], m[1], m[3]) for m in (a, *more)))


def inverse(s):
    scale = 1.0 / (s[0] * s[2] - s[1] * s[1])
    return (s[2] * scale, -s[1] * scale, s[0] * scale)


def conduct(signed, inside=None):
    dry = jnp.maximum(signed, 0.0)
    moist = HALF * 0.004 + dry * dry * dry
    pore = signed > 0.0
    heat = jnp.where(pore, HALF + (2.0 * HALF / GROW) * signed, 3.0 * HALF)
    cross = jnp.where(pore, CROSS * moist, 0.0)
    if inside is None:
        return (heat, cross, moist)
    return (jnp.where(inside, heat, 0.0), cross, jnp.where(inside, moist, 0.0))


def flux(k, drop):
    return (k[0] * drop[0] + k[1] * drop[1], k[1] * drop[0] + k[2] * drop[1])


def roll(x, shift, axis):
    return pltpu.roll(x, shift % x.shape[axis], axis)


def down(items, shift):
    return tuple(roll(x, shift, 0) for x in items)


def over_chunks(items):
    for shift in (4, 2, 1):
        items = add(items, down(items, shift))
    return items


def lanes():
    return lax.broadcasted_iota(jnp.int32, TILE, 1)


def chunks():
    return lax.broadcasted_iota(jnp.int32, TILE, 0)


def toward_odd():
    parity = lax.rem(lax.axis_index("tile"), 2)
    return (lanes() >= XS) == (parity == 1)


def load(ref, *index):
    return tuple(ref[(*index, j)] for j in range(ref.shape[len(index)]))


def store(ref, index, items):
    for j, item in enumerate(items):
        ref[(*index, j)] = item


def levels():
    stride = 1
    while stride < STEPS:
        yield stride, range(0, STEPS, 2 * stride), range(stride, STEPS, 2 * stride)
        stride *= 2


def rows_of():
    place, at = {}, 0
    for stride, kept, _ in levels():
        for step in kept:
            place[stride, step] = at
            at += 1
    return place


PLACE = rows_of()


def pack_even(kept, turned, even):
    near = toward_odd()
    half = STEPS // 2
    for j in range(3):
        for i in range(half):
            even[j * half + i] = jnp.where(near, turned[j * half + i], kept[j, i])


def signs(mask, sign):
    sign[...] = jnp.where(jnp.broadcast_to(mask[...], TILE) > 0, -GROW, GROW)


def prepare(field, sat, sign, kept, turned, odd):
    near = toward_odd()
    half = STEPS // 2
    rows = [pl.ds(i, CHUNKS, stride=STEPS) for i in range(STEPS)]
    sign = sign[...]
    low, high = [None] * PACK, [None] * PACK
    for i in (*range(half, STEPS), *range(half)):
        for j, x in reversed(list(enumerate((field[0, rows[i], :], field[1, rows[i], :] * (1.0 / SCALE), sat[rows[i], :] * sign)))):
            if i >= half:
                high[(j - 1) * half + i] = roll(x, XS, 1)
            else:
                low[j * half + i] = x
            kept[j, i] = x
    for i in range(PACK):
        odd[i] = jnp.where(near, low[i], high[i])
    for i in range(PACK):
        turned[i] = high[i]


def tile():
    return lax.axis_index("tile")


def line():
    return lax.axis_index("line")


def at_row_end():
    place = lax.rem(lax.axis_index("tile"), ROW)
    return jnp.logical_or(place == 0, place == ROW - 1)


def inner(field_hbm, sat_hbm, mask_hbm, kept, turned, odd, even, fbuf, sbuf, mbuf, gbuf, sems):
    @pl.when(jnp.logical_not(at_row_end()))
    def _():
        copies = [
            pltpu.make_async_copy(field_hbm, fbuf, sems.at[0]),
            pltpu.make_async_copy(sat_hbm, sbuf, sems.at[1]),
            pltpu.make_async_copy(mask_hbm, mbuf, sems.at[2]),
        ]
        for copy in copies:
            copy.start()
        for copy in copies:
            copy.wait()
        signs(mbuf, gbuf)
        prepare(fbuf, sbuf, gbuf, kept, turned, odd)
        pack_even(kept, turned, even)

    @pl.when(jnp.logical_or(tile() == 2, jnp.logical_and(tile() == 1, line() == 1)))
    def _():
        for i in range(PACK):
            odd[i], even[i] = even[i], odd[i]


def ends(field, sat, sign, kept_in, turned_in, odd_in, kept, turned, odd):
    @pl.when(at_row_end())
    def _():
        prepare(field, sat, sign, kept, turned, odd)

    @pl.when(tile() == 0)
    def _():
        pack_even(kept, turned, odd)


def third(kept, turned, arrived, out):
    relay = jnp.logical_and(tile() == 0, line() == 1)

    @pl.when(jnp.logical_not(relay))
    def _():
        pack_even(kept, turned, out)

    @pl.when(relay)
    def _():
        for i in range(PACK):
            out[i] = arrived[i]


def local(kept, turned, one, k_all, rhs, ab, dinv, ring, final, answer, share, own, green, own_green, known):
    first, last = chunks() == 0, chunks() == CHUNKS - 1
    low_line, high_line = line() == 0, line() == 1
    column = lax.rem(lanes(), XS)
    west_end, east_end = column == 0, column == XS - 1
    half = STEPS // 2

    near = toward_odd()
    k = []
    for i in range(STEPS):
        s = kept[2, i]
        ki = conduct(s)
        k.append(ki)
        store(k_all, (i,), ki)
        f = (kept[0, i], kept[1, i])
        if i < half:
            far, far_s = (roll(f[0], XS, 1), roll(f[1], XS, 1)), roll(s, XS, 1)
        else:
            far, far_s = (turned[i - half], turned[i]), turned[i + half]
        far_k = conduct(far_s)
        if i < half:
            store(own, (i,), (*far_k, *far))
        else:
            held = load(own, i - half)
            store(own, (i - half,), tuple(jnp.where(near, x, y) for x, y in zip((*ki, *f), held)))
        total = flux(add(ki, far_k), (far[0] - f[0], far[1] - f[1]))
        west_k = conduct(roll(s, 1, 1))
        west = flux(add(ki, west_k), (roll(f[0], 1, 1) - f[0], roll(f[1], 1, 1) - f[1]))
        edge = flux(ki, f)
        west = tuple(jnp.where(west_end, -e, w) for e, w in zip(edge, west))
        east = tuple(jnp.where(east_end, e, roll(w, -1, 1)) for e, w in zip(edge, west))
        for j in range(2):
            rhs[j, i] = f[j] + (total[j] + (west[j] - east[j]))

    @pl.when(from_first())
    def _():
        for i in range(STEPS):
            pack = [one[j * half + i % half] for j in range(3)]
            far = pack if i >= half else [roll(x, XS, 1) for x in pack]
            total = flux(add(load(k_all, i), conduct(far[2])), (far[0] - kept[0, i], far[1] - kept[1, i]))
            for j in range(2):
                rhs[j, i] = rhs[j, i] + jnp.where(near, 0.0, total[j])

    upper = {i: wide(add(k[i], k[i + 1])) for i in range(STEPS - 1)}
    upper[STEPS - 1] = wide(tuple(jnp.where(last, 0.0, x) for x in add(k[-1], down(k[0], -1))))
    bottom = jnp.logical_and(first, low_line)
    top = jnp.logical_and(last, high_line)
    bottom = tuple(jnp.where(bottom, x, 0.0) for x in k[0])
    top = tuple(jnp.where(top, x, 0.0) for x in k[-1])
    excess = {}

    for stride, keep, drop in levels():
        lower = {}
        for i in (*keep, *drop):
            left = i - stride
            lower[i] = turn(upper[left] if left >= 0 else down(upper[left + STEPS], 1))
        inv = {}
        for i in drop:
            if stride == 1:
                d = symmetric(lower[i], upper[i])
                d = (d[0] + 1.0, d[1], d[2] + 1.0)
                if i == STEPS - 1:
                    d = add(d, top)
            else:
                d = symmetric(excess[i], lower[i], upper[i])
            inv[i] = inverse(d)
            store(dinv, (i,), inv[i])
        for i in keep:
            right, left = i + stride, i - stride
            if left < 0:
                before = wide(down(inv[left + STEPS], 1))
            else:
                before = wide(inv[left])
            a = mul(lower[i], before)
            b = mul(upper[i], wide(inv[right]))
            store(ab, (PLACE[stride, i],), (*a, *b))
            if stride == 1:
                more = add(a, b)
                more = (more[0] + 1.0, more[1], more[2], more[3] + 1.0)
                if i == 0:
                    more = add(more, wide(bottom))
                if right == STEPS - 1:
                    more = add(more, mul(b, wide(top)))
            else:
                prev = excess[left] if left >= 0 else down(excess[left + STEPS], 1)
                more = add(excess[i], mul(a, prev), mul(b, excess[right]))
            excess[i] = more
            upper[i] = mul(b, upper[right])

    start = jnp.where(jnp.logical_and(high_line, first), 1.0, 0.0)
    end = jnp.logical_and(low_line, last)
    one = jnp.where(end, 1.0, 0.0)
    none = jnp.zeros(TILE, jnp.float32)
    source = (one, none, none, one)
    sides = {STEPS - 1: source}
    for stride, keep, _ in levels():
        b = load(ab, PLACE[stride, keep[-1]])[4:8]
        source = tuple(jnp.where(end, x, 0.0) for x in b) if stride == 1 else mul(b, source)
        sides[keep[-1]] = source
    vec = (source[0] + start, source[1], source[2], source[3] + start)

    up, ex = upper[0], excess[0]
    low = turn(down(up, 1))
    shift, place = 1, 0
    while shift < CHUNKS:
        inv = inverse(symmetric(ex, low, up))
        a = mul(low, wide(down(inv, shift)))
        b = mul(up, wide(down(inv, -shift)))
        store(ring, (place,), (*a, *b))
        vec = add(vec, mul(a, down(vec, shift)), mul(b, down(vec, -shift)))
        ex = add(ex, mul(a, down(ex, shift)), mul(b, down(ex, -shift)))
        up = mul(b, down(up, -shift))
        shift *= 2
        place += 1
        low = turn(down(up, shift))
    inv = inverse((ex[0], ex[1], ex[3]))
    store(final, (), inv)
    w = {0: mul(wide(inv), vec)}
    for stride, keep, drop in reversed(list(levels())):
        for i in drop:
            left, right = i - stride, i + stride
            prev = turn(load(ab, PLACE[stride, left])[4:8])
            if right < STEPS:
                after, later = turn(load(ab, PLACE[stride, right])[0:4]), w[right]
            else:
                after, later = turn(down(load(ab, PLACE[stride, 0])[0:4], -1)), down(w[0], -1)
            w[i] = add(mul(prev, w[left]), mul(after, later))
            if i in sides:
                w[i] = add(w[i], mul(wide(load(dinv, i)), sides[i]))
    for i in range(STEPS):
        store(green, (i,), w[i])
        for j, x in enumerate((w[i][0], w[i][1], SCALE * w[i][2], SCALE * w[i][3])):
            answer[j, pl.ds(i, CHUNKS, stride=STEPS), :] = x

    @pl.when(from_first())
    def _():
        total = apply(turn(w[0]), (rhs[0, 0], rhs[1, 0]))
        for i in range(1, STEPS):
            total = add(total, apply(turn(w[i]), (rhs[0, i], rhs[1, i])))
        store(known, (), over_chunks(total))
        for i in range(half):
            store(own_green, (i,), tuple(jnp.where(near, x, roll(y, XS, 1)) for x, y in zip(w[i + half], w[i])))

    tail = down((w[STEPS - 1][0], w[STEPS - 1][1], w[STEPS - 1][3], kept[2, STEPS - 1]), 1)
    head = (w[0][0], w[0][1], w[0][3], kept[2, 0])
    for j, (x, y) in enumerate(zip(head, tail)):
        share[pl.ds(2 + j, 1), :] = jnp.where(low_line, y, x)[0:1]
    share[pl.ds(0, 2), :] = none[0:2]
    share[pl.ds(6, 2), :] = none[0:2]


def from_first():
    return jnp.logical_and(tile() >= ROW, lax.rem(tile(), ROW) == 0)


def finish(k_all, rhs, kept, own, ab, dinv, ring, final, share, green, own_green, known, one, two, three, local_x, message, pending):
    half = STEPS // 2
    at, high = tile(), line() == 1
    near = toward_odd()
    rest = (ab, dinv, ring, final, share, green, local_x, message, pending)

    @pl.when(from_first())
    def _():
        through = []
        for i in range(half):
            mine = load(own, i)
            drop = (two[i] - mine[3], two[half + i] - mine[4])
            through.append(flux(add(mine[:3], conduct(two[2 * half + i])), drop))

        @pl.when(line() == 0)
        def _():
            message[...] = share[...]
            for i in range(half):
                store(pending, (i,), through[i])
            parts = [apply(turn(load(own_green, i)), through[i]) for i in range(half)]
            while len(parts) > 1:
                parts = [add(x, y) for x, y in zip(parts[::2], parts[1::2])]
            d = over_chunks(parts[0])
            for j in range(2):
                x = known[j] + jnp.where(near, d[j] + roll(d[j], XS, 1), 0.0)
                message[pl.ds(j, 1), :] = x[0:1]

        @pl.when(line() == 1)
        def _():
            b = {}
            for i in range(half):
                b[i + half] = tuple(rhs[j, i + half] + jnp.where(near, through[i][j], 0.0) for j in range(2))
                b[i] = tuple(rhs[j, i] + jnp.where(near, roll(through[i][j], XS, 1), 0.0) for j in range(2))
            conclude(b, *rest)

    def both(halo):
        alone = jnp.logical_or(at == 0, at == lax.axis_size("tile") - 1)
        inside = jnp.logical_not(jnp.logical_and(near, alone))
        far = {}
        for j in range(3):
            for i in range(half):
                o, e = halo(j * half + i)
                far[j, i] = roll(jnp.where(near, e, o), XS, 1)
                far[j, i + half] = jnp.where(near, o, e)
        b = {}
        for i in range(STEPS):
            drop = (far[0, i] - kept[0, i], far[1, i] - kept[1, i])
            total = flux(add(load(k_all, i), conduct(far[2, i], inside)), drop)
            b[i] = (rhs[0, i] + total[0], rhs[1, i] + total[1])
        conclude(b, *rest)

    @pl.when(jnp.logical_and(at >= ROW, jnp.logical_not(from_first())))
    def _():
        both(lambda i: (two[i], three[i]))

    @pl.when(at < ROW)
    def _():
        def halo(i):
            odd = jnp.where(at == 1, one[i], two[i])
            odd = jnp.where(jnp.logical_and(high, at == 2), one[i], odd)
            odd = jnp.where(jnp.logical_and(high, at == 0), three[i], odd)
            even = jnp.where(jnp.logical_or(at == 1, jnp.logical_and(high, at == 0)), two[i], three[i])
            return odd, even

        both(halo)


def conclude(b, ab, dinv, ring, final, share, green, local_x, message, pending):
    message[...] = share[...]

    @pl.when(line() == 0)
    def _():
        parts = []
        for i in range(STEPS):
            w = load(green, i)
            parts.append((w[0] * b[i][0] + w[2] * b[i][1], w[1] * b[i][0] + w[3] * b[i][1]))
            store(pending, (i,), b[i])
        while len(parts) > 1:
            parts = [add(x, y) for x, y in zip(parts[::2], parts[1::2])]
        d = over_chunks(parts[0])
        for j in range(2):
            message[pl.ds(j, 1), :] = d[j][0:1]

    @pl.when(line() == 1)
    def _():
        x = solve(b, ab, dinv, ring, final)
        for j in range(2):
            message[pl.ds(j, 1), :] = x[0][j][0:1]
        for i in range(STEPS):
            here = pl.ds(i, CHUNKS, stride=STEPS)
            local_x[0, here, :] = x[i][0]
            local_x[1, here, :] = SCALE * x[i][1]


def solve(b, ab, dinv, ring, final):
    b = dict(b)
    for stride, keep, drop in levels():
        for i in keep:
            left = i - stride
            prev = b[left] if left >= 0 else down(b[left + STEPS], 1)
            c = load(ab, PLACE[stride, i])
            b[i] = add(b[i], apply(c[0:4], prev), apply(c[4:8], b[i + stride]))
    vec = b[0]
    shift, place = 1, 0
    while shift < CHUNKS:
        c = load(ring, place)
        vec = add(vec, apply(c[0:4], down(vec, shift)), apply(c[4:8], down(vec, -shift)))
        shift *= 2
        place += 1
    x = {0: apply(wide(load(final)), vec)}
    for stride, keep, drop in reversed(list(levels())):
        for i in drop:
            left, right = i - stride, i + stride
            prev = turn(load(ab, PLACE[stride, left])[4:8])
            if right < STEPS:
                after, later = turn(load(ab, PLACE[stride, right])[0:4]), x[right]
            else:
                after, later = turn(down(load(ab, PLACE[stride, 0])[0:4], -1)), down(x[0], -1)
            x[i] = add(apply(wide(load(dinv, i)), b[i]), apply(prev, x[left]), apply(after, later))
    return x


def join(local_x, answer, both, rhs, pending, ab, dinv, ring, final, out_hbm, out, sems):
    def row(who, j):
        return jnp.broadcast_to(both[who, pl.ds(j, 1), :], TILE)

    sign = jnp.where(line() == 0, 1.0, -1.0)
    drop = tuple(sign * (row(1, j) - row(0, j)) for j in range(2))
    reach = wide(tuple(row(0, 2 + j) + row(1, 2 + j) for j in range(3)))
    face = add(conduct(row(0, 5)), conduct(row(1, 5)))
    m = mul(wide(face), reach)
    m = (m[0] + 1.0, m[1], m[2], m[3] + 1.0)
    push = flux(face, drop)
    scale = 1.0 / (m[0] * m[3] - m[1] * m[2])
    through = ((m[3] * push[0] - m[1] * push[1]) * scale, (m[0] * push[1] - m[2] * push[0]) * scale)

    copies = [pltpu.make_async_copy(out.at[j], out_hbm.at[j], sems.at[j]) for j in range(2)]

    @pl.when(line() == 0)
    def _():
        half = STEPS // 2
        near = toward_odd()
        packed = from_first()
        b = {}
        for i in range(half):
            low, high = load(pending, i), load(pending, i + half)
            for step, left, flow in ((i, low, tuple(roll(x, XS, 1) for x in low)), (i + half, high, low)):
                b[step] = tuple(
                    jnp.where(packed, rhs[j, step] + jnp.where(near, flow[j], 0.0), left[j]) for j in range(2)
                )
        last = chunks() == CHUNKS - 1
        b[STEPS - 1] = add(b[STEPS - 1], tuple(jnp.where(last, x, 0.0) for x in through))
        x = solve(b, ab, dinv, ring, final)
        for i in range(STEPS):
            here = pl.ds(i, CHUNKS, stride=STEPS)
            out[0, here, :] = x[i][0]
            out[1, here, :] = SCALE * x[i][1]
        whole = pltpu.make_async_copy(out, out_hbm, sems.at[0])
        whole.start()
        whole.wait()

    @pl.when(line() == 1)
    def _():
        for j in range(2):
            for i in range(STEPS):
                here = pl.ds(i * CHUNKS, CHUNKS)
                change = answer[2 * j, here, :] * through[0] + answer[2 * j + 1, here, :] * through[1]
                out[j, here, :] = local_x[j, here, :] + change
            copies[j].start()
        for copy in copies:
            copy.wait()


def tiles(*lead):
    return jax.ShapeDtypeStruct((*lead, *TILE), jnp.float32)


def call(kernel, outs, args, name, flops, **more):
    vmem = pl.BlockSpec(memory_space=pltpu.VMEM)
    more.setdefault("in_specs", [vmem] * len(args))
    if "out_specs" not in more:
        more["out_specs"] = [vmem] * len(outs)
    return pl.pallas_call(
        kernel,
        out_shape=outs,
        compiler_params=pltpu.CompilerParams(vmem_limit_bytes=LIMIT),
        cost_estimate=pl.CostEstimate(flops=flops, bytes_accessed=1 << 20, transcendentals=0),
        name=name,
        **more,
    )(*args)


def moves(count):
    ops = [[], [], []]
    for base in (0, count):
        for t in range(base, base + count, ROW):
            ops[2] += [(t + 2, t + 3), (t + 3, t + 2)]
            if t > base:
                ops[0].append((t + 1, t))
                ops[1] += [(t - 1, t), (t, t - 1), (t + 1, t + 2), (t + 2, t + 1)]
                ops[2].append((t, t + 1))
    ops[0] += [(1, count), (2, 1), (count + 1, count + 2), (count + 2, count + 1)]
    ops[1] += [(0, 1), (1, 2), (count, count + 1), (count + 1, count)]
    ops[2].append((count, 0))
    return ops


def body(field, saturation, solid_mask):
    ops = moves(lax.axis_size("tile"))
    both_axes = ("line", "tile")
    cells = STEPS * CHUNKS
    in_hbm = [pltpu.with_memory_space_constraint(x, pltpu.HBM) for x in (field, saturation, solid_mask)]
    kept, turned, two, one = call(
        inner,
        [tiles(3, STEPS), tiles(PACK), tiles(PACK), tiles(PACK)],
        in_hbm,
        "inner",
        1 << 16,
        in_specs=[pl.BlockSpec(memory_space=pltpu.HBM)] * 3,
        scratch_shapes=[
            pltpu.VMEM((2, cells, LANES), jnp.float32),
            pltpu.VMEM((cells, LANES), jnp.float32),
            pltpu.VMEM((1, LANES), jnp.int32),
            pltpu.VMEM(TILE, jnp.float32),
            pltpu.SemaphoreType.DMA((3,)),
        ],
    )
    from_one = lax.ppermute(one, both_axes, ops[0])
    (sign,) = call(signs, [tiles()], (solid_mask,), "signs", 1 << 8)
    kept, turned, two = call(
        ends,
        [tiles(3, STEPS), tiles(PACK), tiles(PACK)],
        (field, saturation, sign, kept, turned, two),
        "ends",
        1 << 16,
        input_output_aliases={3: 0, 4: 1, 5: 2},
    )
    from_two = lax.ppermute(two, both_axes, ops[1])
    (three,) = call(third, [tiles(PACK)], (kept, turned, from_one), "third", 1 << 12)
    from_three = lax.ppermute(three, both_axes, ops[2])
    k_all, rhs, ab, dinv, ring, final, answer, share, own, green, own_green, known = call(
        local,
        [
            tiles(STEPS, 3),
            tiles(2, STEPS),
            tiles(STEPS - 1, 8),
            tiles(STEPS, 3),
            tiles(3, 8),
            tiles(3),
            jax.ShapeDtypeStruct((4, cells, LANES), jnp.float32),
            jax.ShapeDtypeStruct((8, LANES), jnp.float32),
            tiles(STEPS // 2, 5),
            tiles(STEPS, 4),
            tiles(STEPS // 2, 4),
            tiles(2),
        ],
        (kept, turned, from_one),
        "local",
        1 << 23,
    )
    local_x, message, pending = call(
        finish,
        [jax.ShapeDtypeStruct((2, cells, LANES), jnp.float32), jax.ShapeDtypeStruct((8, LANES), jnp.float32), tiles(STEPS, 2)],
        (k_all, rhs, kept, own, ab, dinv, ring, final, share, green, own_green, known, from_one, from_two, from_three),
        "finish",
        1 << 21,
    )
    both = lax.all_gather(message, "line", axis=0)
    return call(
        join,
        jax.ShapeDtypeStruct((2, cells, LANES), jnp.float32),
        (local_x, answer, both, rhs, pending, ab, dinv, ring, final),
        "join",
        1 << 18,
        out_specs=pl.BlockSpec(memory_space=pltpu.HBM),
        scratch_shapes=[pltpu.VMEM((2, cells, LANES), jnp.float32), pltpu.SemaphoreType.DMA((2,))],
    )


def solution(mesh):
    in_specs = (P(None, "line", "tile"), P("line", "tile"), P("line", "tile"))
    out_specs = P(None, "line", "tile")
    return jax.shard_map(body, mesh=mesh, in_specs=in_specs, out_specs=out_specs, check_vma=False)
```
